256 devices in a mesh: dp: 2 (over x_lo), row: 32 (over z, y), col: 4 (over x_hi, core).
Axes of the slice: x: 4 (x_hi: 2, x_lo: 2; x = x_hi * 2 + x_lo), y: 4, z: 8, core: 2. Of those that a mesh axis runs over, the one named last changes fastest.
Arguments:
- layer_input: bfloat16 [2048, 6144], P(('dp', 'row'), 'col'), may hold values from -0.8984375 to 0.8984375
- grad_output: bfloat16 [2048, 6144], P(('dp', 'row'), 'col'), may hold values from -3 to 3
- gate_saved: bfloat16 [2048, 16384], P(('dp', 'col'), 'row'), may hold values from -9 to 9
- up_saved: bfloat16 [2048, 16384], P(('dp', 'col'), 'row'), may hold values from -0.8984375 to 0.8984375
- w_gate: bfloat16 [6144, 16384], P('col', 'row'), may hold values from -0.078125 to 0.078125
- w_up: bfloat16 [6144, 16384], P('col', 'row'), may hold values from -0.078125 to 0.078125
- w_down: bfloat16 [16384, 6144], P('row', 'col'), may hold values from -0.046875 to 0.046875
Outputs:
- grad_input: bfloat16 [2048, 6144], P(('dp', 'row'), 'col')
- grad_gate: bfloat16 [6144, 16384], P('col', 'row')
- grad_up: bfloat16 [6144, 16384], P('col', 'row')
- grad_down: bfloat16 [16384, 6144], P('row', 'col')
The draws below stay inside these ranges and needn't reach their ends.
All inputs are finite; a program needn't handle non-finite values.
Results may differ from the reference program's by a relative error of at most 0.022.
Values may be sent and summed in bfloat16 or wider, within the bound.
No kernel may reach another device: no remote copies, remote signals or barrier semaphores. Data moves between devices by JAX's collectives and lax.ppermute only.
A program may use at most 64 MiB of HBM per device.

```python
import jax
import jax.numpy as jnp

D = 6144
FF = 16384
TOK = 1024
TOKENS = 2048
N_DP = 2


def block_scale(stream_key, shape, shards, low, high):
    factor_of = 1.0
    for position, blocks in shards:
        heights = jax.random.uniform(jax.random.fold_in(jax.random.fold_in(stream_key, 6), position), (blocks,), jnp.float32, low / len(shards), high / len(shards))
        factor_of = factor_of * jnp.repeat(jnp.exp(heights), shape[position] // blocks).reshape((-1,) + (1,) * (len(shape) - 1 - position))
    return factor_of


def centred(stream_key, extent, spread, bound, split=(), held_as=jnp.bfloat16):
    array = spread * jax.random.normal(stream_key, extent, jnp.float32)
    if split:
        array = array * block_scale(stream_key, extent, split, -0.22, 0.18)
    return jnp.clip(array, -bound, bound).astype(held_as)


def setup_inputs(seed: int = 0) -> dict:
    splits = jax.random.split(jax.random.key(seed), 8)
    layer_input = centred(splits[0], (TOKENS, D), 0.15, 0.8984375, ((0, 64), (1, 4)))
    grad_output = centred(splits[1], (TOKENS, D), 0.5, 3.0, ((0, 64), (1, 4)))
    gate_saved = centred(splits[2], (TOKENS, FF), 1.5, 9.0, ((0, 8), (1, 32)))
    up_saved = centred(splits[3], (TOKENS, FF), 0.15, 0.8984375, ((0, 8), (1, 32)))
    w_gate = centred(splits[4], (D, FF), D ** -0.5, 0.078125, ((0, 4), (1, 32)))
    w_up = centred(splits[5], (D, FF), D ** -0.5, 0.078125, ((0, 4), (1, 32)))
    w_down = centred(splits[6], (FF, D), FF ** -0.5, 0.046875, ((0, 32), (1, 4)))
    return {"layer_input": layer_input, "grad_output": grad_output, "gate_saved": gate_saved, "up_saved": up_saved, "w_gate": w_gate, "w_up": w_up, "w_down": w_down}


def replica_pass(layer_input, grad_output, gate_saved, up_saved, w_gate, w_up, w_down):
    grad_hidden = jnp.dot(grad_output, w_down.T, preferred_element_type=jnp.float32)
    gate_val = gate_saved.astype(jnp.float32)
    up_val = up_saved.astype(jnp.float32)
    sigma = jax.nn.sigmoid(gate_val)
    active = gate_val * sigma
    hidden = (active * up_val).astype(jnp.bfloat16)
    grad_gate_act = (grad_hidden * up_val * sigma * (1.0 + gate_val * (1.0 - sigma))).astype(jnp.bfloat16)
    grad_up_act = (grad_hidden * active).astype(jnp.bfloat16)
    grad_input = (jnp.dot(grad_gate_act, w_gate.T, preferred_element_type=jnp.float32)
                  + jnp.dot(grad_up_act, w_up.T, preferred_element_type=jnp.float32)).astype(jnp.bfloat16)
    part_gate = jnp.dot(layer_input.T, grad_gate_act, preferred_element_type=jnp.float32).astype(jnp.bfloat16)
    part_up = jnp.dot(layer_input.T, grad_up_act, preferred_element_type=jnp.float32).astype(jnp.bfloat16)
    part_down = jnp.dot(hidden.T, grad_output, preferred_element_type=jnp.float32).astype(jnp.bfloat16)
    return grad_input, part_gate, part_up, part_down


def reference(layer_input, grad_output, gate_saved, up_saved, w_gate, w_up, w_down):
    inputs = []
    sum_gate = jnp.zeros(w_gate.shape, jnp.float32)
    sum_up = jnp.zeros(w_up.shape, jnp.float32)
    sum_down = jnp.zeros(w_down.shape, jnp.float32)
    for replica in range(N_DP):
        lo = replica * TOK
        result = replica_pass(layer_input[lo:lo + TOK], grad_output[lo:lo + TOK],
                              gate_saved[lo:lo + TOK], up_saved[lo:lo + TOK], w_gate, w_up, w_down)
        inputs.append(result[0])
        sum_gate = sum_gate + result[1].astype(jnp.float32)
        sum_up = sum_up + result[2].astype(jnp.float32)
        sum_down = sum_down + result[3].astype(jnp.float32)
    grad_input = jnp.concatenate(inputs, axis=0)
    return grad_input, sum_gate.astype(jnp.bfloat16), sum_up.astype(jnp.bfloat16), sum_down.astype(jnp.bfloat16)
```

```python
import jax
import jax.numpy as jnp
from jax import lax
from jax.sharding import Mesh, PartitionSpec as P

F32, BF16 = jnp.float32, jnp.bfloat16
NZ, NY = 8, 4


def dot(left, right, dims):
    return lax.dot_general(left, right, (dims, ((), ())), preferred_element_type=F32)


def contract_last(left, right):
    return dot(left, right, ((1,), (1,)))


def contract_first(left, right):
    return dot(left, right, ((0,), (0,)))


def from_ahead(x, axis, n, k):
    return lax.ppermute(x, axis, [((d + k) % n, d) for d in range(n)])


def swap(x, axis):
    return lax.ppermute(x, axis, [(0, 1), (1, 0)])


def after(x, *others):
    return lax.optimization_barrier((x, *others))[0]


def natural(parts, index):
    n = len(parts)
    both = jnp.concatenate(parts + parts, axis=0)
    rows = parts[0].shape[0]
    return lax.dynamic_slice_in_dim(both, ((n - index) % n) * rows, n * rows, axis=0)


def gather_direct(x, axis, n):
    parts = [x] + [from_ahead(x, axis, n, k) for k in range(1, n)]
    return natural(parts, lax.axis_index(axis))


def ordered(mine, other, index, axis):
    low = jnp.where(index == 0, mine, other)
    high = jnp.where(index == 0, other, mine)
    return jnp.stack([low, high], axis=axis)


def body(layer_input, grad_output, gate_saved, up_saved, w_gate, w_up, w_down):
    z, y = lax.axis_index("z"), lax.axis_index("y")
    xh, core = lax.axis_index("xh"), lax.axis_index("core")

    go_y = gather_direct(grad_output, "y", NY)
    go = lax.all_gather(go_y, "z", axis=0, tiled=True)

    gate = ordered(gate_saved, swap(gate_saved, "xh"), xh, 0).astype(F32)
    up = ordered(up_saved, swap(up_saved, "xh"), xh, 0).astype(F32)
    sigma = jax.nn.sigmoid(gate)
    active = gate * sigma
    hidden_own = (active * up).astype(BF16)
    hidden = ordered(hidden_own, swap(hidden_own, "core"), core, 1).reshape(1024, 512)

    partner = swap(layer_input, "dp")
    partner_z = gather_direct(partner, "z", NZ)
    partner_parts = [partner_z] + [from_ahead(partner_z, "y", NY, k) for k in range(1, NY)]
    partner_input = jnp.concatenate(partner_parts, axis=0)

    own_y = gather_direct(layer_input, "y", NY)
    own_input = lax.all_gather(after(own_y, go), "z", axis=0, tiled=True)

    part = contract_last(go, w_down).reshape(2, 2, 256, 512)
    part_mine = jnp.where(core == 0, part[:, 0], part[:, 1])
    part_other = jnp.where(core == 0, part[:, 1], part[:, 0]).astype(BF16)
    chip = part_mine + swap(part_other, "core").astype(F32)
    grad_hidden = chip + swap(chip.astype(BF16), "xh").astype(F32)

    gg_own = (grad_hidden * up * sigma * (1.0 + gate * (1.0 - sigma))).astype(BF16)
    gu_own = (grad_hidden * active).astype(BF16)
    gg = ordered(gg_own, swap(gg_own, "core"), core, 1).reshape(1024, 512)
    gu = ordered(gu_own, swap(gu_own, "core"), core, 1).reshape(1024, 512)

    partial_in = (contract_last(gg, w_gate) + contract_last(gu, w_up)).astype(BF16)
    in_z = lax.psum_scatter(partial_in, "z", scatter_dimension=0, tiled=True).reshape(NY, 32, 1536)
    total = lax.dynamic_index_in_dim(in_z, y, 0, keepdims=False).astype(F32)
    for k in range(1, NY):
        piece = lax.dynamic_index_in_dim(in_z, (y + k) % NY, 0, keepdims=False)
        total = total + from_ahead(piece, "y", NY, NY - k).astype(F32)
    grad_input = total.astype(BF16)

    gg_far, gu_far = swap(gg_own, "dp"), swap(gu_own, "dp")
    part_down = contract_first(hidden, go).astype(BF16)
    down_far = swap(after(part_down, gg_far, gu_far), "dp")

    def far(own):
        whole = ordered(own, swap(own, "core"), core, 1).reshape(NZ, NY, 32, 512)
        twice = jnp.concatenate([whole, whole], axis=1)
        rolled = lax.dynamic_slice_in_dim(twice, y, NY, axis=1)
        return rolled.transpose(1, 0, 2, 3).reshape(1024, 512)

    grad_gate = contract_first(own_input, gg) + contract_first(partner_input, far(gg_far))
    grad_up = contract_first(own_input, gu) + contract_first(partner_input, far(gu_far))
    grad_down = part_down.astype(F32) + down_far.astype(F32)
    return grad_input, grad_gate.astype(BF16), grad_up.astype(BF16), grad_down.astype(BF16)


def solution(mesh):
    fine = Mesh(mesh.devices.reshape(2, NZ, NY, 2, 2), ("dp", "z", "y", "xh", "core"))
    tokens, col, row = ("dp", "z", "y"), ("xh", "core"), ("z", "y")
    in_specs = (
        P(tokens, col),
        P(tokens, col),
        P(("dp",) + col, row),
        P(("dp",) + col, row),
        P(col, row),
        P(col, row),
        P(row, col),
    )
    out_specs = (P(tokens, col), P(col, row), P(col, row), P(row, col))
    return jax.shard_map(body, mesh=fine, in_specs=in_specs, out_specs=out_specs, check_vma=False)
```

```python
import functools

import jax
import jax.numpy as jnp
from jax import lax
from jax.experimental import pallas as pl
from jax.experimental.pallas import tpu as pltpu
from jax.sharding import Mesh, PartitionSpec as P

F32, BF16 = jnp.float32, jnp.bfloat16
NZ, NY = 8, 4
VMEM = pl.BlockSpec(memory_space=pltpu.VMEM)
SMEM = pl.BlockSpec(memory_space=pltpu.SMEM)


def dot(left, right, left_dim, right_dim):
    dims = (((left_dim,), (right_dim,)), ((), ()))
    return lax.dot_general(left, right, dims, preferred_element_type=F32)


def from_ahead(x, axis, n, k):
    return lax.ppermute(x, axis, [((d + k) % n, d) for d in range(n)])


def swap(x, axis):
    return lax.ppermute(x, axis, [(0, 1), (1, 0)])


def params(mib):
    return pltpu.CompilerParams(vmem_limit_bytes=mib << 20)


def arrange_kernel(n, slot, place, *refs):
    for k in range(n):
        refs[n][(place[slot] + k) % n] = refs[k][...]


def arrange(place, slot, parts):
    n = len(parts)
    rows, cols = parts[0].shape
    out = pl.pallas_call(
        functools.partial(arrange_kernel, n, slot),
        out_shape=jax.ShapeDtypeStruct((n, rows, cols), BF16),
        in_specs=[SMEM] + [VMEM] * n,
        out_specs=VMEM,
        compiler_params=params(16),
    )(place, *parts)
    return out.reshape(n * rows, cols)


def hidden_grad_kernel(place, go, w_down, mine, send):
    step = pl.program_id(0)
    half, side = step // 2, step % 2
    part = dot(go[...], w_down[...], 1, 1)

    @pl.when(side == place[3])
    def _():
        mine[half] = part

    @pl.when(side != place[3])
    def _():
        send[half] = part.astype(BF16)


def hidden_grad(place, go, w_down):
    whole = pl.BlockSpec((2, 256, 512), lambda i: (0, 0, 0))
    return pl.pallas_call(
        hidden_grad_kernel,
        grid=(4,),
        out_shape=(
            jax.ShapeDtypeStruct((2, 256, 512), F32),
            jax.ShapeDtypeStruct((2, 256, 512), BF16),
        ),
        in_specs=[
            SMEM,
            pl.BlockSpec((256, 1536), lambda i: (i, 0)),
            pl.BlockSpec((512, 1536), lambda i: (0, 0)),
        ],
        out_specs=(whole, whole),
        compiler_params=params(32),
        cost_estimate=pl.CostEstimate(flops=2 * 1024 * 1536 * 512, bytes_accessed=6 << 20, transcendentals=0),
    )(place, go, w_down)


def input_grad_kernel(place, gg, gg_other, gu, gu_other, w_gate, w_up, out):
    step = pl.program_id(0)
    half, side = step // 2, step % 2

    def emit(gate_ref, up_ref):
        total = dot(gate_ref[half], w_gate[...], 1, 1) + dot(up_ref[half], w_up[...], 1, 1)
        out[...] = total.astype(BF16)

    @pl.when(side == place[3])
    def _():
        emit(gg, gu)

    @pl.when(side != place[3])
    def _():
        emit(gg_other, gu_other)


def input_grad(place, gg, gg_other, gu, gu_other, w_gate, w_up):
    whole = pl.BlockSpec((2, 256, 512), lambda i: (0, 0, 0))
    weight = pl.BlockSpec((1536, 512), lambda i: (0, 0))
    return pl.pallas_call(
        input_grad_kernel,
        grid=(4,),
        out_shape=jax.ShapeDtypeStruct((1024, 1536), BF16),
        in_specs=[SMEM] + [whole] * 4 + [weight] * 2,
        out_specs=pl.BlockSpec((256, 1536), lambda i: (i, 0)),
        compiler_params=params(40),
        cost_estimate=pl.CostEstimate(flops=4 * 1024 * 1536 * 512, bytes_accessed=8 << 20, transcendentals=0),
    )(place, gg, gg_other, gu, gu_other, w_gate, w_up)


def fill_natural(place, own, other, rows, col):
    for half in range(2):
        base = half * 512
        start = pl.multiple_of(base + place[3] * 256, 256)
        rows[pl.ds(start, 256), col:col + 512] = own[half]
        start = pl.multiple_of(base + (1 - place[3]) * 256, 256)
        rows[pl.ds(start, 256), col:col + 512] = other[half]


def down_kernel(place, hidden, hidden_other, go, out, rows):
    @pl.when(pl.program_id(0) == 0)
    def _():
        fill_natural(place, hidden, hidden_other, rows, 0)

    out[...] = dot(rows[...], go[...], 0, 0).astype(BF16)


def down_grad(place, hidden, hidden_other, go):
    whole = pl.BlockSpec((2, 256, 512), lambda i: (0, 0, 0))
    return pl.pallas_call(
        down_kernel,
        grid=(3,),
        out_shape=jax.ShapeDtypeStruct((512, 1536), BF16),
        in_specs=[SMEM, whole, whole, pl.BlockSpec((1024, 512), lambda i: (0, i))],
        out_specs=pl.BlockSpec((512, 512), lambda i: (0, i)),
        scratch_shapes=[pltpu.VMEM((1024, 512), BF16)],
        compiler_params=params(32),
        cost_estimate=pl.CostEstimate(flops=2 * 1024 * 1536 * 512, bytes_accessed=6 << 20, transcendentals=0),
    )(place, hidden, hidden_other, go)


def fill_rolled(place, own, other, rows, col):
    for half in range(2):
        for pair in range(2):
            for y in range(NY):
                k = (y - place[1] + NY) % NY
                lines = pl.ds(pair * 128 + y * 32, 32)
                z_own = 4 * half + 2 * place[3] + pair
                rows[k, z_own, :, col:col + 512] = own[half, lines, :]
                z_other = 4 * half + 2 * (1 - place[3]) + pair
                rows[k, z_other, :, col:col + 512] = other[half, lines, :]


def weight_kernel(place, own, p0, p1, p2, p3, gg, gg_o, gu, gu_o, fgg, fgg_o, fgu, fgu_o, d_gate, d_up, near, far):
    @pl.when(pl.program_id(0) == 0)
    def _():
        fill_natural(place, gg, gg_o, near, 0)
        fill_natural(place, gu, gu_o, near, 512)
        fill_rolled(place, fgg, fgg_o, far, 0)
        fill_rolled(place, fgu, fgu_o, far, 512)

    total = dot(own[...], near[...], 0, 0)
    for k, piece in enumerate((p0, p1, p2, p3)):
        total = total + dot(piece[...], far[k].reshape(256, 1024), 0, 0)
    d_gate[...] = total[:, :512].astype(BF16)
    d_up[...] = total[:, 512:].astype(BF16)


def weight_grads(place, own, pieces, grads):
    whole = pl.BlockSpec((2, 256, 512), lambda i: (0, 0, 0))
    piece = pl.BlockSpec((256, 256), lambda i: (0, i))
    tile = pl.BlockSpec((256, 512), lambda i: (i, 0))
    shape = jax.ShapeDtypeStruct((1536, 512), BF16)
    return pl.pallas_call(
        weight_kernel,
        grid=(6,),
        out_shape=(shape, shape),
        in_specs=[SMEM, pl.BlockSpec((1024, 256), lambda i: (0, i))] + [piece] * 4 + [whole] * 8,
        out_specs=(tile, tile),
        scratch_shapes=[pltpu.VMEM((1024, 1024), BF16), pltpu.VMEM((NY, NZ, 32, 1024), BF16)],
        compiler_params=params(40),
        cost_estimate=pl.CostEstimate(flops=8 * 1024 * 1536 * 512, bytes_accessed=16 << 20, transcendentals=0),
    )(place, own, *pieces, *grads)


def ring(x, axis, n):
    ahead, behind = [], []
    up, down = x, x
    for step in range(1, n // 2 + 1):
        up = from_ahead(up, axis, n, 1)
        ahead.append(up)
        if step < n // 2:
            down = from_ahead(down, axis, n, n - 1)
            behind.append(down)
    return [x] + ahead + behind[::-1]


def ordered(mine, other, index):
    low = jnp.where(index == 0, mine, other)
    high = jnp.where(index == 0, other, mine)
    return jnp.stack([low, high], axis=0)


def body(layer_input, grad_output, gate_saved, up_saved, w_gate, w_up, w_down):
    place = jnp.stack([lax.axis_index(name) for name in ("z", "y", "xh", "core")]).astype(jnp.int32)
    xh = place[2]

    go_y = arrange(place, 1, [grad_output] + [from_ahead(grad_output, "y", NY, k) for k in (1, 2, 3)])
    go = lax.all_gather(go_y, "z", axis=0, tiled=True)

    gate = ordered(gate_saved, swap(gate_saved, "xh"), xh)
    up = ordered(up_saved, swap(up_saved, "xh"), xh)
    gate_val, up_val = gate.astype(F32), up.astype(F32)
    hidden = (gate_val * jax.nn.sigmoid(gate_val) * up_val).astype(BF16)
    hidden_other = swap(hidden, "core")
    partner = swap(layer_input, "dp")
    partner_z = arrange(place, 0, ring(partner, "z", NZ))
    own_y = arrange(place, 1, [layer_input] + [from_ahead(layer_input, "y", NY, k) for k in (1, 2, 3)])

    go, gate, up, hidden, hidden_other, partner_z, own_y = lax.optimization_barrier(
        (go, gate, up, hidden, hidden_other, partner_z, own_y)
    )

    own_input = lax.all_gather(own_y, "z", axis=0, tiled=True)
    mine, send = hidden_grad(place, go, w_down)
    chip = mine + swap(send, "core").astype(F32)
    chip_far = swap(chip.astype(BF16), "xh")
    part_down = down_grad(place, hidden, hidden_other, go)
    piece1 = from_ahead(partner_z, "y", NY, 1)
    piece3 = from_ahead(partner_z, "y", NY, 3)

    chip, chip_far, part_down, piece1, piece3 = lax.optimization_barrier(
        (chip, chip_far, part_down, piece1, piece3)
    )

    grad_hidden = chip + chip_far.astype(F32)
    gate_val, up_val = gate.astype(F32), up.astype(F32)
    sigma = jax.nn.sigmoid(gate_val)
    gg = (grad_hidden * up_val * sigma * (1.0 + gate_val * (1.0 - sigma))).astype(BF16)
    gu = (grad_hidden * gate_val * sigma).astype(BF16)
    gg_other, gu_other = swap(gg, "core"), swap(gu, "core")
    gg_far, gu_far = swap(gg, "dp"), swap(gu, "dp")
    partial_in = input_grad(place, gg, gg_other, gu, gu_other, w_gate, w_up)
    in_z = lax.psum_scatter(partial_in, "z", scatter_dimension=0, tiled=True).reshape(NY, 32, 1536)

    piece2 = from_ahead(partner_z, "y", NY, 2)
    gg_far, gu_far, part_down, piece2 = lax.optimization_barrier((gg_far, gu_far, part_down, piece2))
    down_far = swap(part_down, "dp")
    grads = (gg, gg_other, gu, gu_other, gg_far, swap(gg_far, "core"), gu_far, swap(gu_far, "core"))
    grad_gate, grad_up = weight_grads(place, own_input, (partner_z, piece1, piece2, piece3), grads)
    grad_down = (part_down.astype(F32) + down_far.astype(F32)).astype(BF16)
    in_z, grad_gate, grad_up, grad_down = lax.optimization_barrier((in_z, grad_gate, grad_up, grad_down))

    y = place[1]
    total = lax.dynamic_index_in_dim(in_z, y, 0, keepdims=False).astype(F32)
    for k in range(1, NY):
        slab = lax.dynamic_index_in_dim(in_z, (y + k) % NY, 0, keepdims=False)
        total = total + from_ahead(slab, "y", NY, NY - k).astype(F32)
    return total.astype(BF16), grad_gate, grad_up, grad_down


def solution(mesh):
    fine = Mesh(mesh.devices.reshape(2, NZ, NY, 2, 2), ("dp", "z", "y", "xh", "core"))
    tokens, col, row = ("dp", "z", "y"), ("xh", "core"), ("z", "y")
    in_specs = (
        P(tokens, col),
        P(tokens, col),
        P(("dp",) + col, row),
        P(("dp",) + col, row),
        P(col, row),
        P(col, row),
        P(row, col),
    )
    out_specs = (P(tokens, col), P(col, row), P(col, row), P(row, col))
    return jax.shard_map(body, mesh=fine, in_specs=in_specs, out_specs=out_specs, check_vma=False)
```

```python
import functools

import jax
import jax.numpy as jnp
from jax import lax
from jax.experimental import pallas as pl
from jax.experimental.pallas import tpu as pltpu
from jax.sharding import Mesh, PartitionSpec as P

F32, BF16 = jnp.float32, jnp.bfloat16
NZ, NY = 8, 4
VMEM = pl.BlockSpec(memory_space=pltpu.VMEM)
SMEM = pl.BlockSpec(memory_space=pltpu.SMEM)
HBM = pl.BlockSpec(memory_space=pltpu.HBM)


def dot(left, right, left_dim, right_dim):
    dims = (((left_dim,), (right_dim,)), ((), ()))
    return lax.dot_general(left, right, dims, preferred_element_type=F32)


def from_ahead(x, axis, n, k):
    return lax.ppermute(x, axis, [((d + k) % n, d) for d in range(n)])


def swap(x, axis):
    return lax.ppermute(x, axis, [(0, 1), (1, 0)])


def params(mib):
    return pltpu.CompilerParams(vmem_limit_bytes=mib << 20)


def arrange_kernel(n, slot, place, *refs):
    for k in range(n):
        refs[n][(place[slot] + k) % n] = refs[k][...]


def arrange(place, slot, parts):
    n = len(parts)
    rows, cols = parts[0].shape
    out = pl.pallas_call(
        functools.partial(arrange_kernel, n, slot),
        out_shape=jax.ShapeDtypeStruct((n, rows, cols), BF16),
        in_specs=[SMEM] + [VMEM] * n,
        out_specs=VMEM,
        compiler_params=params(16),
    )(place, *parts)
    return out.reshape(n * rows, cols)


def hidden_grad_kernel(place, go, w_down, mine, send, rows, sems):
    copies = [
        pltpu.make_async_copy(go.at[pl.ds(256 * block, 256)], rows.at[block], sems.at[block])
        for block in range(4)
    ]
    for copy in copies:
        copy.start()
    for block, copy in enumerate(copies):
        copy.wait()
        half, side = block // 2, block % 2
        part = dot(rows[block], w_down[...], 1, 1)

        @pl.when(side == place[3])
        def _():
            mine[half] = part

        @pl.when(side != place[3])
        def _():
            send[half] = part.astype(BF16)


def hidden_grad(place, go, w_down):
    return pl.pallas_call(
        hidden_grad_kernel,
        out_shape=(
            jax.ShapeDtypeStruct((2, 256, 512), F32),
            jax.ShapeDtypeStruct((2, 256, 512), BF16),
        ),
        in_specs=[SMEM, HBM, VMEM],
        out_specs=(VMEM, VMEM),
        scratch_shapes=[pltpu.VMEM((4, 256, 1536), BF16), pltpu.SemaphoreType.DMA((4,))],
        compiler_params=params(24),
        cost_estimate=pl.CostEstimate(flops=2 * 1024 * 1536 * 512, bytes_accessed=6 << 20, transcendentals=0),
    )(place, go, w_down)


def input_grad_kernel(place, gg, gg_other, gu, gu_other, w_gate, w_up, out):
    step = pl.program_id(0)
    half, side = step // 2, step % 2

    def emit(gate_ref, up_ref):
        total = dot(gate_ref[half], w_gate[...], 1, 1) + dot(up_ref[half], w_up[...], 1, 1)
        out[...] = total.astype(BF16)

    @pl.when(side == place[3])
    def _():
        emit(gg, gu)

    @pl.when(side != place[3])
    def _():
        emit(gg_other, gu_other)


def input_grad(place, gg, gg_other, gu, gu_other, w_gate, w_up):
    return pl.pallas_call(
        input_grad_kernel,
        grid=(4,),
        out_shape=jax.ShapeDtypeStruct((1024, 1536), BF16),
        in_specs=[SMEM] + [VMEM] * 6,
        out_specs=pl.BlockSpec((256, 1536), lambda i: (i, 0)),
        compiler_params=params(24),
        cost_estimate=pl.CostEstimate(flops=4 * 1024 * 1536 * 512, bytes_accessed=8 << 20, transcendentals=0),
    )(place, gg, gg_other, gu, gu_other, w_gate, w_up)


def fill_natural(place, own, other, rows, col):
    for half in range(2):
        base = half * 512
        start = pl.multiple_of(base + place[3] * 256, 256)
        rows[pl.ds(start, 256), col:col + 512] = own[half]
        start = pl.multiple_of(base + (1 - place[3]) * 256, 256)
        rows[pl.ds(start, 256), col:col + 512] = other[half]


def down_kernel(place, hidden, hidden_other, go, out, rows):
    @pl.when(pl.program_id(0) == 0)
    def _():
        fill_natural(place, hidden, hidden_other, rows, 0)

    out[...] = dot(rows[...], go[...], 0, 0).astype(BF16)


def down_grad(place, hidden, hidden_other, go):
    return pl.pallas_call(
        down_kernel,
        grid=(3,),
        out_shape=jax.ShapeDtypeStruct((512, 1536), BF16),
        in_specs=[SMEM, VMEM, VMEM, pl.BlockSpec((1024, 512), lambda i: (0, i))],
        out_specs=pl.BlockSpec((512, 512), lambda i: (0, i)),
        scratch_shapes=[pltpu.VMEM((1024, 512), BF16)],
        compiler_params=params(32),
        cost_estimate=pl.CostEstimate(flops=2 * 1024 * 1536 * 512, bytes_accessed=6 << 20, transcendentals=0),
    )(place, hidden, hidden_other, go)


def fill_rolled(place, own, other, rows, col):
    for half in range(2):
        for pair in range(2):
            for y in range(NY):
                k = (y - place[1] + NY) % NY
                lines = pl.ds(pair * 128 + y * 32, 32)
                z_own = 4 * half + 2 * place[3] + pair
                rows[k, z_own, :, col:col + 512] = own[half, lines, :]
                z_other = 4 * half + 2 * (1 - place[3]) + pair
                rows[k, z_other, :, col:col + 512] = other[half, lines, :]


def weight_kernel(place, *refs):
    pieces, grads, (d_gate, d_up, rows) = refs[:8], refs[8:16], refs[16:]

    @pl.when(pl.program_id(0) == 0)
    def _():
        for replica in range(2):
            fill_rolled(place, *grads[4 * replica:4 * replica + 2], rows.at[replica], 0)
            fill_rolled(place, *grads[4 * replica + 2:4 * replica + 4], rows.at[replica], 512)

    total = jnp.zeros((256, 1024), F32)
    for k, piece in enumerate(pieces):
        total = total + dot(piece[...], rows[k // NY, k % NY].reshape(256, 1024), 0, 0)
    d_gate[...] = total[:, :512].astype(BF16)
    d_up[...] = total[:, 512:].astype(BF16)


def weight_grads(place, pieces, grads):
    tile = pl.BlockSpec((256, 512), lambda i: (i, 0))
    shape = jax.ShapeDtypeStruct((1536, 512), BF16)
    return pl.pallas_call(
        weight_kernel,
        grid=(6,),
        out_shape=(shape, shape),
        in_specs=[SMEM] + [pl.BlockSpec((256, 256), lambda i: (0, i))] * 8 + [VMEM] * 8,
        out_specs=(tile, tile),
        scratch_shapes=[pltpu.VMEM((2, NY, NZ, 32, 1024), BF16)],
        compiler_params=params(28),
        cost_estimate=pl.CostEstimate(flops=8 * 1024 * 1536 * 512, bytes_accessed=16 << 20, transcendentals=0),
    )(place, *pieces, *grads)


def gather_z(x):
    f1, f2, b1, b2 = (from_ahead(x, "z", NZ, k) for k in (1, 2, 7, 6))
    f3, b3 = from_ahead(f2, "z", NZ, 1), from_ahead(b2, "z", NZ, 7)
    f4 = from_ahead(f2, "z", NZ, 2)
    return [x, f1, f2, f3, f4, b3, b2, b1]


def ordered(mine, other, index):
    low = jnp.where(index == 0, mine, other)
    high = jnp.where(index == 0, other, mine)
    return jnp.stack([low, high], axis=0)


def body(layer_input, grad_output, gate_saved, up_saved, w_gate, w_up, w_down):
    place = jnp.stack([lax.axis_index(name) for name in ("z", "y", "xh", "core")]).astype(jnp.int32)
    xh = place[2]

    go_y = arrange(place, 1, [grad_output] + [from_ahead(grad_output, "y", NY, k) for k in (1, 2, 3)])
    go = lax.all_gather(go_y, "z", axis=0, tiled=True)

    gate = ordered(gate_saved, swap(gate_saved, "xh"), xh)
    up = ordered(up_saved, swap(up_saved, "xh"), xh)
    gate_val, up_val = gate.astype(F32), up.astype(F32)
    hidden = (gate_val * jax.nn.sigmoid(gate_val) * up_val).astype(BF16)
    hidden_other = swap(hidden, "core")
    own_z = arrange(place, 0, gather_z(layer_input))
    partner_z = swap(own_z, "dp")
    own1, own3 = from_ahead(own_z, "y", NY, 1), from_ahead(own_z, "y", NY, 3)

    go, gate, up, hidden, hidden_other, partner_z, own1, own3 = lax.optimization_barrier(
        (go, gate, up, hidden, hidden_other, partner_z, own1, own3)
    )

    own2 = from_ahead(own_z, "y", NY, 2)
    mine, send = hidden_grad(place, go, w_down)
    chip = mine + swap(send, "core").astype(F32)
    chip_far = swap(chip.astype(BF16), "xh")
    part_down = down_grad(place, hidden, hidden_other, go)

    chip, chip_far, part_down, own2 = lax.optimization_barrier((chip, chip_far, part_down, own2))

    grad_hidden = chip + chip_far.astype(F32)
    gate_val, up_val = gate.astype(F32), up.astype(F32)
    sigma = jax.nn.sigmoid(gate_val)
    gg = (grad_hidden * up_val * sigma * (1.0 + gate_val * (1.0 - sigma))).astype(BF16)
    gu = (grad_hidden * gate_val * sigma).astype(BF16)
    gg_other, gu_other = swap(gg, "core"), swap(gu, "core")
    gg_far, gu_far = swap(gg, "dp"), swap(gu, "dp")
    partner = [partner_z] + [from_ahead(partner_z, "y", NY, k) for k in (1, 2, 3)]
    partial_in = input_grad(place, gg, gg_other, gu, gu_other, w_gate, w_up)
    in_z = lax.psum_scatter(partial_in, "z", scatter_dimension=0, tiled=True).reshape(NY, 32, 1536)

    gg_far, gu_far, part_down = lax.optimization_barrier((gg_far, gu_far, part_down))
    down_far = swap(part_down, "dp")
    grads = (gg, gg_other, gu, gu_other, gg_far, swap(gg_far, "core"), gu_far, swap(gu_far, "core"))
    grad_gate, grad_up = weight_grads(place, [own_z, own1, own2, own3] + partner, grads)
    grad_gate, grad_up, down_far = lax.optimization_barrier((grad_gate, grad_up, down_far))
    grad_down = (part_down.astype(F32) + down_far.astype(F32)).astype(BF16)

    y = place[1]
    total = lax.dynamic_index_in_dim(in_z, y, 0, keepdims=False).astype(F32)
    for k in range(1, NY):
        slab = lax.dynamic_index_in_dim(in_z, (y + k) % NY, 0, keepdims=False)
        total = total + from_ahead(slab, "y", NY, NY - k).astype(F32)
    return total.astype(BF16), grad_gate, grad_up, grad_down


def solution(mesh):
    fine = Mesh(mesh.devices.reshape(2, NZ, NY, 2, 2), ("dp", "z", "y", "xh", "core"))
    tokens, col, row = ("dp", "z", "y"), ("xh", "core"), ("z", "y")
    in_specs = (
        P(tokens, col),
        P(tokens, col),
        P(("dp",) + col, row),
        P(("dp",) + col, row),
        P(col, row),
        P(col, row),
        P(row, col),
    )
    out_specs = (P(tokens, col), P(col, row), P(col, row), P(row, col))
    return jax.shard_map(body, mesh=fine, in_specs=in_specs, out_specs=out_specs, check_vma=False)
```

```python
import functools

import jax
import jax.numpy as jnp
from jax import lax
from jax.experimental import pallas as pl
from jax.experimental.pallas import tpu as pltpu
from jax.sharding import Mesh, PartitionSpec as P

F32, BF16 = jnp.float32, jnp.bfloat16
NZ, NY = 8, 4
WIDE, SIDE = 1024, 512
FIRST = 64
VMEM = pl.BlockSpec(memory_space=pltpu.VMEM)
SMEM = pl.BlockSpec(memory_space=pltpu.SMEM)
HBM = pl.BlockSpec(memory_space=pltpu.HBM)


def dot(left, right, left_dim, right_dim):
    dims = (((left_dim,), (right_dim,)), ((), ()))
    return lax.dot_general(left, right, dims, preferred_element_type=F32)


def from_ahead(x, axis, n, k):
    return lax.ppermute(x, axis, [((d + k) % n, d) for d in range(n)])


def swap(x, axis):
    return lax.ppermute(x, axis, [(0, 1), (1, 0)])


def params(mib):
    return pltpu.CompilerParams(vmem_limit_bytes=mib << 20)


def prepare_kernel(layer_input, grad_output, wide, mixed):
    wide[...] = grad_output[:, :WIDE]
    mixed[:, :1536] = layer_input[...]
    mixed[:, 1536:] = grad_output[:, WIDE:]


def prepare(layer_input, grad_output):
    return pl.pallas_call(
        prepare_kernel,
        out_shape=(
            jax.ShapeDtypeStruct((32, WIDE), BF16),
            jax.ShapeDtypeStruct((32, 1536 + SIDE), BF16),
        ),
        in_specs=[VMEM] * 2,
        out_specs=(VMEM,) * 2,
        compiler_params=params(4),
    )(layer_input, grad_output)


def arrange_kernel(n, slot, cuts, place, *refs):
    for k in range(n):
        there = (place[slot] + k) % n
        for out, (low, high) in zip(refs[n:], cuts):
            out[there] = refs[k][:, low:high]


def arrange(place, slot, parts, cuts):
    n, rows = len(parts), parts[0].shape[0]
    outs = pl.pallas_call(
        functools.partial(arrange_kernel, n, slot, cuts),
        out_shape=tuple(jax.ShapeDtypeStruct((n, rows, high - low), BF16) for low, high in cuts),
        in_specs=[SMEM] + [VMEM] * n,
        out_specs=(VMEM,) * len(cuts),
        compiler_params=params(6),
    )(place, *parts)
    return [out.reshape(n * rows, -1) for out in outs]


def hidden_grad_kernel(place, go, s0, s1, s2, s3, w_down, mine, send, side, rows, sems):
    copies = [
        pltpu.make_async_copy(go.at[pl.ds(512 * half, 512)], rows.at[half], sems.at[half])
        for half in range(2)
    ]
    for copy in copies:
        copy.start()
    for k, piece in enumerate((s0, s1, s2, s3)):
        there = (place[1] + k) % NY
        for z in range(NZ):
            side[z, there] = piece[32 * z:32 * z + 32, :]
    for half, copy in enumerate(copies):
        copy.wait()
        part = dot(rows[half], w_down[:, :WIDE], 1, 1)
        part = part + dot(side[4 * half:4 * half + 4].reshape(512, SIDE), w_down[:, WIDE:], 1, 1)
        for which in range(2):
            block = part[256 * which:256 * which + 256]

            @pl.when(place[3] == which)
            def _():
                mine[half] = block

            @pl.when(place[3] != which)
            def _():
                send[half] = block.astype(BF16)


def hidden_grad(place, go, sides, w_down):
    return pl.pallas_call(
        hidden_grad_kernel,
        out_shape=(
            jax.ShapeDtypeStruct((2, 256, 512), F32),
            jax.ShapeDtypeStruct((2, 256, 512), BF16),
            jax.ShapeDtypeStruct((NZ, NY, 32, SIDE), BF16),
        ),
        in_specs=[SMEM, HBM] + [VMEM] * 5,
        out_specs=(VMEM,) * 3,
        scratch_shapes=[pltpu.VMEM((2, 512, WIDE), BF16), pltpu.SemaphoreType.DMA((2,))],
        compiler_params=params(16),
    )(place, go, *sides, w_down)


def input_grad_kernel(place, gg, gg_other, gu, gu_other, w_gate, w_up, out):
    def emit(gate_ref, up_ref, core):
        gate_rows, up_rows = gate_ref[...].reshape(512, 512), up_ref[...].reshape(512, 512)
        total = (dot(gate_rows, w_gate[...], 1, 1) + dot(up_rows, w_up[...], 1, 1)).astype(BF16)
        for half in range(2):
            start = pl.multiple_of(512 * half + 256 * core, 256)
            out[pl.ds(start, 256), :] = total[256 * half:256 * half + 256]

    emit(gg, gu, place[3])
    emit(gg_other, gu_other, 1 - place[3])


def input_grad(place, gg, gg_other, gu, gu_other, w_gate, w_up):
    weight = pl.BlockSpec((512, 512), lambda i: (i, 0))
    return pl.pallas_call(
        input_grad_kernel,
        grid=(3,),
        out_shape=jax.ShapeDtypeStruct((1024, 1536), BF16),
        in_specs=[SMEM] + [VMEM] * 4 + [weight] * 2,
        out_specs=pl.BlockSpec((1024, 512), lambda i: (0, i)),
        compiler_params=params(16),
    )(place, gg, gg_other, gu, gu_other, w_gate, w_up)


def fill_natural(place, own, other, rows, col):
    for half in range(2):
        base = half * 512
        start = pl.multiple_of(base + place[3] * 256, 256)
        rows[pl.ds(start, 256), col:col + 512] = own[half]
        start = pl.multiple_of(base + (1 - place[3]) * 256, 256)
        rows[pl.ds(start, 256), col:col + 512] = other[half]


def down_kernel(place, hidden, hidden_other, go, side, first, rest, rows):
    step = pl.program_id(0)

    @pl.when(step == 0)
    def _():
        fill_natural(place, hidden, hidden_other, rows, 0)

    def emit(right):
        total = dot(rows[...], right, 0, 0).astype(BF16)
        first[...] = total[:FIRST]
        rest[...] = total[FIRST:]

    @pl.when(step < WIDE // 512)
    def _():
        emit(go[...])

    @pl.when(step == WIDE // 512)
    def _():
        emit(side[...].reshape(1024, SIDE))


def down_grad(place, hidden, hidden_other, go, side):
    return pl.pallas_call(
        down_kernel,
        grid=(3,),
        out_shape=(
            jax.ShapeDtypeStruct((FIRST, 1536), BF16),
            jax.ShapeDtypeStruct((512 - FIRST, 1536), BF16),
        ),
        in_specs=[SMEM, VMEM, VMEM, pl.BlockSpec((1024, 512), lambda i: (0, jnp.minimum(i, 1))), VMEM],
        out_specs=(
            pl.BlockSpec((FIRST, 512), lambda i: (0, i)),
            pl.BlockSpec((512 - FIRST, 512), lambda i: (0, i)),
        ),
        scratch_shapes=[pltpu.VMEM((1024, 512), BF16)],
        compiler_params=params(12),
    )(place, hidden, hidden_other, go, side)


def fill_rolled(place, own, other, rows, col):
    for half in range(2):
        for pair in range(2):
            for y in range(NY):
                k = (y - place[1] + NY) % NY
                lines = pl.ds(pair * 128 + y * 32, 32)
                z_own = 4 * half + 2 * place[3] + pair
                rows[k, z_own, :, col:col + 512] = own[half, lines, :]
                z_other = 4 * half + 2 * (1 - place[3]) + pair
                rows[k, z_other, :, col:col + 512] = other[half, lines, :]


def weight_kernel(place, *refs):
    pieces, grads, (d_gate, d_up, rows) = refs[:8], refs[8:16], refs[16:]

    @pl.when(pl.program_id(0) == 0)
    def _():
        for replica in range(2):
            fill_rolled(place, *grads[4 * replica:4 * replica + 2], rows.at[replica], 0)
            fill_rolled(place, *grads[4 * replica + 2:4 * replica + 4], rows.at[replica], 512)

    total = jnp.zeros((256, 1024), F32)
    for k, piece in enumerate(pieces):
        total = total + dot(piece[...], rows[k // NY, k % NY].reshape(256, 1024), 0, 0)
    d_gate[...] = total[:, :512].astype(BF16)
    d_up[...] = total[:, 512:].astype(BF16)


def weight_grads(place, pieces, grads):
    tile = pl.BlockSpec((256, 512), lambda i: (i, 0))
    shape = jax.ShapeDtypeStruct((1536, 512), BF16)
    return pl.pallas_call(
        weight_kernel,
        grid=(6,),
        out_shape=(shape, shape),
        in_specs=[SMEM] + [pl.BlockSpec((256, 256), lambda i: (0, i))] * 8 + [VMEM] * 8,
        out_specs=(tile, tile),
        scratch_shapes=[pltpu.VMEM((2, NY, NZ, 32, 1024), BF16)],
        compiler_params=params(18),
    )(place, *pieces, *grads)


def gather_z_near(x):
    return [from_ahead(x, "z", NZ, k) for k in (1, 2, 6, 7)]


def gather_z_far(x, f1, f2, b2, b1):
    f3, b3 = from_ahead(f2, "z", NZ, 1), from_ahead(b2, "z", NZ, 7)
    f4 = from_ahead(f2, "z", NZ, 2)
    return [x, f1, f2, f3, f4, b3, b2, b1]


def ordered(mine, other, index):
    low = jnp.where(index == 0, mine, other)
    high = jnp.where(index == 0, other, mine)
    return jnp.stack([low, high], axis=0)


def body(layer_input, grad_output, gate_saved, up_saved, w_gate, w_up, w_down):
    place = jnp.stack([lax.axis_index(name) for name in ("z", "y", "xh", "core")]).astype(jnp.int32)
    xh = place[2]

    wide, mixed = prepare(layer_input, grad_output)
    wide_parts = [from_ahead(wide, "y", NY, k) for k in (1, 2, 3)]
    near = gather_z_near(mixed)
    wide_parts, near = lax.optimization_barrier((wide_parts, near))
    (go_y,) = arrange(place, 1, [wide] + wide_parts, ((0, WIDE),))
    go = lax.all_gather(go_y, "z", axis=0, tiled=True)
    own_z, side_z = arrange(place, 0, gather_z_far(mixed, *near), ((0, 1536), (1536, 1536 + SIDE)))
    sides = [side_z] + [from_ahead(side_z, "y", NY, k) for k in (1, 2, 3)]
    partner_z = swap(own_z, "dp")

    gate = ordered(gate_saved, swap(gate_saved, "xh"), xh)
    up = ordered(up_saved, swap(up_saved, "xh"), xh)
    gate_val, up_val = gate.astype(F32), up.astype(F32)
    hidden = (gate_val * jax.nn.sigmoid(gate_val) * up_val).astype(BF16)
    hidden_other = swap(hidden, "core")
    go, gate, up, hidden, hidden_other, own_z, partner_z, *sides = lax.optimization_barrier(
        (go, gate, up, hidden, hidden_other, own_z, partner_z, *sides)
    )

    own1, own3 = from_ahead(own_z, "y", NY, 1), from_ahead(own_z, "y", NY, 3)
    mine, send, side = hidden_grad(place, go, sides, w_down)
    chip = mine + swap(send, "core").astype(F32)
    chip_far = swap(chip.astype(BF16), "xh")
    down_first, down_rest = down_grad(place, hidden, hidden_other, go, side)

    chip, chip_far, down_first, down_rest = lax.optimization_barrier((chip, chip_far, down_first, down_rest))

    first_far = swap(down_first, "dp")
    grad_hidden = chip + chip_far.astype(F32)
    gate_val, up_val = gate.astype(F32), up.astype(F32)
    sigma = jax.nn.sigmoid(gate_val)
    gg = (grad_hidden * up_val * sigma * (1.0 + gate_val * (1.0 - sigma))).astype(BF16)
    gu = (grad_hidden * gate_val * sigma).astype(BF16)
    gg_other, gu_other = swap(gg, "core"), swap(gu, "core")
    gg_other, gu_other, own1, own3, first_far = lax.optimization_barrier((gg_other, gu_other, own1, own3, first_far))
    partial_in = input_grad(place, gg, gg_other, gu, gu_other, w_gate, w_up)
    in_z = lax.psum_scatter(partial_in, "z", scatter_dimension=0, tiled=True).reshape(NY, 32, 1536)

    gg_far, gu_far = swap(gg, "dp"), swap(gu, "dp")
    partner1, partner3 = from_ahead(partner_z, "y", NY, 1), from_ahead(partner_z, "y", NY, 3)
    own2 = from_ahead(own_z, "y", NY, 2)
    gg_far, gu_far, down_rest, partner1, partner3 = lax.optimization_barrier(
        (gg_far, gu_far, down_rest, partner1, partner3)
    )
    rest_far = swap(down_rest, "dp")
    partner2 = from_ahead(partner_z, "y", NY, 2)
    gg_far_other, gu_far_other = swap(gg_far, "core"), swap(gu_far, "core")

    y = place[1]
    slabs = [lax.dynamic_index_in_dim(in_z, (y + k) % NY, 0, keepdims=False) for k in range(NY)]
    total = slabs[0].astype(F32)
    for k in range(1, NY):
        total = total + from_ahead(slabs[k], "y", NY, NY - k).astype(F32)
    grad_input = total.astype(BF16)
    grad_input, own2, partner2, gg_far_other, gu_far_other = lax.optimization_barrier(
        (grad_input, own2, partner2, gg_far_other, gu_far_other)
    )
    pieces = (own_z, own1, own2, own3, partner_z, partner1, partner2, partner3)
    grads = (gg, gg_other, gu, gu_other, gg_far, gg_far_other, gu_far, gu_far_other)
    grad_gate, grad_up = weight_grads(place, pieces, grads)
    grad_gate, grad_up, rest_far = lax.optimization_barrier((grad_gate, grad_up, rest_far))
    first = down_first.astype(F32) + first_far.astype(F32)
    rest = down_rest.astype(F32) + rest_far.astype(F32)
    grad_down = jnp.concatenate([first, rest], axis=0).astype(BF16)
    return grad_input, grad_gate, grad_up, grad_down


def solution(mesh):
    fine = Mesh(mesh.devices.reshape(2, NZ, NY, 2, 2), ("dp", "z", "y", "xh", "core"))
    tokens, col, row = ("dp", "z", "y"), ("xh", "core"), ("z", "y")
    in_specs = (
        P(tokens, col),
        P(tokens, col),
        P(("dp",) + col, row),
        P(("dp",) + col, row),
        P(col, row),
        P(col, row),
        P(row, col),
    )
    out_specs = (P(tokens, col), P(col, row), P(col, row), P(row, col))
    return jax.shard_map(body, mesh=fine, in_specs=in_specs, out_specs=out_specs, check_vma=False)
```

```python
import functools

import jax
import jax.numpy as jnp
from jax import lax
from jax.experimental import pallas as pl
from jax.experimental.pallas import tpu as pltpu
from jax.sharding import Mesh, PartitionSpec as P

F32, BF16 = jnp.float32, jnp.bfloat16
NZ, NY = 8, 4
HALF = 768
VMEM = pl.BlockSpec(memory_space=pltpu.VMEM)
SMEM = pl.BlockSpec(memory_space=pltpu.SMEM)
HBM = pl.BlockSpec(memory_space=pltpu.HBM)


def dot(left, right, left_dim, right_dim):
    dims = (((left_dim,), (right_dim,)), ((), ()))
    return lax.dot_general(left, right, dims, preferred_element_type=F32)


def from_ahead(x, axis, n, k):
    return lax.ppermute(x, axis, [((d + k) % n, d) for d in range(n)])


def swap(x, axis):
    return lax.ppermute(x, axis, [(0, 1), (1, 0)])


def grant(mib):
    return pltpu.CompilerParams(vmem_limit_bytes=mib << 20)


def in_hbm(x):
    return pltpu.with_memory_space_constraint(x, pltpu.HBM)


def prepare_kernel(grad_output, layer_input, mixed):
    mixed[:, :1536] = grad_output[...]
    mixed[:, 1536:] = layer_input[:, :HALF]


def prepare(grad_output, layer_input):
    return pl.pallas_call(
        prepare_kernel,
        out_shape=jax.ShapeDtypeStruct((32, 1536 + HALF), BF16),
        in_specs=[VMEM] * 2,
        out_specs=VMEM,
        compiler_params=grant(4),
    )(grad_output, layer_input)


def arrange_kernel(n, slot, cuts, place, *refs):
    for k in range(n):
        there = (place[slot] + k) % n
        for out, (low, high) in zip(refs[n:], cuts):
            out[there] = refs[k][:, low:high]


def arrange(place, slot, parts, cuts):
    n, rows = len(parts), parts[0].shape[0]
    outs = pl.pallas_call(
        functools.partial(arrange_kernel, n, slot, cuts),
        out_shape=tuple(jax.ShapeDtypeStruct((n, rows, high - low), BF16) for low, high in cuts),
        in_specs=[SMEM] + [VMEM] * n,
        out_specs=(VMEM,) * len(cuts),
        compiler_params=grant(6),
    )(place, *parts)
    return [out.reshape(n * rows, -1) for out in outs]


def hidden_grad_kernel(place, go, w_down, mine, send, rows, sems):
    copies = [
        pltpu.make_async_copy(go.at[pl.ds(512 * half, 512)], rows.at[half], sems.at[half])
        for half in range(2)
    ]
    for copy in copies:
        copy.start()
    for half, copy in enumerate(copies):
        copy.wait()
        part = dot(rows[half], w_down[...], 1, 1)
        for which in range(2):
            block = part[256 * which:256 * which + 256]

            @pl.when(place[3] == which)
            def _():
                mine[half] = block

            @pl.when(place[3] != which)
            def _():
                send[half] = block.astype(BF16)


def hidden_grad(place, go, w_down):
    return pl.pallas_call(
        hidden_grad_kernel,
        out_shape=(
            jax.ShapeDtypeStruct((2, 256, 512), F32),
            jax.ShapeDtypeStruct((2, 256, 512), BF16),
        ),
        in_specs=[SMEM, HBM, VMEM],
        out_specs=(VMEM,) * 2,
        scratch_shapes=[pltpu.VMEM((2, 512, 1536), BF16), pltpu.SemaphoreType.DMA((2,))],
        compiler_params=grant(16),
    )(place, in_hbm(go), w_down)


def input_grad_kernel(place, gg, gg_other, gu, gu_other, w_gate, w_up, out):
    def emit(gate_ref, up_ref, core):
        gate_rows, up_rows = gate_ref[...].reshape(512, 512), up_ref[...].reshape(512, 512)
        total = (dot(gate_rows, w_gate[...], 1, 1) + dot(up_rows, w_up[...], 1, 1)).astype(BF16)
        for half in range(2):
            start = pl.multiple_of(512 * half + 256 * core, 256)
            out[pl.ds(start, 256), :] = total[256 * half:256 * half + 256]

    emit(gg, gu, place[3])
    emit(gg_other, gu_other, 1 - place[3])


def input_grad(place, gg, gg_other, gu, gu_other, w_gate, w_up):
    weight = pl.BlockSpec((512, 512), lambda i: (i, 0))
    return pl.pallas_call(
        input_grad_kernel,
        grid=(3,),
        out_shape=jax.ShapeDtypeStruct((1024, 1536), BF16),
        in_specs=[SMEM] + [VMEM] * 4 + [weight] * 2,
        out_specs=pl.BlockSpec((1024, 512), lambda i: (0, i)),
        compiler_params=grant(16),
    )(place, gg, gg_other, gu, gu_other, w_gate, w_up)


def fill_natural(place, own, other, rows, col):
    for half in range(2):
        base = half * 512
        start = pl.multiple_of(base + place[3] * 256, 256)
        rows[pl.ds(start, 256), col:col + 512] = own[half]
        start = pl.multiple_of(base + (1 - place[3]) * 256, 256)
        rows[pl.ds(start, 256), col:col + 512] = other[half]


def down_kernel(place, hidden, hidden_other, go, out, rows):
    @pl.when(pl.program_id(0) == 0)
    def _():
        fill_natural(place, hidden, hidden_other, rows, 0)

    out[...] = dot(rows[...], go[...], 0, 0).astype(BF16)


def down_grad(place, hidden, hidden_other, go):
    return pl.pallas_call(
        down_kernel,
        grid=(3,),
        out_shape=jax.ShapeDtypeStruct((512, 1536), BF16),
        in_specs=[SMEM, VMEM, VMEM, pl.BlockSpec((1024, 512), lambda i: (0, i))],
        out_specs=pl.BlockSpec((512, 512), lambda i: (0, i)),
        scratch_shapes=[pltpu.VMEM((1024, 512), BF16)],
        compiler_params=grant(12),
    )(place, hidden, hidden_other, in_hbm(go))


def fill_rolled(place, own, other, rows, col):
    for half in range(2):
        for pair in range(2):
            for y in range(NY):
                k = (y - place[1] + NY) % NY
                lines = pl.ds(pair * 128 + y * 32, 32)
                z_own = 4 * half + 2 * place[3] + pair
                rows[k, z_own, :, col:col + 512] = own[half, lines, :]
                z_other = 4 * half + 2 * (1 - place[3]) + pair
                rows[k, z_other, :, col:col + 512] = other[half, lines, :]


def weight_kernel(place, own, *refs):
    pieces, grads, (d_gate, d_up, natural, rows) = refs[:8], refs[8:16], refs[16:]
    step = pl.program_id(0)

    @pl.when(step == 0)
    def _():
        fill_natural(place, *grads[0:2], natural, 0)
        fill_natural(place, *grads[2:4], natural, 512)
        for replica in range(2):
            fill_rolled(place, *grads[4 * replica:4 * replica + 2], rows.at[replica], 0)
            fill_rolled(place, *grads[4 * replica + 2:4 * replica + 4], rows.at[replica], 512)

    def rolled(replica):
        total = jnp.zeros((256, 1024), F32)
        for k in range(NY):
            total = total + dot(pieces[NY * replica + k][...], rows[replica, k].reshape(256, 1024), 0, 0)
        return total

    def emit(total):
        d_gate[...] = total[:, :512].astype(BF16)
        d_up[...] = total[:, 512:].astype(BF16)

    @pl.when(step < 3)
    def _():
        emit(dot(own[...], natural[...], 0, 0) + rolled(1))

    @pl.when(step >= 3)
    def _():
        emit(rolled(0) + rolled(1))


def weight_grads(place, own, own_pieces, partner_pieces, grads):
    tile = pl.BlockSpec((256, 512), lambda i: (i, 0))
    shape = jax.ShapeDtypeStruct((1536, 512), BF16)
    low = pl.BlockSpec((1024, 256), lambda i: (0, jnp.minimum(i, 2)))
    high = pl.BlockSpec((256, 256), lambda i: (0, jnp.maximum(i - 3, 0)))
    every = pl.BlockSpec((256, 256), lambda i: (0, i))
    high0, high1, high2, high3 = own_pieces
    partner0, partner1, partner2, partner3 = partner_pieces
    early = [in_hbm(x) for x in (own, high0, high1)]
    partner = [in_hbm(x) for x in (high3, partner0, partner1)]
    partner3 = in_hbm(partner3)
    near = [in_hbm(x) for x in grads[:4]]
    return pl.pallas_call(
        weight_kernel,
        grid=(6,),
        out_shape=(shape, shape),
        in_specs=[SMEM, low] + [high] * 4 + [every] * 4 + [VMEM] * 8,
        out_specs=(tile, tile),
        scratch_shapes=[pltpu.VMEM((1024, 1024), BF16), pltpu.VMEM((2, NY, NZ, 32, 1024), BF16)],
        compiler_params=grant(24),
    )(place, *early, high2, *partner, partner2, partner3, *near, *grads[4:])


def ring(x, axis, n):
    ahead, behind = [], []
    up, down = x, x
    for step in range(1, n // 2 + 1):
        up = from_ahead(up, axis, n, 1)
        ahead.append(up)
        if step < n // 2:
            down = from_ahead(down, axis, n, n - 1)
            behind.append(down)
    return [x] + ahead + behind[::-1]


def ordered(mine, other, index):
    low = jnp.where(index == 0, mine, other)
    high = jnp.where(index == 0, other, mine)
    return jnp.stack([low, high], axis=0)


def body(layer_input, grad_output, gate_saved, up_saved, w_gate, w_up, w_down):
    place = jnp.stack([lax.axis_index(name) for name in ("z", "y", "xh", "core")]).astype(jnp.int32)
    xh = place[2]

    mixed = prepare(grad_output, layer_input)
    mixed_parts = [mixed] + [from_ahead(mixed, "y", NY, k) for k in (1, 2, 3)]
    go_y, own_y = arrange(place, 1, mixed_parts, ((0, 1536), (1536, 1536 + HALF)))
    go = lax.all_gather(go_y, "z", axis=0, tiled=True)
    own_z, high_z = arrange(place, 0, ring(layer_input, "z", NZ), ((0, 1536), (HALF, 1536)))
    partner_z = swap(own_z, "dp")
    high1, high3 = from_ahead(high_z, "y", NY, 1), from_ahead(high_z, "y", NY, 3)

    gate = ordered(gate_saved, swap(gate_saved, "xh"), xh)
    up = ordered(up_saved, swap(up_saved, "xh"), xh)
    gate_val, up_val = gate.astype(F32), up.astype(F32)
    hidden = (gate_val * jax.nn.sigmoid(gate_val) * up_val).astype(BF16)
    hidden_other = swap(hidden, "core")
    go, gate, up, hidden, hidden_other, own_y, high_z, partner_z, high1, high3 = lax.optimization_barrier(
        (go, gate, up, hidden, hidden_other, own_y, high_z, partner_z, high1, high3)
    )

    own_low = lax.all_gather(own_y, "z", axis=0, tiled=True)
    partner1, partner3 = from_ahead(partner_z, "y", NY, 1), from_ahead(partner_z, "y", NY, 3)
    mine, send = hidden_grad(place, go, w_down)
    chip = mine + swap(send, "core").astype(F32)
    chip_far = swap(chip.astype(BF16), "xh")
    part_down = down_grad(place, hidden, hidden_other, go)

    chip, chip_far, part_down = lax.optimization_barrier((chip, chip_far, part_down))

    grad_hidden = chip + chip_far.astype(F32)
    gate_val, up_val = gate.astype(F32), up.astype(F32)
    sigma = jax.nn.sigmoid(gate_val)
    gg = (grad_hidden * up_val * sigma * (1.0 + gate_val * (1.0 - sigma))).astype(BF16)
    gu = (grad_hidden * gate_val * sigma).astype(BF16)
    gg_other, gu_other = swap(gg, "core"), swap(gu, "core")
    gg_other, gu_other, partner1, partner3 = lax.optimization_barrier((gg_other, gu_other, partner1, partner3))
    partial_in = input_grad(place, gg, gg_other, gu, gu_other, w_gate, w_up)
    in_z = lax.psum_scatter(partial_in, "z", scatter_dimension=0, tiled=True).reshape(NY, 32, 1536)

    gg_far, gu_far = swap(gg, "dp"), swap(gu, "dp")
    high2, partner2 = from_ahead(high_z, "y", NY, 2), from_ahead(partner_z, "y", NY, 2)
    gg_far, gu_far, part_down, high2 = lax.optimization_barrier((gg_far, gu_far, part_down, high2))
    down_far = swap(part_down, "dp")
    grads = (gg, gg_other, gu, gu_other, gg_far, swap(gg_far, "core"), gu_far, swap(gu_far, "core"))
    own_pieces, partner_pieces = (high_z, high1, high2, high3), (partner_z, partner1, partner2, partner3)
    grad_gate, grad_up = weight_grads(place, own_low, own_pieces, partner_pieces, grads)
    in_z, grad_gate, grad_up = lax.optimization_barrier((in_z, grad_gate, grad_up))

    y = place[1]
    total = lax.dynamic_index_in_dim(in_z, y, 0, keepdims=False).astype(F32)
    for k in range(1, NY):
        slab = lax.dynamic_index_in_dim(in_z, (y + k) % NY, 0, keepdims=False)
        total = total + from_ahead(slab, "y", NY, NY - k).astype(F32)
    grad_input = total.astype(BF16)
    grad_input, down_far = lax.optimization_barrier((grad_input, down_far))
    grad_down = (part_down.astype(F32) + down_far.astype(F32)).astype(BF16)
    return grad_input, grad_gate, grad_up, grad_down


def solution(mesh):
    fine = Mesh(mesh.devices.reshape(2, NZ, NY, 2, 2), ("dp", "z", "y", "xh", "core"))
    tokens, col, row = ("dp", "z", "y"), ("xh", "core"), ("z", "y")
    in_specs = (
        P(tokens, col),
        P(tokens, col),
        P(("dp",) + col, row),
        P(("dp",) + col, row),
        P(col, row),
        P(col, row),
        P(row, col),
    )
    out_specs = (P(tokens, col), P(col, row), P(col, row), P(row, col))
    return jax.shard_map(body, mesh=fine, in_specs=in_specs, out_specs=out_specs, check_vma=False)
```

```python
import functools

import jax
import jax.numpy as jnp
from jax import lax
from jax.experimental import pallas as pl
from jax.experimental.pallas import tpu as pltpu
from jax.sharding import Mesh, PartitionSpec as P

F32, BF16 = jnp.float32, jnp.bfloat16
NZ, NY = 8, 4
HALF = 768
VMEM = pl.BlockSpec(memory_space=pltpu.VMEM)
SMEM = pl.BlockSpec(memory_space=pltpu.SMEM)
HBM = pl.BlockSpec(memory_space=pltpu.HBM)


def dot(left, right, left_dim, right_dim):
    dims = (((left_dim,), (right_dim,)), ((), ()))
    return lax.dot_general(left, right, dims, preferred_element_type=F32)


def from_ahead(x, axis, n, k):
    return lax.ppermute(x, axis, [((d + k) % n, d) for d in range(n)])


def swap(x, axis):
    return lax.ppermute(x, axis, [(0, 1), (1, 0)])


def grant(mib):
    return pltpu.CompilerParams(vmem_limit_bytes=mib << 20)


def in_hbm(x):
    return pltpu.with_memory_space_constraint(x, pltpu.HBM)


def prepare_kernel(grad_output, layer_input, mixed):
    mixed[:, :1536] = grad_output[...]
    mixed[:, 1536:] = layer_input[:, :HALF]


def prepare(grad_output, layer_input):
    return pl.pallas_call(
        prepare_kernel,
        out_shape=jax.ShapeDtypeStruct((32, 1536 + HALF), BF16),
        in_specs=[VMEM] * 2,
        out_specs=VMEM,
        compiler_params=grant(4),
    )(in_hbm(grad_output), in_hbm(layer_input))


def arrange_kernel(n, slot, cuts, place, *refs):
    for k in range(n):
        there = (place[slot] + k) % n
        for out, (low, high) in zip(refs[n:], cuts):
            out[there] = refs[k][:, low:high]


def arrange(place, slot, parts, cuts):
    n, rows = len(parts), parts[0].shape[0]
    outs = pl.pallas_call(
        functools.partial(arrange_kernel, n, slot, cuts),
        out_shape=tuple(jax.ShapeDtypeStruct((n, rows, high - low), BF16) for low, high in cuts),
        in_specs=[SMEM] + [VMEM] * n,
        out_specs=(VMEM,) * len(cuts),
        compiler_params=grant(6),
    )(place, *parts)
    return [out.reshape(n * rows, -1) for out in outs]


def hidden_grad_kernel(place, go, w_down, mine, send, rows, sems):
    copies = [
        pltpu.make_async_copy(go.at[pl.ds(512 * half, 512)], rows.at[half], sems.at[half])
        for half in range(2)
    ]
    for copy in copies:
        copy.start()
    for half, copy in enumerate(copies):
        copy.wait()
        part = dot(rows[half], w_down[...], 1, 1)
        for which in range(2):
            block = part[256 * which:256 * which + 256]

            @pl.when(place[3] == which)
            def _():
                mine[half] = block

            @pl.when(place[3] != which)
            def _():
                send[half] = block.astype(BF16)


def hidden_grad(place, go, w_down):
    return pl.pallas_call(
        hidden_grad_kernel,
        out_shape=(
            jax.ShapeDtypeStruct((2, 256, 512), F32),
            jax.ShapeDtypeStruct((2, 256, 512), BF16),
        ),
        in_specs=[SMEM, HBM, VMEM],
        out_specs=(VMEM,) * 2,
        scratch_shapes=[pltpu.VMEM((2, 512, 1536), BF16), pltpu.SemaphoreType.DMA((2,))],
        compiler_params=grant(16),
    )(place, in_hbm(go), w_down)


def input_grad_kernel(place, gg, gg_other, gu, gu_other, w_gate, w_up, out):
    def emit(gate_ref, up_ref, core):
        gate_rows, up_rows = gate_ref[...].reshape(512, 512), up_ref[...].reshape(512, 512)
        total = (dot(gate_rows, w_gate[...], 1, 1) + dot(up_rows, w_up[...], 1, 1)).astype(BF16)
        for half in range(2):
            start = pl.multiple_of(512 * half + 256 * core, 256)
            out[pl.ds(start, 256), :] = total[256 * half:256 * half + 256]

    emit(gg, gu, place[3])
    emit(gg_other, gu_other, 1 - place[3])


def input_grad(place, gg, gg_other, gu, gu_other, w_gate, w_up):
    weight = pl.BlockSpec((512, 512), lambda i: (i, 0))
    return pl.pallas_call(
        input_grad_kernel,
        grid=(3,),
        out_shape=jax.ShapeDtypeStruct((1024, 1536), BF16),
        in_specs=[SMEM] + [VMEM] * 4 + [weight] * 2,
        out_specs=pl.BlockSpec((1024, 512), lambda i: (0, i)),
        compiler_params=grant(16),
    )(place, gg, gg_other, gu, gu_other, w_gate, w_up)


def fill_natural(place, own, other, rows, col):
    for half in range(2):
        base = half * 512
        start = pl.multiple_of(base + place[3] * 256, 256)
        rows[pl.ds(start, 256), col:col + 512] = own[half]
        start = pl.multiple_of(base + (1 - place[3]) * 256, 256)
        rows[pl.ds(start, 256), col:col + 512] = other[half]


def down_kernel(place, hidden, hidden_other, go, out, rows):
    @pl.when(pl.program_id(0) == 0)
    def _():
        fill_natural(place, hidden, hidden_other, rows, 0)

    out[...] = dot(rows[...], go[...], 0, 0).astype(BF16)


def down_grad(place, hidden, hidden_other, go):
    return pl.pallas_call(
        down_kernel,
        grid=(3,),
        out_shape=jax.ShapeDtypeStruct((512, 1536), BF16),
        in_specs=[SMEM, VMEM, VMEM, pl.BlockSpec((1024, 512), lambda i: (0, i))],
        out_specs=pl.BlockSpec((512, 512), lambda i: (0, i)),
        scratch_shapes=[pltpu.VMEM((1024, 512), BF16)],
        compiler_params=grant(12),
    )(place, hidden, hidden_other, in_hbm(go))


def fill_rolled(place, own, other, rows, col):
    for half in range(2):
        for pair in range(2):
            for y in range(NY):
                k = (y - place[1] + NY) % NY
                lines = pl.ds(pair * 128 + y * 32, 32)
                z_own = 4 * half + 2 * place[3] + pair
                rows[k, z_own, :, col:col + 512] = own[half, lines, :]
                z_other = 4 * half + 2 * (1 - place[3]) + pair
                rows[k, z_other, :, col:col + 512] = other[half, lines, :]


def own_kernel(place, own, p0, p1, p2, p3, gg, gg_other, gu, gu_other, d_gate, d_up, natural, rows):
    step = pl.program_id(0)

    @pl.when(step == 0)
    def _():
        fill_natural(place, gg, gg_other, natural, 0)
        fill_natural(place, gu, gu_other, natural, 512)
        fill_rolled(place, gg, gg_other, rows, 0)
        fill_rolled(place, gu, gu_other, rows, 512)

    def emit(total):
        d_gate[...] = total[:, :512].astype(BF16)
        d_up[...] = total[:, 512:].astype(BF16)

    @pl.when(step < 3)
    def _():
        emit(dot(own[...], natural[...], 0, 0))

    @pl.when(step >= 3)
    def _():
        total = jnp.zeros((256, 1024), F32)
        for k, piece in enumerate((p0, p1, p2, p3)):
            total = total + dot(piece[...], rows[k].reshape(256, 1024), 0, 0)
        emit(total)


def partner_kernel(place, p0, p1, p2, p3, gg, gg_other, gu, gu_other, own_gate, own_up, d_gate, d_up, rows):
    @pl.when(pl.program_id(0) == 0)
    def _():
        fill_rolled(place, gg, gg_other, rows, 0)
        fill_rolled(place, gu, gu_other, rows, 512)

    total = jnp.zeros((256, 1024), F32)
    for k, piece in enumerate((p0, p1, p2, p3)):
        total = total + dot(piece[...], rows[k].reshape(256, 1024), 0, 0)
    d_gate[...] = (total[:, :512].astype(BF16).astype(F32) + own_gate[...].astype(F32)).astype(BF16)
    d_up[...] = (total[:, 512:].astype(BF16).astype(F32) + own_up[...].astype(F32)).astype(BF16)


TILE = pl.BlockSpec((256, 512), lambda i: (i, 0))
WEIGHT = jax.ShapeDtypeStruct((1536, 512), BF16)
ROLLED = pltpu.VMEM((NY, NZ, 32, 1024), BF16)


def own_weight_grads(place, own, pieces, grads):
    low = pl.BlockSpec((1024, 256), lambda i: (0, jnp.minimum(i, 2)))
    high = pl.BlockSpec((256, 256), lambda i: (0, jnp.maximum(i - 3, 0)))
    return pl.pallas_call(
        own_kernel,
        grid=(6,),
        out_shape=(WEIGHT, WEIGHT),
        in_specs=[SMEM, low] + [high] * 4 + [VMEM] * 4,
        out_specs=(TILE, TILE),
        scratch_shapes=[pltpu.VMEM((1024, 1024), BF16), ROLLED],
        compiler_params=grant(16),
    )(place, in_hbm(own), *(in_hbm(x) for x in pieces), *grads)


def partner_weight_grads(place, pieces, grads, own_gate, own_up):
    every = pl.BlockSpec((256, 256), lambda i: (0, i))
    return pl.pallas_call(
        partner_kernel,
        grid=(6,),
        out_shape=(WEIGHT, WEIGHT),
        in_specs=[SMEM] + [every] * 4 + [VMEM] * 4 + [TILE] * 2,
        out_specs=(TILE, TILE),
        scratch_shapes=[ROLLED],
        compiler_params=grant(16),
    )(place, *(x if k == 2 else in_hbm(x) for k, x in enumerate(pieces)), *grads, own_gate, own_up)


def add_kernel(left, right, out):
    out[...] = (left[...].astype(F32) + right[...].astype(F32)).astype(BF16)


def add(left, right):
    block = pl.BlockSpec((128, 1536), lambda i: (i, 0))
    return pl.pallas_call(
        add_kernel,
        grid=(4,),
        out_shape=jax.ShapeDtypeStruct((512, 1536), BF16),
        in_specs=[block] * 2,
        out_specs=block,
        compiler_params=grant(8),
    )(left, right)


def ring(x, up, down, axis, n):
    ahead, behind = [up], [down]
    for step in range(2, n // 2 + 1):
        up = from_ahead(up, axis, n, 1)
        ahead.append(up)
        if step < n // 2:
            down = from_ahead(down, axis, n, n - 1)
            behind.append(down)
    return [x] + ahead + behind[::-1]


def ordered(mine, other, index):
    low = jnp.where(index == 0, mine, other)
    high = jnp.where(index == 0, other, mine)
    return jnp.stack([low, high], axis=0)


def body(layer_input, grad_output, gate_saved, up_saved, w_gate, w_up, w_down):
    place = jnp.stack([lax.axis_index(name) for name in ("z", "y", "xh", "core")]).astype(jnp.int32)
    xh = place[2]

    mixed = prepare(grad_output, layer_input)
    mixed_parts = [mixed] + [from_ahead(mixed, "y", NY, k) for k in (1, 2, 3)]
    z_up, z_down = from_ahead(layer_input, "z", NZ, 1), from_ahead(layer_input, "z", NZ, NZ - 1)
    mixed_parts, z_up, z_down = lax.optimization_barrier((mixed_parts, z_up, z_down))
    go_y, own_y = arrange(place, 1, mixed_parts, ((0, 1536), (1536, 1536 + HALF)))
    go = lax.all_gather(go_y, "z", axis=0, tiled=True)
    own_z, high_z = arrange(place, 0, ring(layer_input, z_up, z_down, "z", NZ), ((0, 1536), (HALF, 1536)))
    partner_z = swap(own_z, "dp")
    high1, high3 = from_ahead(high_z, "y", NY, 1), from_ahead(high_z, "y", NY, 3)

    gate = ordered(gate_saved, swap(gate_saved, "xh"), xh)
    up = ordered(up_saved, swap(up_saved, "xh"), xh)
    gate_val, up_val = gate.astype(F32), up.astype(F32)
    hidden = (gate_val * jax.nn.sigmoid(gate_val) * up_val).astype(BF16)
    hidden_other = swap(hidden, "core")
    go, gate, up, hidden, hidden_other, own_y, high_z, partner_z, high1, high3 = lax.optimization_barrier(
        (go, gate, up, hidden, hidden_other, own_y, high_z, partner_z, high1, high3)
    )

    own_low = lax.all_gather(own_y, "z", axis=0, tiled=True)
    partner1, partner3 = from_ahead(partner_z, "y", NY, 1), from_ahead(partner_z, "y", NY, 3)
    mine, send = hidden_grad(place, go, w_down)
    chip = mine + swap(send, "core").astype(F32)
    chip_far = swap(chip.astype(BF16), "xh")
    part_down = down_grad(place, hidden, hidden_other, go)

    chip, chip_far, part_down = lax.optimization_barrier((chip, chip_far, part_down))

    grad_hidden = chip + chip_far.astype(F32)
    gate_val, up_val = gate.astype(F32), up.astype(F32)
    sigma = jax.nn.sigmoid(gate_val)
    gg = (grad_hidden * up_val * sigma * (1.0 + gate_val * (1.0 - sigma))).astype(BF16)
    gu = (grad_hidden * gate_val * sigma).astype(BF16)
    gg_other, gu_other = swap(gg, "core"), swap(gu, "core")
    partial_in = input_grad(place, gg, gg_other, gu, gu_other, w_gate, w_up)
    partial_in, partner1, partner3 = lax.optimization_barrier((partial_in, partner1, partner3))
    in_z = lax.psum_scatter(partial_in, "z", scatter_dimension=0, tiled=True).reshape(NY, 32, 1536)

    gg_far, gu_far = swap(gg, "dp"), swap(gu, "dp")
    high2, partner2 = from_ahead(high_z, "y", NY, 2), from_ahead(partner_z, "y", NY, 2)
    gg_far, gu_far, part_down, high2 = lax.optimization_barrier((gg_far, gu_far, part_down, high2))
    down_far = swap(part_down, "dp")
    own_pieces, partner_pieces = (high_z, high1, high2, high3), (partner_z, partner1, partner2, partner3)
    own_gate, own_up = own_weight_grads(place, own_low, own_pieces, (gg, gg_other, gu, gu_other))
    far = (gg_far, swap(gg_far, "core"), gu_far, swap(gu_far, "core"))
    grad_gate, grad_up = partner_weight_grads(place, partner_pieces, far, own_gate, own_up)
    in_z, grad_gate, grad_up = lax.optimization_barrier((in_z, grad_gate, grad_up))

    y = place[1]
    total = lax.dynamic_index_in_dim(in_z, y, 0, keepdims=False).astype(F32)
    for k in range(1, NY):
        slab = lax.dynamic_index_in_dim(in_z, (y + k) % NY, 0, keepdims=False)
        total = total + from_ahead(slab, "y", NY, NY - k).astype(F32)
    grad_input = total.astype(BF16)
    grad_input, down_far = lax.optimization_barrier((grad_input, down_far))
    grad_down = add(part_down, down_far)
    return grad_input, grad_gate, grad_up, grad_down


def solution(mesh):
    fine = Mesh(mesh.devices.reshape(2, NZ, NY, 2, 2), ("dp", "z", "y", "xh", "core"))
    tokens, col, row = ("dp", "z", "y"), ("xh", "core"), ("z", "y")
    in_specs = (
        P(tokens, col),
        P(tokens, col),
        P(("dp",) + col, row),
        P(("dp",) + col, row),
        P(col, row),
        P(col, row),
        P(row, col),
    )
    out_specs = (P(tokens, col), P(col, row), P(col, row), P(row, col))
    return jax.shard_map(body, mesh=fine, in_specs=in_specs, out_specs=out_specs, check_vma=False)
```

```python
import functools

import jax
import jax.numpy as jnp
from jax import lax
from jax.experimental import pallas as pl
from jax.experimental.pallas import tpu as pltpu
from jax.sharding import Mesh, PartitionSpec as P

F32, BF16 = jnp.float32, jnp.bfloat16
NZ, NY = 8, 4
FIRST = 64
VMEM = pl.BlockSpec(memory_space=pltpu.VMEM)
SMEM = pl.BlockSpec(memory_space=pltpu.SMEM)
HBM = pl.BlockSpec(memory_space=pltpu.HBM)


def dot(left, right, left_dim, right_dim):
    dims = (((left_dim,), (right_dim,)), ((), ()))
    return lax.dot_general(left, right, dims, preferred_element_type=F32)


def from_ahead(x, axis, n, k):
    return lax.ppermute(x, axis, [((d + k) % n, d) for d in range(n)])


def swap(x, axis):
    return lax.ppermute(x, axis, [(0, 1), (1, 0)])


def grant(mib):
    return pltpu.CompilerParams(vmem_limit_bytes=mib << 20)


def in_hbm(x):
    return pltpu.with_memory_space_constraint(x, pltpu.HBM)


def arrange_kernel(n, slot, place, *refs):
    for k in range(n):
        refs[n][(place[slot] + k) % n] = refs[k][...]


def arrange(place, slot, parts):
    n, (rows, cols) = len(parts), parts[0].shape
    out = pl.pallas_call(
        functools.partial(arrange_kernel, n, slot),
        out_shape=jax.ShapeDtypeStruct((n, rows, cols), BF16),
        in_specs=[SMEM] + [VMEM] * n,
        out_specs=VMEM,
        compiler_params=grant(6),
    )(place, in_hbm(parts[0]), *parts[1:])
    return out.reshape(n * rows, cols)


def hidden_grad_kernel(place, go, w_down, mine, send, rows, sems):
    copies = [
        pltpu.make_async_copy(go.at[pl.ds(512 * half, 512)], rows.at[half], sems.at[half])
        for half in range(2)
    ]
    for copy in copies:
        copy.start()
    for half, copy in enumerate(copies):
        copy.wait()
        part = dot(rows[half], w_down[...], 1, 1)
        for which in range(2):
            block = part[256 * which:256 * which + 256]

            @pl.when(place[3] == which)
            def _():
                mine[half] = block

            @pl.when(place[3] != which)
            def _():
                send[half] = block.astype(BF16)


def hidden_grad(place, go, w_down):
    return pl.pallas_call(
        hidden_grad_kernel,
        out_shape=(
            jax.ShapeDtypeStruct((2, 256, 512), F32),
            jax.ShapeDtypeStruct((2, 256, 512), BF16),
        ),
        in_specs=[SMEM, HBM, VMEM],
        out_specs=(VMEM,) * 2,
        scratch_shapes=[pltpu.VMEM((2, 512, 1536), BF16), pltpu.SemaphoreType.DMA((2,))],
        compiler_params=grant(16),
    )(place, in_hbm(go), w_down)


def input_grad_kernel(place, gg, gg_other, gu, gu_other, w_gate, w_up, out):
    def emit(gate_ref, up_ref, core):
        gate_rows, up_rows = gate_ref[...].reshape(512, 512), up_ref[...].reshape(512, 512)
        total = (dot(gate_rows, w_gate[...], 1, 1) + dot(up_rows, w_up[...], 1, 1)).astype(BF16)
        for half in range(2):
            start = pl.multiple_of(512 * half + 256 * core, 256)
            out[pl.ds(start, 256), :] = total[256 * half:256 * half + 256]

    emit(gg, gu, place[3])
    emit(gg_other, gu_other, 1 - place[3])


def input_grad(place, gg, gg_other, gu, gu_other, w_gate, w_up):
    weight = pl.BlockSpec((512, 512), lambda i: (i, 0))
    return pl.pallas_call(
        input_grad_kernel,
        grid=(3,),
        out_shape=jax.ShapeDtypeStruct((1024, 1536), BF16),
        in_specs=[SMEM] + [VMEM] * 4 + [weight] * 2,
        out_specs=pl.BlockSpec((1024, 512), lambda i: (0, i)),
        compiler_params=grant(16),
    )(place, gg, gg_other, gu, gu_other, w_gate, w_up)


def fill_natural(place, own, other, rows, col):
    for half in range(2):
        base = half * 512
        start = pl.multiple_of(base + place[3] * 256, 256)
        rows[pl.ds(start, 256), col:col + 512] = own[half]
        start = pl.multiple_of(base + (1 - place[3]) * 256, 256)
        rows[pl.ds(start, 256), col:col + 512] = other[half]


def down_kernel(place, hidden, hidden_other, go, first, rest, rows):
    @pl.when(pl.program_id(0) == 0)
    def _():
        fill_natural(place, hidden, hidden_other, rows, 0)

    total = dot(rows[...], go[...], 0, 0).astype(BF16)
    first[...] = total[:FIRST]
    rest[...] = total[FIRST:]


def down_grad(place, hidden, hidden_other, go):
    return pl.pallas_call(
        down_kernel,
        grid=(3,),
        out_shape=(
            jax.ShapeDtypeStruct((FIRST, 1536), BF16),
            jax.ShapeDtypeStruct((512 - FIRST, 1536), BF16),
        ),
        in_specs=[SMEM, VMEM, VMEM, pl.BlockSpec((1024, 512), lambda i: (0, i))],
        out_specs=(
            pl.BlockSpec((FIRST, 512), lambda i: (0, i)),
            pl.BlockSpec((512 - FIRST, 512), lambda i: (0, i)),
        ),
        scratch_shapes=[pltpu.VMEM((1024, 512), BF16)],
        compiler_params=grant(12),
    )(place, hidden, hidden_other, in_hbm(go))


def fill_rolled(place, own, other, rows, col):
    for half in range(2):
        for pair in range(2):
            for y in range(NY):
                k = (y - place[1] + NY) % NY
                lines = pl.ds(pair * 128 + y * 32, 32)
                z_own = 4 * half + 2 * place[3] + pair
                rows[k, z_own, :, col:col + 512] = own[half, lines, :]
                z_other = 4 * half + 2 * (1 - place[3]) + pair
                rows[k, z_other, :, col:col + 512] = other[half, lines, :]


def rolled_total(place, pieces, grads, rows):
    @pl.when(pl.program_id(0) == 0)
    def _():
        fill_rolled(place, *grads[:2], rows, 0)
        fill_rolled(place, *grads[2:], rows, 512)

    total = jnp.zeros((256, 1024), F32)
    for k, piece in enumerate(pieces):
        total = total + dot(piece[...], rows[k].reshape(256, 1024), 0, 0)
    return total.astype(BF16)


def own_kernel(place, *refs):
    total = rolled_total(place, refs[:4], refs[4:8], refs[10])
    refs[8][...] = total[:, :512]
    refs[9][...] = total[:, 512:]


def partner_kernel(place, *refs):
    total = rolled_total(place, refs[:4], refs[4:8], refs[12]).astype(F32)
    refs[10][...] = (total[:, :512] + refs[8][...].astype(F32)).astype(BF16)
    refs[11][...] = (total[:, 512:] + refs[9][...].astype(F32)).astype(BF16)


TILE = pl.BlockSpec((256, 512), lambda i: (i, 0))
WEIGHT = jax.ShapeDtypeStruct((1536, 512), BF16)
ROLLED = pltpu.VMEM((NY, NZ, 32, 1024), BF16)


def own_weight_grads(place, pieces, grads):
    every = pl.BlockSpec((256, 256), lambda i: (0, i))
    return pl.pallas_call(
        own_kernel,
        grid=(6,),
        out_shape=(WEIGHT, WEIGHT),
        in_specs=[SMEM] + [every] * 4 + [VMEM] * 4,
        out_specs=(TILE, TILE),
        scratch_shapes=[ROLLED],
        compiler_params=grant(16),
    )(place, *(in_hbm(x) for x in pieces), *grads)


def partner_weight_grads(place, pieces, grads, own_gate, own_up):
    every = pl.BlockSpec((256, 256), lambda i: (0, i))
    return pl.pallas_call(
        partner_kernel,
        grid=(6,),
        out_shape=(WEIGHT, WEIGHT),
        in_specs=[SMEM] + [every] * 4 + [VMEM] * 4 + [TILE] * 2,
        out_specs=(TILE, TILE),
        scratch_shapes=[ROLLED],
        compiler_params=grant(16),
    )(place, in_hbm(pieces[0]), *pieces[1:], *grads, own_gate, own_up)


def add_kernel(first, first_far, rest, rest_far, out):
    out[:FIRST] = (first[...].astype(F32) + first_far[...].astype(F32)).astype(BF16)
    out[FIRST:] = (rest[...].astype(F32) + rest_far[...].astype(F32)).astype(BF16)


def add(first, first_far, rest, rest_far):
    top = pl.BlockSpec((FIRST, 512), lambda i: (0, i))
    low = pl.BlockSpec((512 - FIRST, 512), lambda i: (0, i))
    return pl.pallas_call(
        add_kernel,
        grid=(3,),
        out_shape=jax.ShapeDtypeStruct((512, 1536), BF16),
        in_specs=[top, top, low, low],
        out_specs=pl.BlockSpec((512, 512), lambda i: (0, i)),
        compiler_params=grant(8),
    )(first, first_far, rest, rest_far)


def ring(x, up, down, axis, n):
    ahead, behind = [up], [down]
    for step in range(2, n // 2 + 1):
        up = from_ahead(up, axis, n, 1)
        ahead.append(up)
        if step < n // 2:
            down = from_ahead(down, axis, n, n - 1)
            behind.append(down)
    return [x] + ahead + behind[::-1]


def ordered(mine, other, index):
    low = jnp.where(index == 0, mine, other)
    high = jnp.where(index == 0, other, mine)
    return jnp.stack([low, high], axis=0)


def body(layer_input, grad_output, gate_saved, up_saved, w_gate, w_up, w_down):
    place = jnp.stack([lax.axis_index(name) for name in ("z", "y", "xh", "core")]).astype(jnp.int32)
    xh = place[2]

    go_parts = [grad_output] + [from_ahead(grad_output, "y", NY, k) for k in (1, 2, 3)]
    z_up, z_down = from_ahead(layer_input, "z", NZ, 1), from_ahead(layer_input, "z", NZ, NZ - 1)
    go_parts, z_up, z_down = lax.optimization_barrier((go_parts, z_up, z_down))
    go = lax.all_gather(arrange(place, 1, go_parts), "z", axis=0, tiled=True)
    own_z = arrange(place, 0, ring(layer_input, z_up, z_down, "z", NZ))
    partner_z = swap(own_z, "dp")
    own1, own3 = from_ahead(own_z, "y", NY, 1), from_ahead(own_z, "y", NY, 3)

    gate = ordered(gate_saved, swap(gate_saved, "xh"), xh)
    up = ordered(up_saved, swap(up_saved, "xh"), xh)
    gate_val, up_val = gate.astype(F32), up.astype(F32)
    hidden = (gate_val * jax.nn.sigmoid(gate_val) * up_val).astype(BF16)
    hidden_other = swap(hidden, "core")
    go, gate, up, hidden, hidden_other, own_z, partner_z, own1, own3 = lax.optimization_barrier(
        (go, gate, up, hidden, hidden_other, own_z, partner_z, own1, own3)
    )

    own2 = from_ahead(own_z, "y", NY, 2)
    mine, send = hidden_grad(place, go, w_down)
    chip = mine + swap(send, "core").astype(F32)
    chip_far = swap(chip.astype(BF16), "xh")
    down_first, down_rest = down_grad(place, hidden, hidden_other, go)

    chip, chip_far, down_first, down_rest = lax.optimization_barrier((chip, chip_far, down_first, down_rest))
    first_far = swap(down_first, "dp")

    grad_hidden = chip + chip_far.astype(F32)
    gate_val, up_val = gate.astype(F32), up.astype(F32)
    sigma = jax.nn.sigmoid(gate_val)
    gg = (grad_hidden * up_val * sigma * (1.0 + gate_val * (1.0 - sigma))).astype(BF16)
    gu = (grad_hidden * gate_val * sigma).astype(BF16)
    gg_other, gu_other = swap(gg, "core"), swap(gu, "core")
    partial_in = input_grad(place, gg, gg_other, gu, gu_other, w_gate, w_up)
    partial_in, own2, first_far = lax.optimization_barrier((partial_in, own2, first_far))
    in_z = lax.psum_scatter(partial_in, "z", scatter_dimension=0, tiled=True).reshape(NY, 32, 1536)

    gg_far, gu_far = swap(gg, "dp"), swap(gu, "dp")
    partner_pieces = [partner_z] + [from_ahead(partner_z, "y", NY, k) for k in (1, 2, 3)]
    own_gate, own_up = own_weight_grads(place, (own_z, own1, own2, own3), (gg, gg_other, gu, gu_other))
    gg_far, gu_far, down_rest, own_gate, own_up = lax.optimization_barrier(
        (gg_far, gu_far, down_rest, own_gate, own_up)
    )
    rest_far = swap(down_rest, "dp")
    far = (gg_far, swap(gg_far, "core"), gu_far, swap(gu_far, "core"))
    grad_gate, grad_up = partner_weight_grads(place, partner_pieces, far, own_gate, own_up)
    in_z, grad_gate, grad_up = lax.optimization_barrier((in_z, grad_gate, grad_up))

    y = place[1]
    total = lax.dynamic_index_in_dim(in_z, y, 0, keepdims=False).astype(F32)
    for k in range(1, NY):
        slab = lax.dynamic_index_in_dim(in_z, (y + k) % NY, 0, keepdims=False)
        total = total + from_ahead(slab, "y", NY, NY - k).astype(F32)
    grad_input = total.astype(BF16)
    grad_input, rest_far = lax.optimization_barrier((grad_input, rest_far))
    return grad_input, grad_gate, grad_up, add(down_first, first_far, down_rest, rest_far)


def solution(mesh):
    fine = Mesh(mesh.devices.reshape(2, NZ, NY, 2, 2), ("dp", "z", "y", "xh", "core"))
    tokens, col, row = ("dp", "z", "y"), ("xh", "core"), ("z", "y")
    in_specs = (
        P(tokens, col),
        P(tokens, col),
        P(("dp",) + col, row),
        P(("dp",) + col, row),
        P(col, row),
        P(col, row),
        P(row, col),
    )
    out_specs = (P(tokens, col), P(col, row), P(col, row), P(row, col))
    return jax.shard_map(body, mesh=fine, in_specs=in_specs, out_specs=out_specs, check_vma=False)
```

```python
import functools

import jax
import jax.numpy as jnp
from jax import lax
from jax.experimental import pallas as pl
from jax.experimental.pallas import tpu as pltpu
from jax.sharding import Mesh, PartitionSpec as P

F32, BF16 = jnp.float32, jnp.bfloat16
NZ, NY = 8, 4
FIRST = 64
VMEM = pl.BlockSpec(memory_space=pltpu.VMEM)
SMEM = pl.BlockSpec(memory_space=pltpu.SMEM)
HBM = pl.BlockSpec(memory_space=pltpu.HBM)


def dot(left, right, left_dim, right_dim):
    dims = (((left_dim,), (right_dim,)), ((), ()))
    return lax.dot_general(left, right, dims, preferred_element_type=F32)


def from_ahead(x, axis, n, k):
    return lax.ppermute(x, axis, [((d + k) % n, d) for d in range(n)])


def swap(x, axis):
    return lax.ppermute(x, axis, [(0, 1), (1, 0)])


def grant(mib):
    return pltpu.CompilerParams(vmem_limit_bytes=mib << 20)


def in_hbm(x):
    return pltpu.with_memory_space_constraint(x, pltpu.HBM)


def arrange_kernel(n, slot, place, *refs):
    for k in range(n):
        refs[n][(place[slot] + k) % n] = refs[k][...]


def arrange(place, slot, parts):
    n, (rows, cols) = len(parts), parts[0].shape
    out = pl.pallas_call(
        functools.partial(arrange_kernel, n, slot),
        out_shape=jax.ShapeDtypeStruct((n, rows, cols), BF16),
        in_specs=[SMEM] + [VMEM] * n,
        out_specs=VMEM,
        compiler_params=grant(6),
    )(place, in_hbm(parts[0]), *parts[1:])
    return out.reshape(n * rows, cols)


def hidden_grad_kernel(place, go, w_down, mine, send, rows, sems):
    copies = [
        pltpu.make_async_copy(go.at[pl.ds(512 * half, 512)], rows.at[half], sems.at[half])
        for half in range(2)
    ]
    for copy in copies:
        copy.start()
    for half, copy in enumerate(copies):
        copy.wait()
        part = dot(rows[half], w_down[...], 1, 1)
        for which in range(2):
            block = part[256 * which:256 * which + 256]

            @pl.when(place[3] == which)
            def _():
                mine[half] = block

            @pl.when(place[3] != which)
            def _():
                send[half] = block.astype(BF16)


def hidden_grad(place, go, w_down):
    return pl.pallas_call(
        hidden_grad_kernel,
        out_shape=(
            jax.ShapeDtypeStruct((2, 256, 512), F32),
            jax.ShapeDtypeStruct((2, 256, 512), BF16),
        ),
        in_specs=[SMEM, HBM, VMEM],
        out_specs=(VMEM,) * 2,
        scratch_shapes=[pltpu.VMEM((2, 512, 1536), BF16), pltpu.SemaphoreType.DMA((2,))],
        compiler_params=grant(16),
    )(place, in_hbm(go), w_down)


def act_kernel(chip, chip_far, gate, up, out0, out1):
    def rows(i, carry):
        lines = pl.ds(pl.multiple_of(i * 32, 32), 32)
        for half, out in enumerate((out0, out1)):
            grad_hidden = chip[half, lines, :] + chip_far[half, lines, :].astype(F32)
            gate_val, up_val = gate[half, lines, :].astype(F32), up[half, lines, :].astype(F32)
            sigma = jax.nn.sigmoid(gate_val)
            out[0, lines, :] = (grad_hidden * up_val * sigma * (1.0 + gate_val * (1.0 - sigma))).astype(BF16)
            out[1, lines, :] = (grad_hidden * gate_val * sigma).astype(BF16)
        return carry

    lax.fori_loop(0, 8, rows, 0)


def act_grad(chip, chip_far, gate, up):
    shape = jax.ShapeDtypeStruct((2, 256, 512), BF16)
    return pl.pallas_call(
        act_kernel,
        out_shape=(shape, shape),
        in_specs=[VMEM] * 4,
        out_specs=(VMEM,) * 2,
        compiler_params=grant(8),
    )(chip, chip_far, gate, up)


def input_grad_kernel(place, near0, near1, other0, other1, w_gate, w_up, out):
    for refs, core in (((near0, near1), place[3]), ((other0, other1), 1 - place[3])):
        for half, ref in enumerate(refs):
            total = dot(ref[0], w_gate[...], 1, 1) + dot(ref[1], w_up[...], 1, 1)
            start = pl.multiple_of(512 * half + 256 * core, 256)
            out[pl.ds(start, 256), :] = total.astype(BF16)


def input_grad(place, near, other, w_gate, w_up):
    weight = pl.BlockSpec((512, 512), lambda i: (i, 0))
    return pl.pallas_call(
        input_grad_kernel,
        grid=(3,),
        out_shape=jax.ShapeDtypeStruct((1024, 1536), BF16),
        in_specs=[SMEM] + [VMEM] * 4 + [weight] * 2,
        out_specs=pl.BlockSpec((1024, 512), lambda i: (0, i)),
        compiler_params=grant(16),
    )(place, *near, *other, w_gate, w_up)


def fill_natural(place, own, other, rows, col):
    for half in range(2):
        base = half * 512
        start = pl.multiple_of(base + place[3] * 256, 256)
        rows[pl.ds(start, 256), col:col + 512] = own[half]
        start = pl.multiple_of(base + (1 - place[3]) * 256, 256)
        rows[pl.ds(start, 256), col:col + 512] = other[half]


def down_kernel(place, hidden, hidden_other, go, first, rest, rows):
    @pl.when(pl.program_id(0) == 0)
    def _():
        fill_natural(place, hidden, hidden_other, rows, 0)

    total = dot(rows[...], go[...], 0, 0).astype(BF16)
    first[...] = total[:FIRST]
    rest[...] = total[FIRST:]


def down_grad(place, hidden, hidden_other, go):
    return pl.pallas_call(
        down_kernel,
        grid=(3,),
        out_shape=(
            jax.ShapeDtypeStruct((FIRST, 1536), BF16),
            jax.ShapeDtypeStruct((512 - FIRST, 1536), BF16),
        ),
        in_specs=[SMEM, VMEM, VMEM, pl.BlockSpec((1024, 512), lambda i: (0, i))],
        out_specs=(
            pl.BlockSpec((FIRST, 512), lambda i: (0, i)),
            pl.BlockSpec((512 - FIRST, 512), lambda i: (0, i)),
        ),
        scratch_shapes=[pltpu.VMEM((1024, 512), BF16)],
        compiler_params=grant(12),
    )(place, hidden, hidden_other, in_hbm(go))


def fill_rolled(place, near, other, rows):
    for refs, core in ((near, place[3]), (other, 1 - place[3])):
        for half, ref in enumerate(refs):
            for pair in range(2):
                z = 4 * half + 2 * core + pair
                for y in range(NY):
                    k = (y - place[1] + NY) % NY
                    lines = slice(pair * 128 + y * 32, pair * 128 + y * 32 + 32)
                    rows[k, z, :, :512] = ref[0, lines, :]
                    rows[k, z, :, 512:] = ref[1, lines, :]


def rolled_total(place, pieces, grads, rows):
    @pl.when(pl.program_id(0) == 0)
    def _():
        fill_rolled(place, grads[:2], grads[2:], rows)

    total = jnp.zeros((256, 1024), F32)
    for k, piece in enumerate(pieces):
        total = total + dot(piece[...], rows[k].reshape(256, 1024), 0, 0)
    return total.astype(BF16)


def own_kernel(place, *refs):
    total = rolled_total(place, refs[:4], refs[4:8], refs[10])
    refs[8][...] = total[:, :512]
    refs[9][...] = total[:, 512:]


def partner_kernel(place, *refs):
    total = rolled_total(place, refs[:4], refs[4:8], refs[12]).astype(F32)
    refs[10][...] = (total[:, :512] + refs[8][...].astype(F32)).astype(BF16)
    refs[11][...] = (total[:, 512:] + refs[9][...].astype(F32)).astype(BF16)


TILE = pl.BlockSpec((256, 512), lambda i: (i, 0))
WEIGHT = jax.ShapeDtypeStruct((1536, 512), BF16)
ROLLED = pltpu.VMEM((NY, NZ, 32, 1024), BF16)


def own_weight_grads(place, pieces, grads):
    every = pl.BlockSpec((256, 256), lambda i: (0, i))
    return pl.pallas_call(
        own_kernel,
        grid=(6,),
        out_shape=(pltpu.HBM((1536, 512), BF16),) * 2,
        in_specs=[SMEM] + [every] * 4 + [VMEM] * 4,
        out_specs=(TILE, TILE),
        scratch_shapes=[ROLLED],
        compiler_params=grant(16),
    )(place, *(in_hbm(x) for x in pieces), *grads)


def partner_weight_grads(place, pieces, grads, own_gate, own_up):
    every = pl.BlockSpec((256, 256), lambda i: (0, i))
    return pl.pallas_call(
        partner_kernel,
        grid=(6,),
        out_shape=(WEIGHT, WEIGHT),
        in_specs=[SMEM] + [every] * 4 + [VMEM] * 4 + [TILE] * 2,
        out_specs=(TILE, TILE),
        scratch_shapes=[ROLLED],
        compiler_params=grant(16),
    )(place, *(in_hbm(x) for x in pieces), *grads, in_hbm(own_gate), in_hbm(own_up))


def add_kernel(first, first_far, rest, rest_far, out):
    out[:FIRST] = (first[...].astype(F32) + first_far[...].astype(F32)).astype(BF16)
    out[FIRST:] = (rest[...].astype(F32) + rest_far[...].astype(F32)).astype(BF16)


def add(first, first_far, rest, rest_far):
    top = pl.BlockSpec((FIRST, 512), lambda i: (0, i))
    low = pl.BlockSpec((512 - FIRST, 512), lambda i: (0, i))
    return pl.pallas_call(
        add_kernel,
        grid=(3,),
        out_shape=jax.ShapeDtypeStruct((512, 1536), BF16),
        in_specs=[top, top, low, low],
        out_specs=pl.BlockSpec((512, 512), lambda i: (0, i)),
        compiler_params=grant(8),
    )(first, first_far, rest, rest_far)


def ring(x, up, down, axis, n):
    ahead, behind = [up], [down]
    for step in range(2, n // 2 + 1):
        up = from_ahead(up, axis, n, 1)
        ahead.append(up)
        if step < n // 2:
            down = from_ahead(down, axis, n, n - 1)
            behind.append(down)
    return [x] + ahead + behind[::-1]


def ordered(mine, other, index):
    low = jnp.where(index == 0, mine, other)
    high = jnp.where(index == 0, other, mine)
    return jnp.stack([low, high], axis=0)


def body(layer_input, grad_output, gate_saved, up_saved, w_gate, w_up, w_down):
    place = jnp.stack([lax.axis_index(name) for name in ("z", "y", "xh", "core")]).astype(jnp.int32)
    xh = place[2]

    go_parts = [grad_output] + [from_ahead(grad_output, "y", NY, k) for k in (1, 2, 3)]
    z_up, z_down = from_ahead(layer_input, "z", NZ, 1), from_ahead(layer_input, "z", NZ, NZ - 1)
    go_parts, z_up, z_down = lax.optimization_barrier((go_parts, z_up, z_down))
    go = lax.all_gather(arrange(place, 1, go_parts), "z", axis=0, tiled=True)
    own_z = arrange(place, 0, ring(layer_input, z_up, z_down, "z", NZ))
    partner_z = swap(own_z, "dp")
    own1, own3 = from_ahead(own_z, "y", NY, 1), from_ahead(own_z, "y", NY, 3)

    gate = ordered(gate_saved, swap(gate_saved, "xh"), xh)
    up = ordered(up_saved, swap(up_saved, "xh"), xh)
    gate_val, up_val = gate.astype(F32), up.astype(F32)
    hidden = (gate_val * jax.nn.sigmoid(gate_val) * up_val).astype(BF16)
    hidden_other = swap(hidden, "core")
    go, gate, up, hidden, hidden_other, own_z, partner_z, own1, own3 = lax.optimization_barrier(
        (go, gate, up, hidden, hidden_other, own_z, partner_z, own1, own3)
    )

    own2 = from_ahead(own_z, "y", NY, 2)
    mine, send = hidden_grad(place, go, w_down)
    chip = mine + swap(send, "core").astype(F32)
    chip_far = swap(chip.astype(BF16), "xh")
    down_first, down_rest = down_grad(place, hidden, hidden_other, go)

    chip, chip_far, down_first, down_rest = lax.optimization_barrier((chip, chip_far, down_first, down_rest))
    first_far = swap(down_first, "dp")

    near = act_grad(chip, chip_far, gate, up)
    other = [swap(half, "core") for half in near]
    partial_in = input_grad(place, near, other, w_gate, w_up)
    partial_in, own2, first_far = lax.optimization_barrier((partial_in, own2, first_far))
    in_z = lax.psum_scatter(partial_in, "z", scatter_dimension=0, tiled=True).reshape(NY, 32, 1536)

    far = [swap(near[0], "dp"), lax.ppermute(near[1], ("dp", "xh"), [(0, 3), (3, 0), (1, 2), (2, 1)])]
    partner1, partner2, partner3 = (from_ahead(partner_z, "y", NY, k) for k in (1, 2, 3))
    own_gate, own_up = own_weight_grads(place, (own_z, own1, own2, own3), (*near, *other))
    far, down_rest, own_gate, own_up, partner1, partner3 = lax.optimization_barrier(
        (far, down_rest, own_gate, own_up, partner1, partner3)
    )
    rest_far = swap(down_rest, "dp")
    far_other = [swap(half, "core") for half in far]

    y = place[1]
    slabs = [lax.dynamic_index_in_dim(in_z, (y + k) % NY, 0, keepdims=False) for k in range(NY)]
    partner = [partner_z, partner1, partner2, partner3]
    slabs, partner, far, far_other = lax.optimization_barrier((slabs, partner, far, far_other))
    total = slabs[0].astype(F32)
    for k in range(1, NY):
        total = total + from_ahead(slabs[k], "y", NY, NY - k).astype(F32)
    grad_input = total.astype(BF16)
    grad_gate, grad_up = partner_weight_grads(place, partner, (*far, *far_other), own_gate, own_up)
    grad_input, grad_gate, grad_up, rest_far = lax.optimization_barrier((grad_input, grad_gate, grad_up, rest_far))
    return grad_input, grad_gate, grad_up, add(down_first, first_far, down_rest, rest_far)


def solution(mesh):
    fine = Mesh(mesh.devices.reshape(2, NZ, NY, 2, 2), ("dp", "z", "y", "xh", "core"))
    tokens, col, row = ("dp", "z", "y"), ("xh", "core"), ("z", "y")
    in_specs = (
        P(tokens, col),
        P(tokens, col),
        P(("dp",) + col, row),
        P(("dp",) + col, row),
        P(col, row),
        P(col, row),
        P(row, col),
    )
    out_specs = (P(tokens, col), P(col, row), P(col, row), P(row, col))
    return jax.shard_map(body, mesh=fine, in_specs=in_specs, out_specs=out_specs, check_vma=False)
```

```python
import functools

import jax
import jax.numpy as jnp
from jax import lax
from jax.experimental import pallas as pl
from jax.experimental.pallas import tpu as pltpu
from jax.sharding import Mesh, PartitionSpec as P

F32, BF16 = jnp.float32, jnp.bfloat16
NZ, NY = 8, 4
FIRST = 64
VMEM = pl.BlockSpec(memory_space=pltpu.VMEM)
SMEM = pl.BlockSpec(memory_space=pltpu.SMEM)
HBM = pl.BlockSpec(memory_space=pltpu.HBM)


def dot(left, right, left_dim, right_dim):
    dims = (((left_dim,), (right_dim,)), ((), ()))
    return lax.dot_general(left, right, dims, preferred_element_type=F32)


def from_ahead(x, axis, n, k):
    return lax.ppermute(x, axis, [((d + k) % n, d) for d in range(n)])


def swap(x, axis):
    return lax.ppermute(x, axis, [(0, 1), (1, 0)])


def grant(mib):
    return pltpu.CompilerParams(vmem_limit_bytes=mib << 20)


def in_hbm(x):
    return pltpu.with_memory_space_constraint(x, pltpu.HBM)


def arrange_kernel(n, slot, place, *refs):
    for k in range(n):
        refs[n][(place[slot] + k) % n] = refs[k][...]


def arrange(place, slot, parts):
    n, (rows, cols) = len(parts), parts[0].shape
    out = pl.pallas_call(
        functools.partial(arrange_kernel, n, slot),
        out_shape=jax.ShapeDtypeStruct((n, rows, cols), BF16),
        in_specs=[SMEM] + [VMEM] * n,
        out_specs=VMEM,
        compiler_params=grant(6),
    )(place, in_hbm(parts[0]), *parts[1:])
    return out.reshape(n * rows, cols)


def hidden_grad_kernel(far, place, go, w_down, out, rows, weight, sems):
    core = 1 - place[3] if far else place[3]
    copies = [pltpu.make_async_copy(w_down, weight, sems.at[2])]
    for half in range(2):
        start = pl.multiple_of(512 * half + 256 * core, 256)
        copies.append(pltpu.make_async_copy(go.at[pl.ds(start, 256)], rows.at[half], sems.at[half]))
    for copy in copies:
        copy.start()
    copies[0].wait()
    for half in range(2):
        copies[1 + half].wait()
        out[half] = dot(rows[half], weight[...], 1, 1).astype(out.dtype)


def hidden_grad(place, go, w_down, far):
    return pl.pallas_call(
        functools.partial(hidden_grad_kernel, far),
        out_shape=jax.ShapeDtypeStruct((2, 256, 512), BF16 if far else F32),
        in_specs=[SMEM, HBM, HBM],
        out_specs=VMEM,
        scratch_shapes=[
            pltpu.VMEM((2, 256, 1536), BF16),
            pltpu.VMEM((512, 1536), BF16),
            pltpu.SemaphoreType.DMA((3,)),
        ],
        compiler_params=grant(12),
    )(place, in_hbm(go), in_hbm(w_down))


def act_kernel(chip, chip_far, gate, up, out0, out1):
    def rows(i, carry):
        lines = pl.ds(pl.multiple_of(i * 32, 32), 32)
        for half, out in enumerate((out0, out1)):
            grad_hidden = chip[half, lines, :] + chip_far[half, lines, :].astype(F32)
            gate_val, up_val = gate[half, lines, :].astype(F32), up[half, lines, :].astype(F32)
            sigma = jax.nn.sigmoid(gate_val)
            out[0, lines, :] = (grad_hidden * up_val * sigma * (1.0 + gate_val * (1.0 - sigma))).astype(BF16)
            out[1, lines, :] = (grad_hidden * gate_val * sigma).astype(BF16)
        return carry

    lax.fori_loop(0, 8, rows, 0)


def act_grad(chip, chip_far, gate, up):
    shape = jax.ShapeDtypeStruct((2, 256, 512), BF16)
    return pl.pallas_call(
        act_kernel,
        out_shape=(shape, shape),
        in_specs=[VMEM] * 4,
        out_specs=(VMEM,) * 2,
        compiler_params=grant(8),
    )(chip, chip_far, gate, up)


def near_input_kernel(near0, near1, w_gate, w_up, out):
    for half, ref in enumerate((near0, near1)):
        total = dot(ref[0], w_gate[...], 1, 1) + dot(ref[1], w_up[...], 1, 1)
        out[256 * half:256 * half + 256, :] = total.astype(BF16)


def near_input_grad(near, w_gate, w_up):
    weight = pl.BlockSpec((512, 512), lambda i: (i, 0))
    return pl.pallas_call(
        near_input_kernel,
        grid=(3,),
        out_shape=jax.ShapeDtypeStruct((512, 1536), BF16),
        in_specs=[VMEM] * 2 + [weight] * 2,
        out_specs=pl.BlockSpec((512, 512), lambda i: (0, i)),
        compiler_params=grant(12),
    )(*near, w_gate, w_up)


def input_grad_kernel(place, near, other0, other1, w_gate, w_up, out):
    for half, ref in enumerate((other0, other1)):
        start = pl.multiple_of(512 * half + 256 * place[3], 256)
        out[pl.ds(start, 256), :] = near[256 * half:256 * half + 256, :]
        total = dot(ref[0], w_gate[...], 1, 1) + dot(ref[1], w_up[...], 1, 1)
        start = pl.multiple_of(512 * half + 256 * (1 - place[3]), 256)
        out[pl.ds(start, 256), :] = total.astype(BF16)


def input_grad(place, near, other, w_gate, w_up):
    weight = pl.BlockSpec((512, 512), lambda i: (i, 0))
    return pl.pallas_call(
        input_grad_kernel,
        grid=(3,),
        out_shape=jax.ShapeDtypeStruct((1024, 1536), BF16),
        in_specs=[SMEM, pl.BlockSpec((512, 512), lambda i: (0, i))] + [VMEM] * 2 + [weight] * 2,
        out_specs=pl.BlockSpec((1024, 512), lambda i: (0, i)),
        compiler_params=grant(14),
    )(place, near, *other, w_gate, w_up)


def fill_natural(place, own, other, rows, col):
    for half in range(2):
        base = half * 512
        start = pl.multiple_of(base + place[3] * 256, 256)
        rows[pl.ds(start, 256), col:col + 512] = own[half]
        start = pl.multiple_of(base + (1 - place[3]) * 256, 256)
        rows[pl.ds(start, 256), col:col + 512] = other[half]


def down_kernel(place, hidden, hidden_other, go, first, rest, rows):
    @pl.when(pl.program_id(0) == 0)
    def _():
        fill_natural(place, hidden, hidden_other, rows, 0)

    total = dot(rows[...], go[...], 0, 0).astype(BF16)
    first[...] = total[:FIRST]
    rest[...] = total[FIRST:]


def down_grad(place, hidden, hidden_other, go):
    return pl.pallas_call(
        down_kernel,
        grid=(3,),
        out_shape=(
            jax.ShapeDtypeStruct((FIRST, 1536), BF16),
            jax.ShapeDtypeStruct((512 - FIRST, 1536), BF16),
        ),
        in_specs=[SMEM, VMEM, VMEM, pl.BlockSpec((1024, 512), lambda i: (0, i))],
        out_specs=(
            pl.BlockSpec((FIRST, 512), lambda i: (0, i)),
            pl.BlockSpec((512 - FIRST, 512), lambda i: (0, i)),
        ),
        scratch_shapes=[pltpu.VMEM((1024, 512), BF16)],
        compiler_params=grant(12),
    )(place, hidden, hidden_other, in_hbm(go))


def weight_kernel(slots, based, place, *refs):
    count = len(slots)
    pieces, grads, base = refs[:count], refs[count:count + 4], refs[count + 4:-3]
    d_gate, d_up, rows = refs[-3:]

    @pl.when(pl.program_id(0) == 0)
    def _():
        for half in range(4):
            core = place[3] if half < 2 else 1 - place[3]
            for pair in range(2):
                z = 4 * (half % 2) + 2 * core + pair
                for index, k in enumerate(slots):
                    start = pair * 128 + (place[1] + k) % NY * 32
                    lines = pl.ds(pl.multiple_of(start, 32), 32)
                    rows[index, z, :, :512] = grads[half][0, lines, :]
                    rows[index, z, :, 512:] = grads[half][1, lines, :]

    total = jnp.zeros((256, 1024), F32)
    for index, piece in enumerate(pieces):
        total = total + dot(piece[...], rows[index].reshape(256, 1024), 0, 0)
    gate, up = total[:, :512], total[:, 512:]
    if based:
        gate = gate + base[0][...].astype(F32)
        up = up + base[1][...].astype(F32)
    d_gate[...] = gate.astype(BF16)
    d_up[...] = up.astype(BF16)


def weight_grads(place, slots, pieces, grads, base=(), last=False):
    piece = pl.BlockSpec((256, 256), lambda i: (0, i))
    tile = pl.BlockSpec((256, 512), lambda i: (i, 0))
    shape = jax.ShapeDtypeStruct((1536, 512), BF16) if last else pltpu.HBM((1536, 512), BF16)
    return pl.pallas_call(
        functools.partial(weight_kernel, slots, bool(base)),
        grid=(6,),
        out_shape=(shape, shape),
        in_specs=[SMEM] + [piece] * len(slots) + [VMEM] * 4 + [tile] * len(base),
        out_specs=(tile, tile),
        scratch_shapes=[pltpu.VMEM((len(slots), NZ, 32, 1024), BF16)],
        compiler_params=grant(16),
    )(place, *(x if last else in_hbm(x) for x in pieces), *grads, *(in_hbm(x) for x in base))


def add_kernel(first, first_far, rest, rest_far, out):
    @pl.when(pl.program_id(0) == 0)
    def _():
        out[...] = (first[...].astype(F32) + first_far[...].astype(F32)).astype(BF16)

    @pl.when(pl.program_id(0) > 0)
    def _():
        out[...] = (rest[...].astype(F32) + rest_far[...].astype(F32)).astype(BF16)


def add(first, first_far, rest, rest_far):
    top = pl.BlockSpec((FIRST, 1536), lambda i: (0, 0))
    low = pl.BlockSpec((FIRST, 1536), lambda i: (jnp.maximum(i - 1, 0), 0))
    return pl.pallas_call(
        add_kernel,
        grid=(512 // FIRST,),
        out_shape=jax.ShapeDtypeStruct((512, 1536), BF16),
        in_specs=[top, top, low, low],
        out_specs=pl.BlockSpec((FIRST, 1536), lambda i: (i, 0)),
        compiler_params=grant(8),
    )(first, first_far, rest, rest_far)


def ring(x, up, down, axis, n):
    ahead, behind = [up], [down]
    for step in range(2, n // 2 + 1):
        up = from_ahead(up, axis, n, 1)
        ahead.append(up)
        if step < n // 2:
            down = from_ahead(down, axis, n, n - 1)
            behind.append(down)
    return [x] + ahead + behind[::-1]


def ordered(mine, other, index):
    low = jnp.where(index == 0, mine, other)
    high = jnp.where(index == 0, other, mine)
    return jnp.stack([low, high], axis=0)


def body(layer_input, grad_output, gate_saved, up_saved, w_gate, w_up, w_down):
    place = jnp.stack([lax.axis_index(name) for name in ("z", "y", "xh", "core")]).astype(jnp.int32)
    xh = place[2]

    go_parts = [grad_output] + [from_ahead(grad_output, "y", NY, k) for k in (1, 2, 3)]
    z_up, z_down = from_ahead(layer_input, "z", NZ, 1), from_ahead(layer_input, "z", NZ, NZ - 1)
    go_parts, z_up, z_down = lax.optimization_barrier((go_parts, z_up, z_down))
    go = lax.all_gather(arrange(place, 1, go_parts), "z", axis=0, tiled=True)
    own_z = arrange(place, 0, ring(layer_input, z_up, z_down, "z", NZ))
    partner_z = swap(own_z, "dp")
    own1, own3 = from_ahead(own_z, "y", NY, 1), from_ahead(own_z, "y", NY, 3)

    gate = ordered(gate_saved, swap(gate_saved, "xh"), xh)
    up = ordered(up_saved, swap(up_saved, "xh"), xh)
    gate_val, up_val = gate.astype(F32), up.astype(F32)
    hidden = (gate_val * jax.nn.sigmoid(gate_val) * up_val).astype(BF16)
    hidden_other = swap(hidden, "core")
    go, gate, up, hidden, hidden_other, own_z, partner_z, own1, own3 = lax.optimization_barrier(
        (go, gate, up, hidden, hidden_other, own_z, partner_z, own1, own3)
    )

    own2 = from_ahead(own_z, "y", NY, 2)
    from_other = swap(hidden_grad(place, go, w_down, True), "core")
    chip = hidden_grad(place, go, w_down, False) + from_other.astype(F32)
    chip_far = swap(chip.astype(BF16), "xh")
    down_first, down_rest = down_grad(place, hidden, hidden_other, go)

    chip, chip_far, down_first, down_rest = lax.optimization_barrier((chip, chip_far, down_first, down_rest))
    first_far = swap(down_first, "dp")

    near = act_grad(chip, chip_far, gate, up)
    other = [swap(half, "core") for half in near]
    partial_in = input_grad(place, near_input_grad(near, w_gate, w_up), other, w_gate, w_up)
    partial_in, own2, first_far = lax.optimization_barrier((partial_in, own2, first_far))
    in_z = lax.psum_scatter(partial_in, "z", scatter_dimension=0, tiled=True).reshape(NY, 32, 1536)

    far = [swap(near[0], "dp"), lax.ppermute(near[1], ("dp", "xh"), [(0, 3), (3, 0), (1, 2), (2, 1)])]
    partner1, partner2, partner3 = (from_ahead(partner_z, "y", NY, k) for k in (1, 2, 3))
    own_gate, own_up = weight_grads(place, (0, 1, 2, 3), (own_z, own1, own2, own3), (*near, *other))
    far, down_rest, own_gate, own_up, partner1, partner3 = lax.optimization_barrier(
        (far, down_rest, own_gate, own_up, partner1, partner3)
    )
    rest_far = swap(down_rest, "dp")
    far_other = [swap(half, "core") for half in far]

    y = place[1]
    slabs = [lax.dynamic_index_in_dim(in_z, (y + k) % NY, 0, keepdims=False) for k in range(NY)]
    grads = (*far, *far_other)
    most = weight_grads(place, (0, 1, 3), (partner_z, partner1, partner3), grads, (own_gate, own_up))
    slabs, partner2, most = lax.optimization_barrier((slabs, partner2, most))
    total = slabs[0].astype(F32)
    for k in range(1, NY):
        total = total + from_ahead(slabs[k], "y", NY, NY - k).astype(F32)
    grad_input = total.astype(BF16)
    grad_gate, grad_up = weight_grads(place, (2,), (partner2,), grads, most, True)
    grad_input, grad_gate, grad_up, rest_far = lax.optimization_barrier((grad_input, grad_gate, grad_up, rest_far))
    return grad_input, grad_gate, grad_up, add(down_first, first_far, down_rest, rest_far)


def solution(mesh):
    fine = Mesh(mesh.devices.reshape(2, NZ, NY, 2, 2), ("dp", "z", "y", "xh", "core"))
    tokens, col, row = ("dp", "z", "y"), ("xh", "core"), ("z", "y")
    in_specs = (
        P(tokens, col),
        P(tokens, col),
        P(("dp",) + col, row),
        P(("dp",) + col, row),
        P(col, row),
        P(col, row),
        P(row, col),
    )
    out_specs = (P(tokens, col), P(col, row), P(col, row), P(row, col))
    return jax.shard_map(body, mesh=fine, in_specs=in_specs, out_specs=out_specs, check_vma=False)
```

```python
import functools

import jax
import jax.numpy as jnp
from jax import lax
from jax.experimental import pallas as pl
from jax.experimental.pallas import tpu as pltpu
from jax.sharding import Mesh, PartitionSpec as P

F32, BF16 = jnp.float32, jnp.bfloat16
NZ, NY = 8, 4
FIRST = 64
VMEM = pl.BlockSpec(memory_space=pltpu.VMEM)
SMEM = pl.BlockSpec(memory_space=pltpu.SMEM)
HBM = pl.BlockSpec(memory_space=pltpu.HBM)


def dot(left, right, left_dim, right_dim):
    dims = (((left_dim,), (right_dim,)), ((), ()))
    return lax.dot_general(left, right, dims, preferred_element_type=F32)


def from_ahead(x, axis, n, k):
    return lax.ppermute(x, axis, [((d + k) % n, d) for d in range(n)])


def swap(x, axis):
    return lax.ppermute(x, axis, [(0, 1), (1, 0)])


def grant(mib):
    return pltpu.CompilerParams(vmem_limit_bytes=mib << 20)


def in_hbm(x):
    return pltpu.with_memory_space_constraint(x, pltpu.HBM)


def in_vmem(x):
    return pltpu.with_memory_space_constraint(x, pltpu.VMEM)


def arrange_kernel(n, slot, place, *refs):
    for k in range(n):
        refs[n][(place[slot] + k) % n] = refs[k][...]


def arrange(place, slot, parts):
    n, (rows, cols) = len(parts), parts[0].shape
    out = pl.pallas_call(
        functools.partial(arrange_kernel, n, slot),
        out_shape=jax.ShapeDtypeStruct((n, rows, cols), BF16),
        in_specs=[SMEM] + [VMEM] * n,
        out_specs=VMEM,
        compiler_params=grant(6),
    )(place, in_hbm(parts[0]), *parts[1:])
    return out.reshape(n * rows, cols)


def hidden_grad_kernel(place, go, w_down, mine, send, rows, weight, sems):
    copies = [pltpu.make_async_copy(w_down, weight, sems.at[2])]
    for half in range(2):
        copies.append(pltpu.make_async_copy(go.at[pl.ds(512 * half, 512)], rows.at[half], sems.at[half]))
    for copy in copies:
        copy.start()
    copies[0].wait()
    for half in range(2):
        copies[1 + half].wait()
        part = dot(rows[half], weight[...], 1, 1)
        for which in range(2):
            block = part[256 * which:256 * which + 256]

            @pl.when(place[3] == which)
            def _():
                mine[half] = block

            @pl.when(place[3] != which)
            def _():
                send[half] = block.astype(BF16)


def hidden_grad(place, go, w_down):
    return pl.pallas_call(
        hidden_grad_kernel,
        out_shape=(
            jax.ShapeDtypeStruct((2, 256, 512), F32),
            jax.ShapeDtypeStruct((2, 256, 512), BF16),
        ),
        in_specs=[SMEM, HBM, HBM],
        out_specs=(VMEM,) * 2,
        scratch_shapes=[
            pltpu.VMEM((2, 512, 1536), BF16),
            pltpu.VMEM((512, 1536), BF16),
            pltpu.SemaphoreType.DMA((3,)),
        ],
        compiler_params=grant(16),
    )(place, in_hbm(go), in_hbm(w_down))


def act_kernel(chip, chip_far, gate, up, out0, out1):
    def rows(i, carry):
        lines = pl.ds(pl.multiple_of(i * 32, 32), 32)
        for half, out in enumerate((out0, out1)):
            grad_hidden = chip[half, lines, :] + chip_far[half, lines, :].astype(F32)
            gate_val, up_val = gate[half, lines, :].astype(F32), up[half, lines, :].astype(F32)
            sigma = jax.nn.sigmoid(gate_val)
            out[0, lines, :] = (grad_hidden * up_val * sigma * (1.0 + gate_val * (1.0 - sigma))).astype(BF16)
            out[1, lines, :] = (grad_hidden * gate_val * sigma).astype(BF16)
        return carry

    lax.fori_loop(0, 8, rows, 0)


def act_grad(chip, chip_far, gate, up):
    shape = jax.ShapeDtypeStruct((2, 256, 512), BF16)
    return pl.pallas_call(
        act_kernel,
        out_shape=(shape, shape),
        in_specs=[VMEM] * 4,
        out_specs=(VMEM,) * 2,
        compiler_params=grant(8),
    )(chip, chip_far, gate, up)


def input_grad_kernel(place, near0, near1, other0, other1, w_gate, w_up, out):
    for refs, core in (((near0, near1), place[3]), ((other0, other1), 1 - place[3])):
        for half, ref in enumerate(refs):
            total = dot(ref[0], w_gate[...], 1, 1) + dot(ref[1], w_up[...], 1, 1)
            start = pl.multiple_of(512 * half + 256 * core, 256)
            out[pl.ds(start, 256), :] = total.astype(BF16)


def input_grad(place, near, other, w_gate, w_up):
    weight = pl.BlockSpec((512, 512), lambda i: (i, 0))
    return pl.pallas_call(
        input_grad_kernel,
        grid=(3,),
        out_shape=jax.ShapeDtypeStruct((1024, 1536), BF16),
        in_specs=[SMEM] + [VMEM] * 4 + [weight] * 2,
        out_specs=pl.BlockSpec((1024, 512), lambda i: (0, i)),
        compiler_params=grant(16),
    )(place, *near, *other, w_gate, w_up)


def fill_natural(place, own, other, rows, col):
    for half in range(2):
        base = half * 512
        start = pl.multiple_of(base + place[3] * 256, 256)
        rows[pl.ds(start, 256), col:col + 512] = own[half]
        start = pl.multiple_of(base + (1 - place[3]) * 256, 256)
        rows[pl.ds(start, 256), col:col + 512] = other[half]


def down_kernel(place, hidden, hidden_other, go, first, rest, rows):
    @pl.when(pl.program_id(0) == 0)
    def _():
        fill_natural(place, hidden, hidden_other, rows, 0)

    total = dot(rows[...], go[...], 0, 0).astype(BF16)
    first[...] = total[:FIRST]
    rest[...] = total[FIRST:]


def down_grad(place, hidden, hidden_other, go):
    return pl.pallas_call(
        down_kernel,
        grid=(3,),
        out_shape=(
            jax.ShapeDtypeStruct((FIRST, 1536), BF16),
            jax.ShapeDtypeStruct((512 - FIRST, 1536), BF16),
        ),
        in_specs=[SMEM, VMEM, VMEM, pl.BlockSpec((1024, 512), lambda i: (0, i))],
        out_specs=(
            pl.BlockSpec((FIRST, 512), lambda i: (0, i)),
            pl.BlockSpec((512 - FIRST, 512), lambda i: (0, i)),
        ),
        scratch_shapes=[pltpu.VMEM((1024, 512), BF16)],
        compiler_params=grant(12),
    )(place, hidden, hidden_other, in_hbm(go))


def weight_kernel(slots, based, place, *refs):
    count = len(slots)
    pieces, grads, base = refs[:count], refs[count:count + 4], refs[count + 4:-3]
    d_gate, d_up, rows = refs[-3:]

    @pl.when(pl.program_id(0) == 0)
    def _():
        for half in range(4):
            core = place[3] if half < 2 else 1 - place[3]
            for pair in range(2):
                z = 4 * (half % 2) + 2 * core + pair
                for index, k in enumerate(slots):
                    start = pair * 128 + (place[1] + k) % NY * 32
                    lines = pl.ds(pl.multiple_of(start, 32), 32)
                    rows[index, z, :, :512] = grads[half][0, lines, :]
                    rows[index, z, :, 512:] = grads[half][1, lines, :]

    total = jnp.zeros((256, 1024), F32)
    for index, piece in enumerate(pieces):
        total = total + dot(piece[...], rows[index].reshape(256, 1024), 0, 0)
    gate, up = total[:, :512], total[:, 512:]
    if based:
        gate = gate + base[0][...].astype(F32)
        up = up + base[1][...].astype(F32)
    d_gate[...] = gate.astype(BF16)
    d_up[...] = up.astype(BF16)


def weight_grads(place, slots, pieces, grads, base=(), last=False, held=False):
    piece = pl.BlockSpec((256, 256), lambda i: (0, i))
    tile = pl.BlockSpec((256, 512), lambda i: (i, 0))
    space = pltpu.VMEM if held else pltpu.HBM
    shape = jax.ShapeDtypeStruct((1536, 512), BF16) if last else space((1536, 512), BF16)
    hold = in_vmem if last else in_hbm
    return pl.pallas_call(
        functools.partial(weight_kernel, slots, bool(base)),
        grid=(6,),
        out_shape=(shape, shape),
        in_specs=[SMEM] + [piece] * len(slots) + [VMEM] * 4 + [tile] * len(base),
        out_specs=(tile, tile),
        scratch_shapes=[pltpu.VMEM((len(slots), NZ, 32, 1024), BF16)],
        compiler_params=grant(16),
    )(place, *(x if last else in_hbm(x) for x in pieces), *grads, *(hold(x) for x in base))


def add_kernel(first, first_far, rest, rest_far, out):
    out[:FIRST] = (first[...].astype(F32) + first_far[...].astype(F32)).astype(BF16)
    out[FIRST:] = (rest[...].astype(F32) + rest_far[...].astype(F32)).astype(BF16)


def add(*parts):
    top = pl.BlockSpec((FIRST, 512), lambda i: (0, i))
    low = pl.BlockSpec((512 - FIRST, 512), lambda i: (0, i))
    return pl.pallas_call(
        add_kernel,
        grid=(3,),
        out_shape=jax.ShapeDtypeStruct((512, 1536), BF16),
        in_specs=[top, top, low, low],
        out_specs=pl.BlockSpec((512, 512), lambda i: (0, i)),
        compiler_params=grant(8),
    )(*(in_vmem(x) for x in parts))


def ring(x, up, down, axis, n):
    ahead, behind = [up], [down]
    for step in range(2, n // 2 + 1):
        up = from_ahead(up, axis, n, 1)
        ahead.append(up)
        if step < n // 2:
            down = from_ahead(down, axis, n, n - 1)
            behind.append(down)
    return [x] + ahead + behind[::-1]


def ordered(mine, other, index):
    low = jnp.where(index == 0, mine, other)
    high = jnp.where(index == 0, other, mine)
    return jnp.stack([low, high], axis=0)


def body(layer_input, grad_output, gate_saved, up_saved, w_gate, w_up, w_down):
    place = jnp.stack([lax.axis_index(name) for name in ("z", "y", "xh", "core")]).astype(jnp.int32)
    xh = place[2]

    go_parts = [grad_output] + [from_ahead(grad_output, "y", NY, k) for k in (1, 2, 3)]
    z_up, z_down = from_ahead(layer_input, "z", NZ, 1), from_ahead(layer_input, "z", NZ, NZ - 1)
    go_parts, z_up, z_down = lax.optimization_barrier((go_parts, z_up, z_down))
    go = lax.all_gather(arrange(place, 1, go_parts), "z", axis=0, tiled=True)
    own_z = arrange(place, 0, ring(layer_input, z_up, z_down, "z", NZ))
    partner_z = swap(own_z, "dp")
    own1, own3 = from_ahead(own_z, "y", NY, 1), from_ahead(own_z, "y", NY, 3)

    gate = ordered(gate_saved, swap(gate_saved, "xh"), xh)
    up = ordered(up_saved, swap(up_saved, "xh"), xh)
    gate_val, up_val = gate.astype(F32), up.astype(F32)
    hidden = (gate_val * jax.nn.sigmoid(gate_val) * up_val).astype(BF16)
    hidden_other = swap(hidden, "core")
    go, gate, up, hidden, hidden_other, own_z, partner_z, own1, own3 = lax.optimization_barrier(
        (go, gate, up, hidden, hidden_other, own_z, partner_z, own1, own3)
    )

    own2 = from_ahead(own_z, "y", NY, 2)
    mine, send = hidden_grad(place, go, w_down)
    chip = mine + swap(send, "core").astype(F32)
    chip_far = swap(chip.astype(BF16), "xh")
    down_first, down_rest = down_grad(place, hidden, hidden_other, go)

    chip, chip_far, down_first, down_rest = lax.optimization_barrier((chip, chip_far, down_first, down_rest))
    first_far = swap(down_first, "dp")

    near = act_grad(chip, chip_far, gate, up)
    other = [swap(half, "core") for half in near]
    partial_in = input_grad(place, near, other, w_gate, w_up)
    partial_in, own2, first_far = lax.optimization_barrier((partial_in, own2, first_far))
    in_z = lax.psum_scatter(partial_in, "z", scatter_dimension=0, tiled=True).reshape(NY, 32, 1536)

    far = [swap(near[0], "dp"), lax.ppermute(near[1], ("dp", "xh"), [(0, 3), (3, 0), (1, 2), (2, 1)])]
    partner1, partner2, partner3 = (from_ahead(partner_z, "y", NY, k) for k in (1, 2, 3))
    own_gate, own_up = weight_grads(place, (0, 1, 2, 3), (own_z, own1, own2, own3), (*near, *other))
    rest_far = swap(down_rest, "dp")
    far, own_gate, own_up, partner1, partner3 = lax.optimization_barrier((far, own_gate, own_up, partner1, partner3))
    far_other = [swap(half, "core") for half in far]

    y = place[1]
    slabs = [lax.dynamic_index_in_dim(in_z, (y + k) % NY, 0, keepdims=False) for k in range(NY)]
    grads = (*far, *far_other)
    most = weight_grads(place, (0, 1, 3), (partner_z, partner1, partner3), grads, (own_gate, own_up), held=True)
    slabs, partner2, most, rest_far = lax.optimization_barrier((slabs, partner2, most, rest_far))
    total = slabs[0].astype(F32)
    for k in range(1, NY):
        total = total + from_ahead(slabs[k], "y", NY, NY - k).astype(F32)
    grad_input = total.astype(BF16)
    grad_gate, grad_up = weight_grads(place, (2,), (partner2,), grads, most, last=True)
    return grad_input, grad_gate, grad_up, add(down_first, first_far, down_rest, rest_far)


def solution(mesh):
    fine = Mesh(mesh.devices.reshape(2, NZ, NY, 2, 2), ("dp", "z", "y", "xh", "core"))
    tokens, col, row = ("dp", "z", "y"), ("xh", "core"), ("z", "y")
    in_specs = (
        P(tokens, col),
        P(tokens, col),
        P(("dp",) + col, row),
        P(("dp",) + col, row),
        P(col, row),
        P(col, row),
        P(row, col),
    )
    out_specs = (P(tokens, col), P(col, row), P(col, row), P(row, col))
    return jax.shard_map(body, mesh=fine, in_specs=in_specs, out_specs=out_specs, check_vma=False)
```

```python
import functools

import jax
import jax.numpy as jnp
from jax import lax
from jax.experimental import pallas as pl
from jax.experimental.pallas import tpu as pltpu
from jax.sharding import Mesh, PartitionSpec as P

F32, BF16 = jnp.float32, jnp.bfloat16
NZ, NY = 8, 4
FIRST = 64
VMEM = pl.BlockSpec(memory_space=pltpu.VMEM)
SMEM = pl.BlockSpec(memory_space=pltpu.SMEM)
HBM = pl.BlockSpec(memory_space=pltpu.HBM)


def dot(left, right, left_dim, right_dim):
    dims = (((left_dim,), (right_dim,)), ((), ()))
    return lax.dot_general(left, right, dims, preferred_element_type=F32)


def from_ahead(x, axis, n, k):
    return lax.ppermute(x, axis, [((d + k) % n, d) for d in range(n)])


def swap(x, axis):
    return lax.ppermute(x, axis, [(0, 1), (1, 0)])


def grant(mib):
    return pltpu.CompilerParams(vmem_limit_bytes=mib << 20)


def in_hbm(x):
    return pltpu.with_memory_space_constraint(x, pltpu.HBM)


def arrange_kernel(n, slot, place, *refs):
    for k in range(n):
        refs[n][(place[slot] + k) % n] = refs[k][...]


def arrange(place, slot, parts):
    n, (rows, cols) = len(parts), parts[0].shape
    out = pl.pallas_call(
        functools.partial(arrange_kernel, n, slot),
        out_shape=jax.ShapeDtypeStruct((n, rows, cols), BF16),
        in_specs=[SMEM] + [VMEM] * n,
        out_specs=VMEM,
        compiler_params=grant(6),
    )(place, in_hbm(parts[0]), *parts[1:])
    return out.reshape(n * rows, cols)


def hidden_grad_kernel(place, go, w_down, mine, send, rows, weight, sems):
    copies = [pltpu.make_async_copy(w_down, weight, sems.at[2])]
    for half in range(2):
        copies.append(pltpu.make_async_copy(go.at[pl.ds(512 * half, 512)], rows.at[half], sems.at[half]))
    for copy in copies:
        copy.start()
    copies[0].wait()
    for half in range(2):
        copies[1 + half].wait()
        part = dot(rows[half], weight[...], 1, 1)
        for which in range(2):
            block = part[256 * which:256 * which + 256]

            @pl.when(place[3] == which)
            def _():
                mine[half] = block

            @pl.when(place[3] != which)
            def _():
                send[half] = block.astype(BF16)


def hidden_grad(place, go, w_down):
    return pl.pallas_call(
        hidden_grad_kernel,
        out_shape=(
            jax.ShapeDtypeStruct((2, 256, 512), F32),
            jax.ShapeDtypeStruct((2, 256, 512), BF16),
        ),
        in_specs=[SMEM, HBM, HBM],
        out_specs=(VMEM,) * 2,
        scratch_shapes=[
            pltpu.VMEM((2, 512, 1536), BF16),
            pltpu.VMEM((512, 1536), BF16),
            pltpu.SemaphoreType.DMA((3,)),
        ],
        compiler_params=grant(16),
    )(place, in_hbm(go), in_hbm(w_down))


def act_kernel(chip, chip_far, gate, up, out0, out1):
    def rows(i, carry):
        lines = pl.ds(pl.multiple_of(i * 32, 32), 32)
        for half, out in enumerate((out0, out1)):
            grad_hidden = chip[half, lines, :] + chip_far[half, lines, :].astype(F32)
            gate_val, up_val = gate[half, lines, :].astype(F32), up[half, lines, :].astype(F32)
            sigma = jax.nn.sigmoid(gate_val)
            out[0, lines, :] = (grad_hidden * up_val * sigma * (1.0 + gate_val * (1.0 - sigma))).astype(BF16)
            out[1, lines, :] = (grad_hidden * gate_val * sigma).astype(BF16)
        return carry

    lax.fori_loop(0, 8, rows, 0)


def act_grad(chip, chip_far, gate, up):
    shape = jax.ShapeDtypeStruct((2, 256, 512), BF16)
    return pl.pallas_call(
        act_kernel,
        out_shape=(shape, shape),
        in_specs=[VMEM] * 4,
        out_specs=(VMEM,) * 2,
        compiler_params=grant(8),
    )(chip, chip_far, gate, up)


def input_grad_kernel(place, near0, near1, other0, other1, w_gate, w_up, out):
    for refs, core in (((near0, near1), place[3]), ((other0, other1), 1 - place[3])):
        for half, ref in enumerate(refs):
            total = dot(ref[0], w_gate[...], 1, 1) + dot(ref[1], w_up[...], 1, 1)
            start = pl.multiple_of(512 * half + 256 * core, 256)
            out[pl.ds(start, 256), :] = total.astype(BF16)


def input_grad(place, near, other, w_gate, w_up):
    weight = pl.BlockSpec((512, 512), lambda i: (i, 0))
    return pl.pallas_call(
        input_grad_kernel,
        grid=(3,),
        out_shape=jax.ShapeDtypeStruct((1024, 1536), BF16),
        in_specs=[SMEM] + [VMEM] * 4 + [weight] * 2,
        out_specs=pl.BlockSpec((1024, 512), lambda i: (0, i)),
        compiler_params=grant(16),
    )(place, *near, *other, w_gate, w_up)


def fill_natural(place, own, other, rows, col):
    for half in range(2):
        base = half * 512
        start = pl.multiple_of(base + place[3] * 256, 256)
        rows[pl.ds(start, 256), col:col + 512] = own[half]
        start = pl.multiple_of(base + (1 - place[3]) * 256, 256)
        rows[pl.ds(start, 256), col:col + 512] = other[half]


def down_kernel(place, hidden, hidden_other, go, first, rest, rows):
    @pl.when(pl.program_id(0) == 0)
    def _():
        fill_natural(place, hidden, hidden_other, rows, 0)

    total = dot(rows[...], go[...], 0, 0).astype(BF16)
    first[...] = total[:FIRST]
    rest[...] = total[FIRST:]


def down_grad(place, hidden, hidden_other, go):
    return pl.pallas_call(
        down_kernel,
        grid=(3,),
        out_shape=(
            jax.ShapeDtypeStruct((FIRST, 1536), BF16),
            jax.ShapeDtypeStruct((512 - FIRST, 1536), BF16),
        ),
        in_specs=[SMEM, VMEM, VMEM, pl.BlockSpec((1024, 512), lambda i: (0, i))],
        out_specs=(
            pl.BlockSpec((FIRST, 512), lambda i: (0, i)),
            pl.BlockSpec((512 - FIRST, 512), lambda i: (0, i)),
        ),
        scratch_shapes=[pltpu.VMEM((1024, 512), BF16)],
        compiler_params=grant(12),
    )(place, hidden, hidden_other, in_hbm(go))


def weight_kernel(slots, based, place, *refs):
    count = len(slots)
    pieces, grads, base = refs[:count], refs[count:count + 4], refs[count + 4:-3]
    d_gate, d_up, rows = refs[-3:]

    @pl.when(pl.program_id(0) == 0)
    def _():
        for half in range(4):
            core = place[3] if half < 2 else 1 - place[3]
            for pair in range(2):
                z = 4 * (half % 2) + 2 * core + pair
                for index, k in enumerate(slots):
                    start = pair * 128 + (place[1] + k) % NY * 32
                    lines = pl.ds(pl.multiple_of(start, 32), 32)
                    rows[index, z, :, :512] = grads[half][0, lines, :]
                    rows[index, z, :, 512:] = grads[half][1, lines, :]

    total = jnp.zeros((d_gate.shape[0], 1024), F32)
    for index, piece in enumerate(pieces):
        total = total + dot(piece[...], rows[index].reshape(256, 1024), 0, 0)
    gate, up = total[:, :512], total[:, 512:]
    if based:
        gate = gate + base[0][...].astype(F32)
        up = up + base[1][...].astype(F32)
    d_gate[...] = gate.astype(BF16)
    d_up[...] = up.astype(BF16)


def weight_grads(place, slots, pieces, grads, base=(), last=False):
    size = 512 if last else 256
    piece = pl.BlockSpec((256, size), lambda i: (0, i))
    tile = pl.BlockSpec((size, 512), lambda i: (i, 0))
    shape = jax.ShapeDtypeStruct((1536, 512), BF16) if last else pltpu.HBM((1536, 512), BF16)
    return pl.pallas_call(
        functools.partial(weight_kernel, slots, bool(base)),
        grid=(1536 // size,),
        out_shape=(shape, shape),
        in_specs=[SMEM] + [piece] * len(slots) + [VMEM] * 4 + [tile] * len(base),
        out_specs=(tile, tile),
        scratch_shapes=[pltpu.VMEM((len(slots), NZ, 32, 1024), BF16)],
        compiler_params=grant(16),
    )(place, *(x if last else in_hbm(x) for x in pieces), *grads, *(in_hbm(x) for x in base))


def add_kernel(first, first_far, rest, rest_far, out):
    out[:FIRST] = (first[...].astype(F32) + first_far[...].astype(F32)).astype(BF16)
    out[FIRST:] = (rest[...].astype(F32) + rest_far[...].astype(F32)).astype(BF16)


def add(*parts):
    top = pl.BlockSpec((FIRST, 512), lambda i: (0, i))
    low = pl.BlockSpec((512 - FIRST, 512), lambda i: (0, i))
    return pl.pallas_call(
        add_kernel,
        grid=(3,),
        out_shape=jax.ShapeDtypeStruct((512, 1536), BF16),
        in_specs=[top, top, low, low],
        out_specs=pl.BlockSpec((512, 512), lambda i: (0, i)),
        compiler_params=grant(8),
    )(*parts)


def ring(x, up, down, axis, n):
    ahead, behind = [up], [down]
    for step in range(2, n // 2 + 1):
        up = from_ahead(up, axis, n, 1)
        ahead.append(up)
        if step < n // 2:
            down = from_ahead(down, axis, n, n - 1)
            behind.append(down)
    return [x] + ahead + behind[::-1]


def ordered(mine, other, index):
    low = jnp.where(index == 0, mine, other)
    high = jnp.where(index == 0, other, mine)
    return jnp.stack([low, high], axis=0)


def body(layer_input, grad_output, gate_saved, up_saved, w_gate, w_up, w_down):
    place = jnp.stack([lax.axis_index(name) for name in ("z", "y", "xh", "core")]).astype(jnp.int32)
    xh = place[2]

    go_parts = [grad_output] + [from_ahead(grad_output, "y", NY, k) for k in (1, 2, 3)]
    z_up, z_down = from_ahead(layer_input, "z", NZ, 1), from_ahead(layer_input, "z", NZ, NZ - 1)
    go_parts, z_up, z_down = lax.optimization_barrier((go_parts, z_up, z_down))
    go = lax.all_gather(arrange(place, 1, go_parts), "z", axis=0, tiled=True)
    own_z = arrange(place, 0, ring(layer_input, z_up, z_down, "z", NZ))
    partner_z = swap(own_z, "dp")
    own1, own3 = from_ahead(own_z, "y", NY, 1), from_ahead(own_z, "y", NY, 3)

    gate = ordered(gate_saved, swap(gate_saved, "xh"), xh)
    up = ordered(up_saved, swap(up_saved, "xh"), xh)
    gate_val, up_val = gate.astype(F32), up.astype(F32)
    hidden = (gate_val * jax.nn.sigmoid(gate_val) * up_val).astype(BF16)
    hidden_other = swap(hidden, "core")
    go, gate, up, hidden, hidden_other, own_z, partner_z, own1, own3 = lax.optimization_barrier(
        (go, gate, up, hidden, hidden_other, own_z, partner_z, own1, own3)
    )

    own2 = from_ahead(own_z, "y", NY, 2)
    mine, send = hidden_grad(place, go, w_down)
    chip = mine + swap(send, "core").astype(F32)
    chip_far = swap(chip.astype(BF16), "xh")
    down_first, down_rest = down_grad(place, hidden, hidden_other, go)

    chip, chip_far, down_first, down_rest = lax.optimization_barrier((chip, chip_far, down_first, down_rest))
    first_far = swap(down_first, "dp")

    near = act_grad(chip, chip_far, gate, up)
    other = [swap(half, "core") for half in near]
    partial_in = input_grad(place, near, other, w_gate, w_up)
    partial_in, own2, first_far = lax.optimization_barrier((partial_in, own2, first_far))
    in_z = lax.psum_scatter(partial_in, "z", scatter_dimension=0, tiled=True).reshape(NY, 32, 1536)

    far = [swap(near[0], "dp"), lax.ppermute(near[1], ("dp", "xh"), [(0, 3), (3, 0), (1, 2), (2, 1)])]
    partner1, partner2, partner3 = (from_ahead(partner_z, "y", NY, k) for k in (1, 2, 3))
    far, down_rest = lax.optimization_barrier((far, down_rest))
    rest_far = swap(down_rest, "dp")
    own_z, partner1, partner3 = lax.optimization_barrier((own_z, partner1, partner3))
    own_gate, own_up = weight_grads(place, (0, 1, 2, 3), (own_z, own1, own2, own3), (*near, *other))
    far_other = [swap(half, "core") for half in far]

    y = place[1]
    slabs = [lax.dynamic_index_in_dim(in_z, (y + k) % NY, 0, keepdims=False) for k in range(NY)]
    grads = (*far, *far_other)
    most = weight_grads(place, (0, 1, 3), (partner_z, partner1, partner3), grads, (own_gate, own_up))
    slabs, partner2, most = lax.optimization_barrier((slabs, partner2, most))
    total = slabs[0].astype(F32)
    for k in range(1, NY):
        total = total + from_ahead(slabs[k], "y", NY, NY - k).astype(F32)
    grad_input = total.astype(BF16)
    grad_gate, grad_up = weight_grads(place, (2,), (partner2,), grads, most, last=True)
    grad_input, grad_gate, grad_up, rest_far = lax.optimization_barrier((grad_input, grad_gate, grad_up, rest_far))
    return grad_input, grad_gate, grad_up, add(down_first, first_far, down_rest, rest_far)


def solution(mesh):
    fine = Mesh(mesh.devices.reshape(2, NZ, NY, 2, 2), ("dp", "z", "y", "xh", "core"))
    tokens, col, row = ("dp", "z", "y"), ("xh", "core"), ("z", "y")
    in_specs = (
        P(tokens, col),
        P(tokens, col),
        P(("dp",) + col, row),
        P(("dp",) + col, row),
        P(col, row),
        P(col, row),
        P(row, col),
    )
    out_specs = (P(tokens, col), P(col, row), P(col, row), P(row, col))
    return jax.shard_map(body, mesh=fine, in_specs=in_specs, out_specs=out_specs, check_vma=False)
```

```python
import functools

import jax
import jax.numpy as jnp
from jax import lax
from jax.experimental import pallas as pl
from jax.experimental.pallas import tpu as pltpu
from jax.sharding import Mesh, PartitionSpec as P

F32, BF16 = jnp.float32, jnp.bfloat16
NZ, NY = 8, 4
FIRST = 64
VMEM = pl.BlockSpec(memory_space=pltpu.VMEM)
SMEM = pl.BlockSpec(memory_space=pltpu.SMEM)
HBM = pl.BlockSpec(memory_space=pltpu.HBM)


def dot(left, right, left_dim, right_dim):
    dims = (((left_dim,), (right_dim,)), ((), ()))
    return lax.dot_general(left, right, dims, preferred_element_type=F32)


def from_ahead(x, axis, n, k):
    return lax.ppermute(x, axis, [((d + k) % n, d) for d in range(n)])


def swap(x, axis):
    return lax.ppermute(x, axis, [(0, 1), (1, 0)])


def grant(mib):
    return pltpu.CompilerParams(vmem_limit_bytes=mib << 20)


def in_hbm(x):
    return pltpu.with_memory_space_constraint(x, pltpu.HBM)


def arrange_kernel(n, slot, place, *refs):
    for k in range(n):
        refs[n][(place[slot] + k) % n] = refs[k][...]


def arrange(place, slot, parts):
    n, (rows, cols) = len(parts), parts[0].shape
    out = pl.pallas_call(
        functools.partial(arrange_kernel, n, slot),
        out_shape=jax.ShapeDtypeStruct((n, rows, cols), BF16),
        in_specs=[SMEM] + [VMEM] * n,
        out_specs=VMEM,
        compiler_params=grant(6),
    )(place, in_hbm(parts[0]), *parts[1:])
    return out.reshape(n * rows, cols)


def hidden_grad_kernel(place, go, w_down, mine, send, rows, weight, sems):
    copies = [pltpu.make_async_copy(w_down, weight, sems.at[2])]
    for half in range(2):
        copies.append(pltpu.make_async_copy(go.at[pl.ds(512 * half, 512)], rows.at[half], sems.at[half]))
    for copy in copies:
        copy.start()
    copies[0].wait()
    for half in range(2):
        copies[1 + half].wait()
        part = dot(rows[half], weight[...], 1, 1)
        for which in range(2):
            block = part[256 * which:256 * which + 256]

            @pl.when(place[3] == which)
            def _():
                mine[half] = block

            @pl.when(place[3] != which)
            def _():
                send[half] = block.astype(BF16)


def hidden_grad(place, go, w_down):
    return pl.pallas_call(
        hidden_grad_kernel,
        out_shape=(
            jax.ShapeDtypeStruct((2, 256, 512), F32),
            jax.ShapeDtypeStruct((2, 256, 512), BF16),
        ),
        in_specs=[SMEM, HBM, HBM],
        out_specs=(VMEM,) * 2,
        scratch_shapes=[
            pltpu.VMEM((2, 512, 1536), BF16),
            pltpu.VMEM((512, 1536), BF16),
            pltpu.SemaphoreType.DMA((3,)),
        ],
        compiler_params=grant(16),
    )(place, in_hbm(go), in_hbm(w_down))


def act_kernel(chip, chip_far, gate, up, out0, out1):
    def rows(i, carry):
        lines = pl.ds(pl.multiple_of(i * 32, 32), 32)
        for half, out in enumerate((out0, out1)):
            grad_hidden = chip[half, lines, :] + chip_far[half, lines, :].astype(F32)
            gate_val, up_val = gate[half, lines, :].astype(F32), up[half, lines, :].astype(F32)
            sigma = jax.nn.sigmoid(gate_val)
            out[0, lines, :] = (grad_hidden * up_val * sigma * (1.0 + gate_val * (1.0 - sigma))).astype(BF16)
            out[1, lines, :] = (grad_hidden * gate_val * sigma).astype(BF16)
        return carry

    lax.fori_loop(0, 8, rows, 0)


def act_grad(chip, chip_far, gate, up):
    shape = jax.ShapeDtypeStruct((2, 256, 512), BF16)
    return pl.pallas_call(
        act_kernel,
        out_shape=(shape, shape),
        in_specs=[VMEM] * 4,
        out_specs=(VMEM,) * 2,
        compiler_params=grant(8),
    )(chip, chip_far, gate, up)


def input_grad_kernel(place, near0, near1, other0, other1, w_gate, w_up, out):
    for refs, core in (((near0, near1), place[3]), ((other0, other1), 1 - place[3])):
        for half, ref in enumerate(refs):
            total = dot(ref[0], w_gate[...], 1, 1) + dot(ref[1], w_up[...], 1, 1)
            start = pl.multiple_of(512 * half + 256 * core, 256)
            out[pl.ds(start, 256), :] = total.astype(BF16)


def input_grad(place, near, other, w_gate, w_up):
    weight = pl.BlockSpec((512, 512), lambda i: (i, 0))
    return pl.pallas_call(
        input_grad_kernel,
        grid=(3,),
        out_shape=jax.ShapeDtypeStruct((1024, 1536), BF16),
        in_specs=[SMEM] + [VMEM] * 4 + [weight] * 2,
        out_specs=pl.BlockSpec((1024, 512), lambda i: (0, i)),
        compiler_params=grant(16),
    )(place, *near, *other, w_gate, w_up)


def fill_natural(place, own, other, rows, col):
    for half in range(2):
        base = half * 512
        start = pl.multiple_of(base + place[3] * 256, 256)
        rows[pl.ds(start, 256), col:col + 512] = own[half]
        start = pl.multiple_of(base + (1 - place[3]) * 256, 256)
        rows[pl.ds(start, 256), col:col + 512] = other[half]


def down_kernel(place, hidden, hidden_other, go, first, rest, rows):
    @pl.when(pl.program_id(0) == 0)
    def _():
        fill_natural(place, hidden, hidden_other, rows, 0)

    total = dot(rows[...], go[...], 0, 0).astype(BF16)
    first[...] = total[:FIRST]
    rest[...] = total[FIRST:]


def down_grad(place, hidden, hidden_other, go):
    return pl.pallas_call(
        down_kernel,
        grid=(3,),
        out_shape=(
            jax.ShapeDtypeStruct((FIRST, 1536), BF16),
            jax.ShapeDtypeStruct((512 - FIRST, 1536), BF16),
        ),
        in_specs=[SMEM, VMEM, VMEM, pl.BlockSpec((1024, 512), lambda i: (0, i))],
        out_specs=(
            pl.BlockSpec((FIRST, 512), lambda i: (0, i)),
            pl.BlockSpec((512 - FIRST, 512), lambda i: (0, i)),
        ),
        scratch_shapes=[pltpu.VMEM((1024, 512), BF16)],
        compiler_params=grant(12),
    )(place, hidden, hidden_other, in_hbm(go))


def weight_kernel(slots, based, place, *refs):
    count = len(slots)
    pieces, grads, base = refs[:count], refs[count:count + 4], refs[count + 4:-3]
    d_gate, d_up, rows = refs[-3:]

    @pl.when(pl.program_id(0) == 0)
    def _():
        for half in range(4):
            core = place[3] if half < 2 else 1 - place[3]
            for pair in range(2):
                z = 4 * (half % 2) + 2 * core + pair
                for index, k in enumerate(slots):
                    start = pair * 128 + (place[1] + k) % NY * 32
                    lines = pl.ds(pl.multiple_of(start, 32), 32)
                    rows[index, z, :, :512] = grads[half][0, lines, :]
                    rows[index, z, :, 512:] = grads[half][1, lines, :]

    total = jnp.zeros((d_gate.shape[0], 1024), F32)
    for index, piece in enumerate(pieces):
        total = total + dot(piece[...], rows[index].reshape(256, 1024), 0, 0)
    gate, up = total[:, :512], total[:, 512:]
    if based:
        gate = gate + base[0][...].astype(F32)
        up = up + base[1][...].astype(F32)
    d_gate[...] = gate.astype(BF16)
    d_up[...] = up.astype(BF16)


def weight_grads(place, slots, pieces, grads, base=(), last=False):
    size = 512 if last else 256
    piece = pl.BlockSpec((256, size), lambda i: (0, i))
    tile = pl.BlockSpec((size, 512), lambda i: (i, 0))
    shape = jax.ShapeDtypeStruct((1536, 512), BF16) if last else pltpu.HBM((1536, 512), BF16)
    return pl.pallas_call(
        functools.partial(weight_kernel, slots, bool(base)),
        grid=(1536 // size,),
        out_shape=(shape, shape),
        in_specs=[SMEM] + [piece] * len(slots) + [VMEM] * 4 + [tile] * len(base),
        out_specs=(tile, tile),
        scratch_shapes=[pltpu.VMEM((len(slots), NZ, 32, 1024), BF16)],
        compiler_params=grant(16),
    )(place, *(x if last else in_hbm(x) for x in pieces), *grads, *(in_hbm(x) for x in base))


def add_kernel(first, first_far, rest, rest_far, out):
    out[:FIRST] = (first[...].astype(F32) + first_far[...].astype(F32)).astype(BF16)
    out[FIRST:] = (rest[...].astype(F32) + rest_far[...].astype(F32)).astype(BF16)


def add(*parts):
    top = pl.BlockSpec((FIRST, 512), lambda i: (0, i))
    low = pl.BlockSpec((512 - FIRST, 512), lambda i: (0, i))
    return pl.pallas_call(
        add_kernel,
        grid=(3,),
        out_shape=jax.ShapeDtypeStruct((512, 1536), BF16),
        in_specs=[top, top, low, low],
        out_specs=pl.BlockSpec((512, 512), lambda i: (0, i)),
        compiler_params=grant(8),
    )(*parts)


def ring(x, up, down, axis, n):
    ahead, behind = [up], [down]
    for step in range(2, n // 2 + 1):
        up = from_ahead(up, axis, n, 1)
        ahead.append(up)
        if step < n // 2:
            down = from_ahead(down, axis, n, n - 1)
            behind.append(down)
    return [x] + ahead + behind[::-1]


def ordered(mine, other, index):
    low = jnp.where(index == 0, mine, other)
    high = jnp.where(index == 0, other, mine)
    return jnp.stack([low, high], axis=0)


def body(layer_input, grad_output, gate_saved, up_saved, w_gate, w_up, w_down):
    place = jnp.stack([lax.axis_index(name) for name in ("z", "y", "xh", "core")]).astype(jnp.int32)
    xh = place[2]

    go_parts = [grad_output] + [from_ahead(grad_output, "y", NY, k) for k in (1, 2, 3)]
    z_up, z_down = from_ahead(layer_input, "z", NZ, 1), from_ahead(layer_input, "z", NZ, NZ - 1)
    go_parts, z_up, z_down = lax.optimization_barrier((go_parts, z_up, z_down))
    go = lax.all_gather(arrange(place, 1, go_parts), "z", axis=0, tiled=True)
    own_z = arrange(place, 0, ring(layer_input, z_up, z_down, "z", NZ))
    partner_z = swap(own_z, "dp")
    own1, own3 = from_ahead(own_z, "y", NY, 1), from_ahead(own_z, "y", NY, 3)

    gate = ordered(gate_saved, swap(gate_saved, "xh"), xh)
    up = ordered(up_saved, swap(up_saved, "xh"), xh)
    gate_val, up_val = gate.astype(F32), up.astype(F32)
    hidden = (gate_val * jax.nn.sigmoid(gate_val) * up_val).astype(BF16)
    hidden_other = swap(hidden, "core")
    go, gate, up, hidden, hidden_other, own_z, partner_z, own1, own3 = lax.optimization_barrier(
        (go, gate, up, hidden, hidden_other, own_z, partner_z, own1, own3)
    )

    own2 = from_ahead(own_z, "y", NY, 2)
    mine, send = hidden_grad(place, go, w_down)
    chip = mine + swap(send, "core").astype(F32)
    chip_far = swap(chip.astype(BF16), "xh")
    down_first, down_rest = down_grad(place, hidden, hidden_other, go)

    chip, chip_far, down_first, down_rest = lax.optimization_barrier((chip, chip_far, down_first, down_rest))
    first_far = swap(down_first, "dp")

    near = act_grad(chip, chip_far, gate, up)
    other = [swap(half, "core") for half in near]
    partial_in = input_grad(place, near, other, w_gate, w_up)
    partial_in, own2, first_far = lax.optimization_barrier((partial_in, own2, first_far))
    in_z = lax.psum_scatter(partial_in, "z", scatter_dimension=0, tiled=True).reshape(NY, 32, 1536)

    far = [swap(near[0], "dp"), lax.ppermute(near[1], ("dp", "xh"), [(0, 3), (3, 0), (1, 2), (2, 1)])]
    partner1, partner3 = from_ahead(partner_z, "y", NY, 1), from_ahead(partner_z, "y", NY, 3)
    far, down_rest = lax.optimization_barrier((far, down_rest))
    rest_far = swap(down_rest, "dp")
    own_z, partner_z, partner1, partner3 = lax.optimization_barrier((own_z, partner_z, partner1, partner3))
    partner2 = from_ahead(partner_z, "y", NY, 2)
    own_gate, own_up = weight_grads(place, (0, 1, 2, 3), (own_z, own1, own2, own3), (*near, *other))
    far_other = [swap(half, "core") for half in far]

    y = place[1]
    slabs = [lax.dynamic_index_in_dim(in_z, (y + k) % NY, 0, keepdims=False) for k in range(NY)]
    grads = (*far, *far_other)
    most = weight_grads(place, (0, 1, 3), (partner_z, partner1, partner3), grads, (own_gate, own_up))
    slabs, partner2, most = lax.optimization_barrier((slabs, partner2, most))
    total = slabs[0].astype(F32)
    for k in range(1, NY):
        total = total + from_ahead(slabs[k], "y", NY, NY - k).astype(F32)
    grad_input = total.astype(BF16)
    grad_gate, grad_up = weight_grads(place, (2,), (partner2,), grads, most, last=True)
    grad_input, grad_gate, grad_up, rest_far = lax.optimization_barrier((grad_input, grad_gate, grad_up, rest_far))
    return grad_input, grad_gate, grad_up, add(down_first, first_far, down_rest, rest_far)


def solution(mesh):
    fine = Mesh(mesh.devices.reshape(2, NZ, NY, 2, 2), ("dp", "z", "y", "xh", "core"))
    tokens, col, row = ("dp", "z", "y"), ("xh", "core"), ("z", "y")
    in_specs = (
        P(tokens, col),
        P(tokens, col),
        P(("dp",) + col, row),
        P(("dp",) + col, row),
        P(col, row),
        P(col, row),
        P(row, col),
    )
    out_specs = (P(tokens, col), P(col, row), P(col, row), P(row, col))
    return jax.shard_map(body, mesh=fine, in_specs=in_specs, out_specs=out_specs, check_vma=False)
```

```python
import functools

import jax
import jax.numpy as jnp
from jax import lax
from jax.experimental import pallas as pl
from jax.experimental.pallas import tpu as pltpu
from jax.sharding import Mesh, PartitionSpec as P

F32, BF16 = jnp.float32, jnp.bfloat16
NZ, NY = 8, 4
FIRST = 64
VMEM = pl.BlockSpec(memory_space=pltpu.VMEM)
SMEM = pl.BlockSpec(memory_space=pltpu.SMEM)
HBM = pl.BlockSpec(memory_space=pltpu.HBM)


def dot(left, right, left_dim, right_dim):
    dims = (((left_dim,), (right_dim,)), ((), ()))
    return lax.dot_general(left, right, dims, preferred_element_type=F32)


def from_ahead(x, axis, n, k):
    return lax.ppermute(x, axis, [((d + k) % n, d) for d in range(n)])


def swap(x, axis):
    return lax.ppermute(x, axis, [(0, 1), (1, 0)])


def grant(mib):
    return pltpu.CompilerParams(vmem_limit_bytes=mib << 20)


def in_hbm(x):
    return pltpu.with_memory_space_constraint(x, pltpu.HBM)


def arrange_kernel(n, slot, place, *refs):
    for k in range(n):
        refs[n][(place[slot] + k) % n] = refs[k][...]


def arrange(place, slot, parts):
    n, (rows, cols) = len(parts), parts[0].shape
    out = pl.pallas_call(
        functools.partial(arrange_kernel, n, slot),
        out_shape=jax.ShapeDtypeStruct((n, rows, cols), BF16),
        in_specs=[SMEM] + [VMEM] * n,
        out_specs=VMEM,
        compiler_params=grant(6),
    )(place, in_hbm(parts[0]), *parts[1:])
    return out.reshape(n * rows, cols)


def hidden_grad_kernel(place, go, w_down, mine, send, rows, weight, sems):
    copies = [pltpu.make_async_copy(w_down, weight, sems.at[2])]
    for half in range(2):
        copies.append(pltpu.make_async_copy(go.at[pl.ds(512 * half, 512)], rows.at[half], sems.at[half]))
    for copy in copies:
        copy.start()
    copies[0].wait()
    for half in range(2):
        copies[1 + half].wait()
        part = dot(rows[half], weight[...], 1, 1)
        for which in range(2):
            block = part[256 * which:256 * which + 256]

            @pl.when(place[3] == which)
            def _():
                mine[half] = block

            @pl.when(place[3] != which)
            def _():
                send[half] = block.astype(BF16)


def hidden_grad(place, go, w_down):
    return pl.pallas_call(
        hidden_grad_kernel,
        out_shape=(
            jax.ShapeDtypeStruct((2, 256, 512), F32),
            jax.ShapeDtypeStruct((2, 256, 512), BF16),
        ),
        in_specs=[SMEM, HBM, HBM],
        out_specs=(VMEM,) * 2,
        scratch_shapes=[
            pltpu.VMEM((2, 512, 1536), BF16),
            pltpu.VMEM((512, 1536), BF16),
            pltpu.SemaphoreType.DMA((3,)),
        ],
        compiler_params=grant(16),
    )(place, in_hbm(go), in_hbm(w_down))


def act_kernel(chip, chip_far, gate, up, out0, out1):
    def rows(i, carry):
        lines = pl.ds(pl.multiple_of(i * 32, 32), 32)
        for half, out in enumerate((out0, out1)):
            grad_hidden = chip[half, lines, :] + chip_far[half, lines, :].astype(F32)
            gate_val, up_val = gate[half, lines, :].astype(F32), up[half, lines, :].astype(F32)
            sigma = jax.nn.sigmoid(gate_val)
            out[0, lines, :] = (grad_hidden * up_val * sigma * (1.0 + gate_val * (1.0 - sigma))).astype(BF16)
            out[1, lines, :] = (grad_hidden * gate_val * sigma).astype(BF16)
        return carry

    lax.fori_loop(0, 8, rows, 0)


def act_grad(chip, chip_far, gate, up):
    shape = jax.ShapeDtypeStruct((2, 256, 512), BF16)
    return pl.pallas_call(
        act_kernel,
        out_shape=(shape, shape),
        in_specs=[VMEM] * 4,
        out_specs=(VMEM,) * 2,
        compiler_params=grant(8),
    )(chip, chip_far, gate, up)


def input_grad_kernel(place, near0, near1, other0, other1, w_gate, w_up, out):
    for refs, core in (((near0, near1), place[3]), ((other0, other1), 1 - place[3])):
        for half, ref in enumerate(refs):
            total = dot(ref[0], w_gate[...], 1, 1) + dot(ref[1], w_up[...], 1, 1)
            start = pl.multiple_of(512 * half + 256 * core, 256)
            out[pl.ds(start, 256), :] = total.astype(BF16)


def input_grad(place, near, other, w_gate, w_up):
    weight = pl.BlockSpec((512, 512), lambda i: (i, 0))
    return pl.pallas_call(
        input_grad_kernel,
        grid=(3,),
        out_shape=jax.ShapeDtypeStruct((1024, 1536), BF16),
        in_specs=[SMEM] + [VMEM] * 4 + [weight] * 2,
        out_specs=pl.BlockSpec((1024, 512), lambda i: (0, i)),
        compiler_params=grant(16),
    )(place, *near, *other, w_gate, w_up)


def fill_natural(place, own, other, rows, col):
    for half in range(2):
        base = half * 512
        start = pl.multiple_of(base + place[3] * 256, 256)
        rows[pl.ds(start, 256), col:col + 512] = own[half]
        start = pl.multiple_of(base + (1 - place[3]) * 256, 256)
        rows[pl.ds(start, 256), col:col + 512] = other[half]


def down_kernel(place, hidden, hidden_other, go, first, rest, rows):
    @pl.when(pl.program_id(0) == 0)
    def _():
        fill_natural(place, hidden, hidden_other, rows, 0)

    total = dot(rows[...], go[...], 0, 0).astype(BF16)
    first[...] = total[:FIRST]
    rest[...] = total[FIRST:]


def down_grad(place, hidden, hidden_other, go):
    return pl.pallas_call(
        down_kernel,
        grid=(3,),
        out_shape=(
            jax.ShapeDtypeStruct((FIRST, 1536), BF16),
            jax.ShapeDtypeStruct((512 - FIRST, 1536), BF16),
        ),
        in_specs=[SMEM, VMEM, VMEM, pl.BlockSpec((1024, 512), lambda i: (0, i))],
        out_specs=(
            pl.BlockSpec((FIRST, 512), lambda i: (0, i)),
            pl.BlockSpec((512 - FIRST, 512), lambda i: (0, i)),
        ),
        scratch_shapes=[pltpu.VMEM((1024, 512), BF16)],
        compiler_params=grant(12),
    )(place, hidden, hidden_other, in_hbm(go))


def weight_kernel(slots, based, place, *refs):
    count, turns = len(slots), sorted({k for k, _, _ in slots})
    pieces, grads, base = refs[:count], refs[count:count + 4], refs[count + 4:-3]
    d_gate, d_up, rows = refs[-3:]

    @pl.when(pl.program_id(0) == 0)
    def _():
        for half in range(4):
            core = place[3] if half < 2 else 1 - place[3]
            for pair in range(2):
                z = 4 * (half % 2) + 2 * core + pair
                for index, k in enumerate(turns):
                    start = pair * 128 + (place[1] + k) % NY * 32
                    lines = pl.ds(pl.multiple_of(start, 32), 32)
                    rows[index, z, :, :512] = grads[half][0, lines, :]
                    rows[index, z, :, 512:] = grads[half][1, lines, :]

    total = jnp.zeros((d_gate.shape[0], 1024), F32)
    for (k, low, high), piece in zip(slots, pieces):
        lines = rows[turns.index(k), low:high].reshape(32 * (high - low), 1024)
        total = total + dot(piece[...], lines, 0, 0)
    gate, up = total[:, :512], total[:, 512:]
    if based:
        gate = gate + base[0][...].astype(F32)
        up = up + base[1][...].astype(F32)
    d_gate[...] = gate.astype(BF16)
    d_up[...] = up.astype(BF16)


def weight_grads(place, slots, pieces, grads, base=(), last=False):
    size = 512 if last else 256
    pieces_in = [pl.BlockSpec((32 * (high - low), size), lambda i: (0, i)) for _, low, high in slots]
    tile = pl.BlockSpec((size, 512), lambda i: (i, 0))
    shape = jax.ShapeDtypeStruct((1536, 512), BF16) if last else pltpu.HBM((1536, 512), BF16)
    return pl.pallas_call(
        functools.partial(weight_kernel, slots, bool(base)),
        grid=(1536 // size,),
        out_shape=(shape, shape),
        in_specs=[SMEM] + pieces_in + [VMEM] * 4 + [tile] * len(base),
        out_specs=(tile, tile),
        scratch_shapes=[pltpu.VMEM((len({k for k, _, _ in slots}), NZ, 32, 1024), BF16)],
        compiler_params=grant(16),
    )(place, *(x if last else in_hbm(x) for x in pieces), *grads, *(in_hbm(x) for x in base))


def add_kernel(first, first_far, rest, rest_far, out):
    out[:FIRST] = (first[...].astype(F32) + first_far[...].astype(F32)).astype(BF16)
    out[FIRST:] = (rest[...].astype(F32) + rest_far[...].astype(F32)).astype(BF16)


def add(*parts):
    top = pl.BlockSpec((FIRST, 512), lambda i: (0, i))
    low = pl.BlockSpec((512 - FIRST, 512), lambda i: (0, i))
    return pl.pallas_call(
        add_kernel,
        grid=(3,),
        out_shape=jax.ShapeDtypeStruct((512, 1536), BF16),
        in_specs=[top, top, low, low],
        out_specs=pl.BlockSpec((512, 512), lambda i: (0, i)),
        compiler_params=grant(8),
    )(*parts)


def ring(x, up, down, axis, n):
    ahead, behind = [up], [down]
    for step in range(2, n // 2 + 1):
        up = from_ahead(up, axis, n, 1)
        ahead.append(up)
        if step < n // 2:
            down = from_ahead(down, axis, n, n - 1)
            behind.append(down)
    return [x] + ahead + behind[::-1]


def whole(*turns):
    return tuple((k, 0, NZ) for k in turns)


OPPOSITE = ((2, 0, NZ // 2), (2, NZ // 2, NZ))


def opposite(ahead, behind):
    top = from_ahead(ahead[:128], "y", NY, 1)
    return top, from_ahead(behind[128:], "y", NY, NY - 1)


def ordered(mine, other, index):
    low = jnp.where(index == 0, mine, other)
    high = jnp.where(index == 0, other, mine)
    return jnp.stack([low, high], axis=0)


def body(layer_input, grad_output, gate_saved, up_saved, w_gate, w_up, w_down):
    place = jnp.stack([lax.axis_index(name) for name in ("z", "y", "xh", "core")]).astype(jnp.int32)
    xh = place[2]

    go_parts = [grad_output] + [from_ahead(grad_output, "y", NY, k) for k in (1, 2, 3)]
    z_up, z_down = from_ahead(layer_input, "z", NZ, 1), from_ahead(layer_input, "z", NZ, NZ - 1)
    go_parts, z_up, z_down = lax.optimization_barrier((go_parts, z_up, z_down))
    go = lax.all_gather(arrange(place, 1, go_parts), "z", axis=0, tiled=True)
    own_z = arrange(place, 0, ring(layer_input, z_up, z_down, "z", NZ))
    partner_z = swap(own_z, "dp")
    own1, own3 = from_ahead(own_z, "y", NY, 1), from_ahead(own_z, "y", NY, 3)

    gate = ordered(gate_saved, swap(gate_saved, "xh"), xh)
    up = ordered(up_saved, swap(up_saved, "xh"), xh)
    gate_val, up_val = gate.astype(F32), up.astype(F32)
    hidden = (gate_val * jax.nn.sigmoid(gate_val) * up_val).astype(BF16)
    hidden_other = swap(hidden, "core")
    go, gate, up, hidden, hidden_other, own_z, partner_z, own1, own3 = lax.optimization_barrier(
        (go, gate, up, hidden, hidden_other, own_z, partner_z, own1, own3)
    )

    own2 = from_ahead(own_z, "y", NY, 2)
    mine, send = hidden_grad(place, go, w_down)
    chip = mine + swap(send, "core").astype(F32)
    chip_far = swap(chip.astype(BF16), "xh")
    down_first, down_rest = down_grad(place, hidden, hidden_other, go)

    chip, chip_far, down_first, down_rest = lax.optimization_barrier((chip, chip_far, down_first, down_rest))
    first_far = swap(down_first, "dp")

    near = act_grad(chip, chip_far, gate, up)
    other = [swap(half, "core") for half in near]
    partial_in = input_grad(place, near, other, w_gate, w_up)
    partial_in, own2, first_far = lax.optimization_barrier((partial_in, own2, first_far))
    in_z = lax.psum_scatter(partial_in, "z", scatter_dimension=0, tiled=True).reshape(NY, 32, 1536)

    far = [swap(near[0], "dp"), lax.ppermute(near[1], ("dp", "xh"), [(0, 3), (3, 0), (1, 2), (2, 1)])]
    partner1, partner3 = from_ahead(partner_z, "y", NY, 1), from_ahead(partner_z, "y", NY, 3)
    far, down_rest = lax.optimization_barrier((far, down_rest))
    rest_far = swap(down_rest, "dp")
    own_z, partner1, partner3 = lax.optimization_barrier((own_z, partner1, partner3))
    partner2 = opposite(partner1, partner3)
    own_gate, own_up = weight_grads(place, whole(0, 1, 2, 3), (own_z, own1, own2, own3), (*near, *other))
    far_other = [swap(half, "core") for half in far]

    y = place[1]
    slabs = [lax.dynamic_index_in_dim(in_z, (y + k) % NY, 0, keepdims=False) for k in range(NY)]
    grads = (*far, *far_other)
    most = weight_grads(place, whole(0, 1, 3), (partner_z, partner1, partner3), grads, (own_gate, own_up))
    grad_gate, grad_up = weight_grads(place, OPPOSITE, partner2, grads, most, last=True)
    slabs, grad_gate, grad_up = lax.optimization_barrier((slabs, grad_gate, grad_up))
    total = slabs[0].astype(F32)
    for k in range(1, NY):
        total = total + from_ahead(slabs[k], "y", NY, NY - k).astype(F32)
    grad_input = total.astype(BF16)
    grad_input, rest_far = lax.optimization_barrier((grad_input, rest_far))
    return grad_input, grad_gate, grad_up, add(down_first, first_far, down_rest, rest_far)


def solution(mesh):
    fine = Mesh(mesh.devices.reshape(2, NZ, NY, 2, 2), ("dp", "z", "y", "xh", "core"))
    tokens, col, row = ("dp", "z", "y"), ("xh", "core"), ("z", "y")
    in_specs = (
        P(tokens, col),
        P(tokens, col),
        P(("dp",) + col, row),
        P(("dp",) + col, row),
        P(col, row),
        P(col, row),
        P(row, col),
    )
    out_specs = (P(tokens, col), P(col, row), P(col, row), P(row, col))
    return jax.shard_map(body, mesh=fine, in_specs=in_specs, out_specs=out_specs, check_vma=False)
```

```python
import functools

import jax
import jax.numpy as jnp
from jax import lax
from jax.experimental import pallas as pl
from jax.experimental.pallas import tpu as pltpu
from jax.sharding import Mesh, PartitionSpec as P

F32, BF16 = jnp.float32, jnp.bfloat16
NZ, NY = 8, 4
FIRST = 64
VMEM = pl.BlockSpec(memory_space=pltpu.VMEM)
SMEM = pl.BlockSpec(memory_space=pltpu.SMEM)
HBM = pl.BlockSpec(memory_space=pltpu.HBM)


def dot(left, right, left_dim, right_dim):
    dims = (((left_dim,), (right_dim,)), ((), ()))
    return lax.dot_general(left, right, dims, preferred_element_type=F32)


def from_ahead(x, axis, n, k):
    return lax.ppermute(x, axis, [((d + k) % n, d) for d in range(n)])


def swap(x, axis):
    return lax.ppermute(x, axis, [(0, 1), (1, 0)])


def grant(mib):
    return pltpu.CompilerParams(vmem_limit_bytes=mib << 20)


def in_hbm(x):
    return pltpu.with_memory_space_constraint(x, pltpu.HBM)


def arrange_kernel(n, slot, place, *refs):
    for k in range(n):
        refs[n][(place[slot] + k) % n] = refs[k][...]


def arrange(place, slot, parts):
    n, (rows, cols) = len(parts), parts[0].shape
    out = pl.pallas_call(
        functools.partial(arrange_kernel, n, slot),
        out_shape=jax.ShapeDtypeStruct((n, rows, cols), BF16),
        in_specs=[SMEM] + [VMEM] * n,
        out_specs=VMEM,
        compiler_params=grant(6),
    )(place, in_hbm(parts[0]), *parts[1:])
    return out.reshape(n * rows, cols)


def hidden_grad_kernel(place, go, w_down, mine, send, rows, weight, sems):
    copies = [pltpu.make_async_copy(w_down, weight, sems.at[2])]
    for half in range(2):
        copies.append(pltpu.make_async_copy(go.at[pl.ds(512 * half, 512)], rows.at[half], sems.at[half]))
    for copy in copies:
        copy.start()
    copies[0].wait()
    for half in range(2):
        copies[1 + half].wait()
        part = dot(rows[half], weight[...], 1, 1)
        for which in range(2):
            block = part[256 * which:256 * which + 256]

            @pl.when(place[3] == which)
            def _():
                mine[half] = block

            @pl.when(place[3] != which)
            def _():
                send[half] = block.astype(BF16)


def hidden_grad(place, go, w_down):
    return pl.pallas_call(
        hidden_grad_kernel,
        out_shape=(
            jax.ShapeDtypeStruct((2, 256, 512), F32),
            jax.ShapeDtypeStruct((2, 256, 512), BF16),
        ),
        in_specs=[SMEM, HBM, HBM],
        out_specs=(VMEM,) * 2,
        scratch_shapes=[
            pltpu.VMEM((2, 512, 1536), BF16),
            pltpu.VMEM((512, 1536), BF16),
            pltpu.SemaphoreType.DMA((3,)),
        ],
        compiler_params=grant(16),
    )(place, in_hbm(go), in_hbm(w_down))


def act_kernel(chip, chip_far, gate, up, out0, out1):
    def rows(i, carry):
        lines = pl.ds(pl.multiple_of(i * 32, 32), 32)
        for half, out in enumerate((out0, out1)):
            grad_hidden = chip[half, lines, :] + chip_far[half, lines, :].astype(F32)
            gate_val, up_val = gate[half, lines, :].astype(F32), up[half, lines, :].astype(F32)
            sigma = jax.nn.sigmoid(gate_val)
            out[0, lines, :] = (grad_hidden * up_val * sigma * (1.0 + gate_val * (1.0 - sigma))).astype(BF16)
            out[1, lines, :] = (grad_hidden * gate_val * sigma).astype(BF16)
        return carry

    lax.fori_loop(0, 8, rows, 0)


def act_grad(chip, chip_far, gate, up):
    shape = jax.ShapeDtypeStruct((2, 256, 512), BF16)
    return pl.pallas_call(
        act_kernel,
        out_shape=(shape, shape),
        in_specs=[VMEM] * 4,
        out_specs=(VMEM,) * 2,
        compiler_params=grant(8),
    )(chip, chip_far, gate, up)


def input_grad_kernel(place, near0, near1, other0, other1, w_gate, w_up, out):
    for refs, core in (((near0, near1), place[3]), ((other0, other1), 1 - place[3])):
        for half, ref in enumerate(refs):
            total = dot(ref[0], w_gate[...], 1, 1) + dot(ref[1], w_up[...], 1, 1)
            start = pl.multiple_of(512 * half + 256 * core, 256)
            out[pl.ds(start, 256), :] = total.astype(BF16)


def input_grad(place, near, other, w_gate, w_up):
    weight = pl.BlockSpec((512, 512), lambda i: (i, 0))
    return pl.pallas_call(
        input_grad_kernel,
        grid=(3,),
        out_shape=jax.ShapeDtypeStruct((1024, 1536), BF16),
        in_specs=[SMEM] + [VMEM] * 4 + [weight] * 2,
        out_specs=pl.BlockSpec((1024, 512), lambda i: (0, i)),
        compiler_params=grant(16),
    )(place, *near, *other, w_gate, w_up)


def fill_natural(place, own, other, rows, col):
    for half in range(2):
        base = half * 512
        start = pl.multiple_of(base + place[3] * 256, 256)
        rows[pl.ds(start, 256), col:col + 512] = own[half]
        start = pl.multiple_of(base + (1 - place[3]) * 256, 256)
        rows[pl.ds(start, 256), col:col + 512] = other[half]


def down_kernel(place, hidden, hidden_other, go, first, rest, rows):
    @pl.when(pl.program_id(0) == 0)
    def _():
        fill_natural(place, hidden, hidden_other, rows, 0)

    total = dot(rows[...], go[...], 0, 0).astype(BF16)
    first[...] = total[:FIRST]
    rest[...] = total[FIRST:]


def down_grad(place, hidden, hidden_other, go):
    return pl.pallas_call(
        down_kernel,
        grid=(3,),
        out_shape=(
            jax.ShapeDtypeStruct((FIRST, 1536), BF16),
            jax.ShapeDtypeStruct((512 - FIRST, 1536), BF16),
        ),
        in_specs=[SMEM, VMEM, VMEM, pl.BlockSpec((1024, 512), lambda i: (0, i))],
        out_specs=(
            pl.BlockSpec((FIRST, 512), lambda i: (0, i)),
            pl.BlockSpec((512 - FIRST, 512), lambda i: (0, i)),
        ),
        scratch_shapes=[pltpu.VMEM((1024, 512), BF16)],
        compiler_params=grant(12),
    )(place, hidden, hidden_other, in_hbm(go))


def weight_kernel(slots, based, place, *refs):
    count, turns = len(slots), sorted({k for k, _, _ in slots})
    pieces, grads, base = refs[:count], refs[count:count + 4], refs[count + 4:-3]
    d_gate, d_up, rows = refs[-3:]

    @pl.when(pl.program_id(0) == 0)
    def _():
        for half in range(4):
            core = place[3] if half < 2 else 1 - place[3]
            for pair in range(2):
                z = 4 * (half % 2) + 2 * core + pair
                for index, k in enumerate(turns):
                    start = pair * 128 + (place[1] + k) % NY * 32
                    lines = pl.ds(pl.multiple_of(start, 32), 32)
                    rows[index, z, :, :512] = grads[half][0, lines, :]
                    rows[index, z, :, 512:] = grads[half][1, lines, :]

    total = jnp.zeros((d_gate.shape[0], 1024), F32)
    for (k, low, high), piece in zip(slots, pieces):
        lines = rows[turns.index(k), low:high].reshape(32 * (high - low), 1024)
        total = total + dot(piece[...], lines, 0, 0)
    gate, up = total[:, :512], total[:, 512:]
    if based:
        gate = gate + base[0][...].astype(F32)
        up = up + base[1][...].astype(F32)
    d_gate[...] = gate.astype(BF16)
    d_up[...] = up.astype(BF16)


def weight_grads(place, slots, pieces, grads, base=(), last=False):
    size = 512 if last else 256
    pieces_in = [pl.BlockSpec((32 * (high - low), size), lambda i: (0, i)) for _, low, high in slots]
    tile = pl.BlockSpec((size, 512), lambda i: (i, 0))
    shape = jax.ShapeDtypeStruct((1536, 512), BF16) if last else pltpu.HBM((1536, 512), BF16)
    return pl.pallas_call(
        functools.partial(weight_kernel, slots, bool(base)),
        grid=(1536 // size,),
        out_shape=(shape, shape),
        in_specs=[SMEM] + pieces_in + [VMEM] * 4 + [tile] * len(base),
        out_specs=(tile, tile),
        scratch_shapes=[pltpu.VMEM((len({k for k, _, _ in slots}), NZ, 32, 1024), BF16)],
        compiler_params=grant(16),
    )(place, *(x if last else in_hbm(x) for x in pieces), *grads, *(in_hbm(x) for x in base))


def add_kernel(first, first_far, rest, rest_far, out):
    out[:FIRST] = (first[...].astype(F32) + first_far[...].astype(F32)).astype(BF16)
    out[FIRST:] = (rest[...].astype(F32) + rest_far[...].astype(F32)).astype(BF16)


def add(*parts):
    top = pl.BlockSpec((FIRST, 512), lambda i: (0, i))
    low = pl.BlockSpec((512 - FIRST, 512), lambda i: (0, i))
    return pl.pallas_call(
        add_kernel,
        grid=(3,),
        out_shape=jax.ShapeDtypeStruct((512, 1536), BF16),
        in_specs=[top, top, low, low],
        out_specs=pl.BlockSpec((512, 512), lambda i: (0, i)),
        compiler_params=grant(8),
    )(*parts)


def ring(x, up, down, axis, n):
    ahead, behind = [up], [down]
    for step in range(2, n // 2 + 1):
        up = from_ahead(up, axis, n, 1)
        ahead.append(up)
        if step < n // 2:
            down = from_ahead(down, axis, n, n - 1)
            behind.append(down)
    return [x] + ahead + behind[::-1]


def whole(*turns):
    return tuple((k, 0, NZ) for k in turns)


OPPOSITE = ((2, 0, NZ // 2), (2, NZ // 2, NZ))


def opposite(ahead, behind):
    top = from_ahead(ahead[:128], "y", NY, 1)
    return top, from_ahead(behind[128:], "y", NY, NY - 1)


def ordered(mine, other, index):
    low = jnp.where(index == 0, mine, other)
    high = jnp.where(index == 0, other, mine)
    return jnp.stack([low, high], axis=0)


def body(layer_input, grad_output, gate_saved, up_saved, w_gate, w_up, w_down):
    place = jnp.stack([lax.axis_index(name) for name in ("z", "y", "xh", "core")]).astype(jnp.int32)
    xh = place[2]

    go_parts = [grad_output] + [from_ahead(grad_output, "y", NY, k) for k in (1, 2, 3)]
    z_up, z_down = from_ahead(layer_input, "z", NZ, 1), from_ahead(layer_input, "z", NZ, NZ - 1)
    go_parts, z_up, z_down = lax.optimization_barrier((go_parts, z_up, z_down))
    go = lax.all_gather(arrange(place, 1, go_parts), "z", axis=0, tiled=True)
    own_z = arrange(place, 0, ring(layer_input, z_up, z_down, "z", NZ))
    partner_z = swap(own_z, "dp")
    own1, own3 = from_ahead(own_z, "y", NY, 1), from_ahead(own_z, "y", NY, 3)

    gate = ordered(gate_saved, swap(gate_saved, "xh"), xh)
    up = ordered(up_saved, swap(up_saved, "xh"), xh)
    gate_val, up_val = gate.astype(F32), up.astype(F32)
    hidden = (gate_val * jax.nn.sigmoid(gate_val) * up_val).astype(BF16)
    hidden_other = swap(hidden, "core")
    go, gate, up, hidden, hidden_other, own_z, partner_z, own1, own3 = lax.optimization_barrier(
        (go, gate, up, hidden, hidden_other, own_z, partner_z, own1, own3)
    )

    own2 = from_ahead(own_z, "y", NY, 2)
    mine, send = hidden_grad(place, go, w_down)
    chip = mine + swap(send, "core").astype(F32)
    chip_far = swap(chip.astype(BF16), "xh")
    down_first, down_rest = down_grad(place, hidden, hidden_other, go)

    chip, chip_far, down_first, down_rest = lax.optimization_barrier((chip, chip_far, down_first, down_rest))
    first_far = swap(down_first, "dp")

    near = act_grad(chip, chip_far, gate, up)
    other = [swap(half, "core") for half in near]
    partial_in = input_grad(place, near, other, w_gate, w_up)
    partial_in, own2, first_far = lax.optimization_barrier((partial_in, own2, first_far))
    in_z = lax.psum_scatter(partial_in, "z", scatter_dimension=0, tiled=True).reshape(NY, 32, 1536)

    far = [swap(near[0], "dp"), lax.ppermute(near[1], ("dp", "xh"), [(0, 3), (3, 0), (1, 2), (2, 1)])]
    partner1, partner3 = from_ahead(partner_z, "y", NY, 1), from_ahead(partner_z, "y", NY, 3)
    own_gate, own_up = weight_grads(place, whole(0, 1, 2, 3), (own_z, own1, own2, own3), (*near, *other))
    far, down_rest, own_gate, own_up = lax.optimization_barrier((far, down_rest, own_gate, own_up))
    rest_far = swap(down_rest, "dp")
    partner1, partner3 = lax.optimization_barrier((partner1, partner3))
    partner2 = opposite(partner1, partner3)
    far_other = [swap(half, "core") for half in far]

    y = place[1]
    slabs = [lax.dynamic_index_in_dim(in_z, (y + k) % NY, 0, keepdims=False) for k in range(NY)]
    grads = (*far, *far_other)
    most = weight_grads(place, whole(0, 1, 3), (partner_z, partner1, partner3), grads, (own_gate, own_up))
    grad_gate, grad_up = weight_grads(place, OPPOSITE, partner2, grads, most, last=True)
    slabs, grad_gate, grad_up = lax.optimization_barrier((slabs, grad_gate, grad_up))
    total = slabs[0].astype(F32)
    for k in range(1, NY):
        total = total + from_ahead(slabs[k], "y", NY, NY - k).astype(F32)
    grad_input = total.astype(BF16)
    return grad_input, grad_gate, grad_up, add(down_first, first_far, down_rest, rest_far)


def solution(mesh):
    fine = Mesh(mesh.devices.reshape(2, NZ, NY, 2, 2), ("dp", "z", "y", "xh", "core"))
    tokens, col, row = ("dp", "z", "y"), ("xh", "core"), ("z", "y")
    in_specs = (
        P(tokens, col),
        P(tokens, col),
        P(("dp",) + col, row),
        P(("dp",) + col, row),
        P(col, row),
        P(col, row),
        P(row, col),
    )
    out_specs = (P(tokens, col), P(col, row), P(col, row), P(row, col))
    return jax.shard_map(body, mesh=fine, in_specs=in_specs, out_specs=out_specs, check_vma=False)
```

```python
import functools

import jax
import jax.numpy as jnp
from jax import lax
from jax.experimental import pallas as pl
from jax.experimental.pallas import tpu as pltpu
from jax.sharding import Mesh, PartitionSpec as P

F32, BF16 = jnp.float32, jnp.bfloat16
NZ, NY = 8, 4
FIRST = 64
VMEM = pl.BlockSpec(memory_space=pltpu.VMEM)
SMEM = pl.BlockSpec(memory_space=pltpu.SMEM)
HBM = pl.BlockSpec(memory_space=pltpu.HBM)


def dot(left, right, left_dim, right_dim):
    dims = (((left_dim,), (right_dim,)), ((), ()))
    return lax.dot_general(left, right, dims, preferred_element_type=F32)


def from_ahead(x, axis, n, k):
    return lax.ppermute(x, axis, [((d + k) % n, d) for d in range(n)])


def swap(x, axis):
    return lax.ppermute(x, axis, [(0, 1), (1, 0)])


def grant(mib):
    return pltpu.CompilerParams(vmem_limit_bytes=mib << 20)


def in_hbm(x):
    return pltpu.with_memory_space_constraint(x, pltpu.HBM)


def arrange_kernel(n, slot, place, *refs):
    for k in range(n):
        refs[n][(place[slot] + k) % n] = refs[k][...]


def arrange(place, slot, parts):
    n, (rows, cols) = len(parts), parts[0].shape
    out = pl.pallas_call(
        functools.partial(arrange_kernel, n, slot),
        out_shape=jax.ShapeDtypeStruct((n, rows, cols), BF16),
        in_specs=[SMEM] + [VMEM] * n,
        out_specs=VMEM,
        compiler_params=grant(6),
    )(place, in_hbm(parts[0]), *parts[1:])
    return out.reshape(n * rows, cols)


def hidden_grad_kernel(place, go, w_down, mine, send, rows, weight, sems):
    copies = [pltpu.make_async_copy(w_down, weight, sems.at[2])]
    for half in range(2):
        copies.append(pltpu.make_async_copy(go.at[pl.ds(512 * half, 512)], rows.at[half], sems.at[half]))
    for copy in copies:
        copy.start()
    copies[0].wait()
    for half in range(2):
        copies[1 + half].wait()
        part = dot(rows[half], weight[...], 1, 1)
        for which in range(2):
            block = part[256 * which:256 * which + 256]

            @pl.when(place[3] == which)
            def _():
                mine[half] = block

            @pl.when(place[3] != which)
            def _():
                send[half] = block.astype(BF16)


def hidden_grad(place, go, w_down):
    return pl.pallas_call(
        hidden_grad_kernel,
        out_shape=(
            jax.ShapeDtypeStruct((2, 256, 512), F32),
            jax.ShapeDtypeStruct((2, 256, 512), BF16),
        ),
        in_specs=[SMEM, HBM, HBM],
        out_specs=(VMEM,) * 2,
        scratch_shapes=[
            pltpu.VMEM((2, 512, 1536), BF16),
            pltpu.VMEM((512, 1536), BF16),
            pltpu.SemaphoreType.DMA((3,)),
        ],
        compiler_params=grant(16),
    )(place, in_hbm(go), in_hbm(w_down))


def act_kernel(chip, chip_far, gate, up, out0, out1):
    def rows(i, carry):
        lines = pl.ds(pl.multiple_of(i * 32, 32), 32)
        for half, out in enumerate((out0, out1)):
            grad_hidden = chip[half, lines, :] + chip_far[half, lines, :].astype(F32)
            gate_val, up_val = gate[half, lines, :].astype(F32), up[half, lines, :].astype(F32)
            sigma = jax.nn.sigmoid(gate_val)
            out[0, lines, :] = (grad_hidden * up_val * sigma * (1.0 + gate_val * (1.0 - sigma))).astype(BF16)
            out[1, lines, :] = (grad_hidden * gate_val * sigma).astype(BF16)
        return carry

    lax.fori_loop(0, 8, rows, 0)


def act_grad(chip, chip_far, gate, up):
    shape = jax.ShapeDtypeStruct((2, 256, 512), BF16)
    return pl.pallas_call(
        act_kernel,
        out_shape=(shape, shape),
        in_specs=[VMEM] * 4,
        out_specs=(VMEM,) * 2,
        compiler_params=grant(8),
    )(chip, chip_far, gate, up)


def input_grad_kernel(place, near0, near1, other0, other1, w_gate, w_up, out):
    for refs, core in (((near0, near1), place[3]), ((other0, other1), 1 - place[3])):
        for half, ref in enumerate(refs):
            total = dot(ref[0], w_gate[...], 1, 1) + dot(ref[1], w_up[...], 1, 1)
            start = pl.multiple_of(512 * half + 256 * core, 256)
            out[pl.ds(start, 256), :] = total.astype(BF16)


def input_grad(place, near, other, w_gate, w_up):
    weight = pl.BlockSpec((512, 512), lambda i: (i, 0))
    return pl.pallas_call(
        input_grad_kernel,
        grid=(3,),
        out_shape=jax.ShapeDtypeStruct((1024, 1536), BF16),
        in_specs=[SMEM] + [VMEM] * 4 + [weight] * 2,
        out_specs=pl.BlockSpec((1024, 512), lambda i: (0, i)),
        compiler_params=grant(16),
    )(place, *near, *other, w_gate, w_up)


def fill_natural(place, own, other, rows, col):
    for half in range(2):
        base = half * 512
        start = pl.multiple_of(base + place[3] * 256, 256)
        rows[pl.ds(start, 256), col:col + 512] = own[half]
        start = pl.multiple_of(base + (1 - place[3]) * 256, 256)
        rows[pl.ds(start, 256), col:col + 512] = other[half]


def down_kernel(place, hidden, hidden_other, go, first, rest, rows):
    @pl.when(pl.program_id(0) == 0)
    def _():
        fill_natural(place, hidden, hidden_other, rows, 0)

    total = dot(rows[...], go[...], 0, 0).astype(BF16)
    first[...] = total[:FIRST]
    rest[...] = total[FIRST:]


def down_grad(place, hidden, hidden_other, go):
    return pl.pallas_call(
        down_kernel,
        grid=(3,),
        out_shape=(
            jax.ShapeDtypeStruct((FIRST, 1536), BF16),
            jax.ShapeDtypeStruct((512 - FIRST, 1536), BF16),
        ),
        in_specs=[SMEM, VMEM, VMEM, pl.BlockSpec((1024, 512), lambda i: (0, i))],
        out_specs=(
            pl.BlockSpec((FIRST, 512), lambda i: (0, i)),
            pl.BlockSpec((512 - FIRST, 512), lambda i: (0, i)),
        ),
        scratch_shapes=[pltpu.VMEM((1024, 512), BF16)],
        compiler_params=grant(12),
    )(place, hidden, hidden_other, in_hbm(go))


def weight_kernel(slots, based, place, *refs):
    count, turns = len(slots), sorted({k for k, _, _ in slots})
    pieces, grads, base = refs[:count], refs[count:count + 4], refs[count + 4:-3]
    d_gate, d_up, rows = refs[-3:]

    @pl.when(pl.program_id(0) == 0)
    def _():
        for half in range(4):
            core = place[3] if half < 2 else 1 - place[3]
            for pair in range(2):
                z = 4 * (half % 2) + 2 * core + pair
                for index, k in enumerate(turns):
                    start = pair * 128 + (place[1] + k) % NY * 32
                    lines = pl.ds(pl.multiple_of(start, 32), 32)
                    rows[index, z, :, :512] = grads[half][0, lines, :]
                    rows[index, z, :, 512:] = grads[half][1, lines, :]

    total = jnp.zeros((d_gate.shape[0], 1024), F32)
    for (k, low, high), piece in zip(slots, pieces):
        lines = rows[turns.index(k), low:high].reshape(32 * (high - low), 1024)
        total = total + dot(piece[...], lines, 0, 0)
    gate, up = total[:, :512], total[:, 512:]
    if based:
        gate = gate + base[0][...].astype(F32)
        up = up + base[1][...].astype(F32)
    d_gate[...] = gate.astype(BF16)
    d_up[...] = up.astype(BF16)


def weight_grads(place, slots, pieces, grads, base=(), last=False):
    size = 512 if last else 256
    pieces_in = [pl.BlockSpec((32 * (high - low), size), lambda i: (0, i)) for _, low, high in slots]
    tile = pl.BlockSpec((size, 512), lambda i: (i, 0))
    shape = jax.ShapeDtypeStruct((1536, 512), BF16) if last else pltpu.HBM((1536, 512), BF16)
    return pl.pallas_call(
        functools.partial(weight_kernel, slots, bool(base)),
        grid=(1536 // size,),
        out_shape=(shape, shape),
        in_specs=[SMEM] + pieces_in + [VMEM] * 4 + [tile] * len(base),
        out_specs=(tile, tile),
        scratch_shapes=[pltpu.VMEM((len({k for k, _, _ in slots}), NZ, 32, 1024), BF16)],
        compiler_params=grant(16),
    )(place, *(x if last else in_hbm(x) for x in pieces), *grads, *(in_hbm(x) for x in base))


def add_kernel(first, first_far, rest, rest_far, out):
    out[:FIRST] = (first[...].astype(F32) + first_far[...].astype(F32)).astype(BF16)
    out[FIRST:] = (rest[...].astype(F32) + rest_far[...].astype(F32)).astype(BF16)


def add(*parts):
    top = pl.BlockSpec((FIRST, 512), lambda i: (0, i))
    low = pl.BlockSpec((512 - FIRST, 512), lambda i: (0, i))
    return pl.pallas_call(
        add_kernel,
        grid=(3,),
        out_shape=jax.ShapeDtypeStruct((512, 1536), BF16),
        in_specs=[top, top, low, low],
        out_specs=pl.BlockSpec((512, 512), lambda i: (0, i)),
        compiler_params=grant(8),
    )(*parts)


def ring(x, up, down, axis, n):
    ahead, behind = [up], [down]
    for step in range(2, n // 2 + 1):
        up = from_ahead(up, axis, n, 1)
        ahead.append(up)
        if step < n // 2:
            down = from_ahead(down, axis, n, n - 1)
            behind.append(down)
    return [x] + ahead + behind[::-1]


def whole(*turns):
    return tuple((k, 0, NZ) for k in turns)


OPPOSITE = ((2, 0, NZ // 2), (2, NZ // 2, NZ))


def opposite(ahead, behind):
    top = from_ahead(ahead[:128], "y", NY, 1)
    return top, from_ahead(behind[128:], "y", NY, NY - 1)


def ordered(mine, other, index):
    low = jnp.where(index == 0, mine, other)
    high = jnp.where(index == 0, other, mine)
    return jnp.stack([low, high], axis=0)


def body(layer_input, grad_output, gate_saved, up_saved, w_gate, w_up, w_down):
    place = jnp.stack([lax.axis_index(name) for name in ("z", "y", "xh", "core")]).astype(jnp.int32)
    xh = place[2]

    go_parts = [grad_output] + [from_ahead(grad_output, "y", NY, k) for k in (1, 2, 3)]
    z_up, z_down = from_ahead(layer_input, "z", NZ, 1), from_ahead(layer_input, "z", NZ, NZ - 1)
    go_parts, z_up = lax.optimization_barrier((go_parts, z_up))
    go = lax.all_gather(arrange(place, 1, go_parts), "z", axis=0, tiled=True)
    own_z = arrange(place, 0, ring(layer_input, z_up, z_down, "z", NZ))
    partner_z = swap(own_z, "dp")
    own1, own3 = from_ahead(own_z, "y", NY, 1), from_ahead(own_z, "y", NY, 3)

    gate = ordered(gate_saved, swap(gate_saved, "xh"), xh)
    up = ordered(up_saved, swap(up_saved, "xh"), xh)
    gate_val, up_val = gate.astype(F32), up.astype(F32)
    hidden = (gate_val * jax.nn.sigmoid(gate_val) * up_val).astype(BF16)
    hidden_other = swap(hidden, "core")
    go, gate, up, hidden, hidden_other, own_z, partner_z, own1, own3 = lax.optimization_barrier(
        (go, gate, up, hidden, hidden_other, own_z, partner_z, own1, own3)
    )

    own2 = from_ahead(own_z, "y", NY, 2)
    mine, send = hidden_grad(place, go, w_down)
    chip = mine + swap(send, "core").astype(F32)
    chip_far = swap(chip.astype(BF16), "xh")
    down_first, down_rest = down_grad(place, hidden, hidden_other, go)

    chip, chip_far, down_first, down_rest = lax.optimization_barrier((chip, chip_far, down_first, down_rest))
    first_far = swap(down_first, "dp")

    near = act_grad(chip, chip_far, gate, up)
    other = [swap(half, "core") for half in near]
    partial_in = input_grad(place, near, other, w_gate, w_up)
    partial_in, own2, first_far = lax.optimization_barrier((partial_in, own2, first_far))
    in_z = lax.psum_scatter(partial_in, "z", scatter_dimension=0, tiled=True).reshape(NY, 32, 1536)

    far = [swap(near[0], "dp"), lax.ppermute(near[1], ("dp", "xh"), [(0, 3), (3, 0), (1, 2), (2, 1)])]
    partner1, partner3 = from_ahead(partner_z, "y", NY, 1), from_ahead(partner_z, "y", NY, 3)
    own_gate, own_up = weight_grads(place, whole(0, 1, 2, 3), (own_z, own1, own2, own3), (*near, *other))
    far, down_rest, own_gate, own_up = lax.optimization_barrier((far, down_rest, own_gate, own_up))
    rest_far = swap(down_rest, "dp")
    partner1, partner3 = lax.optimization_barrier((partner1, partner3))
    partner2 = opposite(partner1, partner3)
    far_other = [swap(half, "core") for half in far]

    y = place[1]
    slabs = [lax.dynamic_index_in_dim(in_z, (y + k) % NY, 0, keepdims=False) for k in range(NY)]
    grads = (*far, *far_other)
    most = weight_grads(place, whole(0, 1, 3), (partner_z, partner1, partner3), grads, (own_gate, own_up))
    grad_gate, grad_up = weight_grads(place, OPPOSITE, partner2, grads, most, last=True)
    slabs, grad_gate, grad_up = lax.optimization_barrier((slabs, grad_gate, grad_up))
    total = slabs[0].astype(F32)
    for k in range(1, NY):
        total = total + from_ahead(slabs[k], "y", NY, NY - k).astype(F32)
    grad_input = total.astype(BF16)
    return grad_input, grad_gate, grad_up, add(down_first, first_far, down_rest, rest_far)


def solution(mesh):
    fine = Mesh(mesh.devices.reshape(2, NZ, NY, 2, 2), ("dp", "z", "y", "xh", "core"))
    tokens, col, row = ("dp", "z", "y"), ("xh", "core"), ("z", "y")
    in_specs = (
        P(tokens, col),
        P(tokens, col),
        P(("dp",) + col, row),
        P(("dp",) + col, row),
        P(col, row),
        P(col, row),
        P(row, col),
    )
    out_specs = (P(tokens, col), P(col, row), P(col, row), P(row, col))
    return jax.shard_map(body, mesh=fine, in_specs=in_specs, out_specs=out_specs, check_vma=False)
```
